128 devices in a mesh: band: 4 (over x), dom: 32 (over y, z, core).
Axes of the slice: x: 4, y: 4, z: 4, core: 2. Of those that a mesh axis runs over, the one named last changes fastest.
Arguments:
- grid_vars: bfloat16 [65536, 227], P(('band', 'dom')), may hold values from -6 to 6
- cotangent: bfloat16 [65536, 227], P(('band', 'dom')), may hold values from -0.011962891 to 0.011962891
- mesh_static: bfloat16 [32768, 512], P(('band', 'dom')), may hold values from -6 to 6
- embed_weight: bfloat16 [227, 512], replicated, may hold values from -0.375 to 0.375
- encode_weight: bfloat16 [512, 512], replicated, may hold values from -0.25 to 0.25
- self_weight: bfloat16 [2, 512, 512], replicated, may hold values from -0.25 to 0.25
- neighbor_weight: bfloat16 [2, 512, 512], replicated, may hold values from -0.25 to 0.25
- decode_weight: bfloat16 [512, 512], replicated, may hold values from -0.25 to 0.25
- output_weight: bfloat16 [512, 227], replicated, may hold values from -0.25 to 0.25
- grid_sender: int32 [491520], P(('band', 'dom')), may hold values from 0 to 511
- mesh_receiver: int32 [491520], P(('band', 'dom')), may hold values from 0 to 256, as said below
- neighbors: int32 [32768, 6], P(('band', 'dom')), may hold values from 0 to 383, as said below
- mesh_sender: int32 [491520], P(('band', 'dom')), may hold values from 0 to 255
- grid_receiver: int32 [491520], P(('band', 'dom')), may hold values from 0 to 512, as said below
Outputs:
- prediction: bfloat16 [65536, 227], P(('band', 'dom'))
- grad_static: float32 [32768, 512], P(('band', 'dom'))
- grad_embed: float32 [227, 512], replicated
- grad_encode: float32 [512, 512], replicated
- grad_self: float32 [2, 512, 512], replicated
- grad_neighbor: float32 [2, 512, 512], replicated
- grad_decode: float32 [512, 512], replicated
- grad_output: float32 [512, 227], replicated
The draws below stay inside these ranges and needn't reach their ends.
Inputs may be any that keep to these rules, and one draw needn't show every extreme that they name: `mesh_receiver`: each device's receiving slots are present with a share that differs from device to device; 256 marks an absent edge. Slots whose sending device would lie outside the bands are absent. `grid_receiver`: each device's receiving slots are present with a share that differs from device to device; 512 marks an absent edge. Slots whose sending device would lie outside the bands are absent. `neighbors`: local row i of a partition has neighbours among extended rows i to i + 128.
All inputs are finite; a program needn't handle non-finite values.
Results may differ from the reference program's by a relative error of at most 0.025.
Values may be sent and summed in bfloat16 or wider, within the bound.
No kernel may reach another device: no remote copies, remote signals or barrier semaphores. Data moves between devices by JAX's collectives and lax.ppermute only.
A program may use at most 64 MiB of HBM per device.

```python
import jax
import jax.numpy as jnp
from jax import lax

VARS = 227
LATENT = 512
GD = 512
MD = 256
CAP = 768
LAYERS = 2
NEAR = 6
RIM = 64
SLOTS = 3840
GRID = 65536
MESH = 32768
N_BAND = 4
N_DOM = 32
DEVICES = 128


def live_targets(key, limit):
    total = DEVICES * 5 * CAP
    key_share, key_chance, key_target = jax.random.split(key, 3)
    live_share = jax.random.randint(key_share, (DEVICES, 1, 1), 60, 101)
    chance = jax.random.randint(key_chance, (DEVICES, 5, CAP), 0, 100)
    target = jax.random.randint(key_target, (DEVICES, 5, CAP), 0, limit)
    result = jnp.where(chance < live_share, target, limit)
    band_of = (jnp.arange(DEVICES, dtype=jnp.int32) // N_DOM)[:, None, None]
    groups = jnp.arange(5, dtype=jnp.int32)[None, :, None]
    outside = (groups == 3) & (band_of == 0) | (groups == 4) & (band_of == N_BAND - 1)
    result = jnp.where(outside, limit, result).reshape(total)
    result = result.at[0].set(0).at[total - 1].set(limit)
    return result.astype(jnp.int32)


def draw_mesh_receiver(key, part):
    key = jax.random.fold_in(key, 11)
    return live_targets(key, MD)


def draw_grid_receiver(key, part):
    key = jax.random.fold_in(key, 12)
    return live_targets(key, GD)


def draw_neighbors(key, part):
    key = jax.random.fold_in(key, 13)
    position = jnp.arange(MD * DEVICES, dtype=jnp.int32) % MD
    offset = jax.random.randint(key, (MD * DEVICES, NEAR), -RIM, RIM + 1)
    result = position[:, None] + RIM + offset
    result = result.at[0, 0].set(0).at[MD - 1, 0].set(MD + 2 * RIM - 1)
    return result.astype(jnp.int32)


def touch_ends(array, stream_key, low, top_value):
    spot = [jax.random.randint(jax.random.fold_in(stream_key, axis), (), 0, length) for axis, length in enumerate(array.shape)]
    widest = array.shape.index(max(array.shape))
    neighbour = spot[:widest] + [(spot[widest] + 1) % array.shape[widest]] + spot[widest + 1:]
    return array.at[tuple(spot)].set(low).at[tuple(neighbour)].set(top_value)


def steps_of(stream_key, shape, shards, low, high):
    def one(dim, parts):
        heights = jax.random.uniform(jax.random.fold_in(jax.random.fold_in(stream_key, 6), dim), (parts,), jnp.float32, low / len(shards), high / len(shards))
        return jnp.repeat(jnp.exp(heights), shape[dim] // parts).reshape((-1,) + (1,) * (len(shape) - dim - 1))

    factor_of = one(*shards[0])
    for cut in shards[1:]:
        factor_of = factor_of * one(*cut)
    return factor_of


def gaussian(own_key, extent, spread, reach, shards=(), kind=jnp.bfloat16):
    loudness = steps_of(own_key, extent, shards, -0.22, 0.18) if shards else 1.0
    drawn = jax.random.normal(own_key, extent, jnp.float32) * spread * loudness
    return jnp.minimum(jnp.maximum(drawn, -reach), reach).astype(kind)


def setup_inputs(seed: int = 0) -> dict:
    keys = jax.random.split(jax.random.key(seed), 15)
    return {
        "grid_vars": gaussian(keys[0], (GRID, VARS), 1.0, 6.0, ((0, 128),)),
        "cotangent": gaussian(keys[1], (GRID, VARS), 0.002, 0.011962891, ((0, 128),)),
        "mesh_static": gaussian(keys[2], (MESH, LATENT), 1.0, 6.0, ((0, 128),)),
        "embed_weight": gaussian(keys[3], (VARS, LATENT), VARS ** -0.5, 0.375),
        "encode_weight": gaussian(keys[4], (LATENT, LATENT), LATENT ** -0.5, 0.25),
        "self_weight": gaussian(keys[5], (LAYERS, LATENT, LATENT), LATENT ** -0.5, 0.25),
        "neighbor_weight": gaussian(keys[6], (LAYERS, LATENT, LATENT), LATENT ** -0.5, 0.25),
        "decode_weight": gaussian(keys[7], (LATENT, LATENT), LATENT ** -0.5, 0.25),
        "output_weight": gaussian(keys[8], (LATENT, VARS), LATENT ** -0.5, 0.25),
        "grid_sender": touch_ends(jax.random.randint(keys[9], (DEVICES * SLOTS,), 0, GD), jax.random.fold_in(keys[9], 1), 0, GD - 1).astype(jnp.int32),
        "mesh_receiver": draw_mesh_receiver(jax.random.fold_in(keys[14], 71), 0),
        "neighbors": draw_neighbors(jax.random.fold_in(keys[14], 71), 0),
        "mesh_sender": touch_ends(jax.random.randint(keys[12], (DEVICES * SLOTS,), 0, MD), jax.random.fold_in(keys[12], 1), 0, MD - 1).astype(jnp.int32),
        "grid_receiver": draw_grid_receiver(jax.random.fold_in(keys[14], 71), 0),
    }


def silu_slope(values):
    sigma = jax.nn.sigmoid(values)
    return sigma * (1.0 + values * (1.0 - sigma))


def matmul(left, right):
    return jnp.dot(left, right, preferred_element_type=jnp.float32)


def outer_sum(left, right):
    return lax.dot_general(left, right, (((0,), (0,)), ((), ())), preferred_element_type=jnp.float32)


def back_mul(left, right):
    return lax.dot_general(left, right, (((1,), (1,)), ((), ())), preferred_element_type=jnp.float32)


def spread_rows(source_table, senders, receivers, count):
    holder = jnp.zeros((count + 1, source_table.shape[1]), jnp.float32)

    def scan_step(running, edge_block):
        sources, targets = edge_block
        return running.at[targets].add(source_table[sources].astype(jnp.float32)), None

    running, _ = lax.scan(scan_step, holder, (senders, receivers))
    return running[:count]


def edge_index(sender, receiver, send_rows, recv_rows):
    owners = jnp.arange(DEVICES, dtype=jnp.int32)
    band_of = owners // N_DOM
    place = owners % N_DOM
    targets = jnp.stack([owners,
                         band_of * N_DOM + jnp.remainder(place + 1, N_DOM),
                         band_of * N_DOM + jnp.remainder(place - 1, N_DOM),
                         (band_of + 1) * N_DOM + place,
                         (band_of - 1) * N_DOM + place], 1).astype(jnp.int32)
    valid = (targets >= 0) & (targets < DEVICES)
    safe = jnp.clip(targets, 0, DEVICES - 1).astype(jnp.int32)
    glob_send = sender.reshape(DEVICES, 5 * CAP) + (owners * send_rows)[:, None]
    received = receiver.reshape(DEVICES, 5, CAP)
    groups = jnp.arange(5, dtype=jnp.int32)
    local_recv = received[safe, groups[None, :], :]
    glob_recv = jnp.where(valid[:, :, None] & (local_recv < recv_rows),
                          local_recv + (safe * recv_rows)[:, :, None], recv_rows * DEVICES)
    return glob_send.astype(jnp.int32), glob_recv.reshape(DEVICES, 5 * CAP).astype(jnp.int32)


def neighbor_index(neighbors):
    position = jnp.arange(MESH, dtype=jnp.int32)
    owner = position // MD
    band_of = owner // N_DOM
    place = owner % N_DOM
    left_owner = band_of * N_DOM + jnp.remainder(place - 1, N_DOM)
    right_owner = band_of * N_DOM + jnp.remainder(place + 1, N_DOM)
    local = neighbors
    glob = jnp.where(local < RIM, left_owner[:, None] * MD + MD - RIM + local,
                     jnp.where(local >= RIM + MD, right_owner[:, None] * MD + local - RIM - MD,
                               owner[:, None] * MD + local - RIM))
    return glob.astype(jnp.int32)


def gather_mean(source_table, source_index):
    running = jnp.zeros((source_index.shape[0], source_table.shape[1]), jnp.float32)
    for column in range(NEAR):
        running = running + source_table[source_index[:, column]].astype(jnp.float32)
    return running * (1.0 / NEAR)


def scatter_back(gradient, source_index, count):
    running = jnp.zeros((count, gradient.shape[1]), jnp.float32)
    for column in range(NEAR):
        running = running.at[source_index[:, column]].add(gradient)
    return running


def reference(grid_vars, cotangent, mesh_static, embed_weight, encode_weight, self_weight, neighbor_weight,
              decode_weight, output_weight, grid_sender, mesh_receiver, neighbors, mesh_sender, grid_receiver):
    latent_width = mesh_static.shape[1]
    embed_pre = matmul(grid_vars, embed_weight)
    latent = jax.nn.silu(embed_pre).astype(jnp.bfloat16)
    grid_send, mesh_recv = edge_index(grid_sender, mesh_receiver, GD, MD)
    encode_in = spread_rows(latent, grid_send, mesh_recv, MESH).astype(jnp.bfloat16)
    encode_pre = matmul(encode_in, encode_weight)
    state = mesh_static.astype(jnp.float32) + jax.nn.silu(encode_pre)
    near_index = neighbor_index(neighbors)
    saved = []
    for layer_index in range(LAYERS):
        state_half = state.astype(jnp.bfloat16)
        nearby_half = gather_mean(state_half, near_index).astype(jnp.bfloat16)
        layer_pre = matmul(state_half, self_weight[layer_index]) + matmul(nearby_half, neighbor_weight[layer_index])
        saved.append((state_half, nearby_half, layer_pre))
        state = state + jax.nn.silu(layer_pre)
    final_half = state.astype(jnp.bfloat16)
    mesh_send, grid_recv = edge_index(mesh_sender, grid_receiver, MD, GD)
    decode_in = spread_rows(final_half, mesh_send, grid_recv, GRID).astype(jnp.bfloat16)
    decode_pre = matmul(decode_in, decode_weight)
    hidden = jax.nn.silu(decode_pre).astype(jnp.bfloat16)
    prediction = (grid_vars.astype(jnp.float32) + matmul(hidden, output_weight)).astype(jnp.bfloat16)

    grad_output = outer_sum(hidden, cotangent)
    hidden_grad = back_mul(cotangent, output_weight)
    decode_grad = (hidden_grad * silu_slope(decode_pre)).astype(jnp.bfloat16)
    grad_decode = outer_sum(decode_in, decode_grad)
    decode_in_grad = back_mul(decode_grad, decode_weight).astype(jnp.bfloat16)
    padded = jnp.concatenate([decode_in_grad, jnp.zeros((1, latent_width), jnp.bfloat16)], 0)
    state_grad = spread_rows(padded, grid_recv, mesh_send, MESH)
    self_list = []
    near_list = []
    for layer_index in range(LAYERS - 1, -1, -1):
        state_half, nearby_half, layer_pre = saved[layer_index]
        layer_grad = (state_grad * silu_slope(layer_pre)).astype(jnp.bfloat16)
        self_list.append(outer_sum(state_half, layer_grad))
        near_list.append(outer_sum(nearby_half, layer_grad))
        own_grad = back_mul(layer_grad, self_weight[layer_index])
        near_grad = back_mul(layer_grad, neighbor_weight[layer_index]) * (1.0 / NEAR)
        state_grad = state_grad + own_grad + scatter_back(near_grad, near_index, MESH)
    grad_static = state_grad
    encode_grad = (state_grad * silu_slope(encode_pre)).astype(jnp.bfloat16)
    grad_encode = outer_sum(encode_in, encode_grad)
    encode_in_grad = back_mul(encode_grad, encode_weight).astype(jnp.bfloat16)
    padded = jnp.concatenate([encode_in_grad, jnp.zeros((1, latent_width), jnp.bfloat16)], 0)
    latent_grad = spread_rows(padded, mesh_recv, grid_send, GRID)
    embed_grad = (latent_grad * silu_slope(embed_pre)).astype(jnp.bfloat16)
    grad_embed = outer_sum(grid_vars, embed_grad)
    grad_self = jnp.stack(self_list[::-1])
    grad_neighbor = jnp.stack(near_list[::-1])
    return prediction, grad_static, grad_embed, grad_encode, grad_self, grad_neighbor, grad_decode, grad_output
```

```python
import jax
import jax.numpy as jnp
from jax import lax
from jax.sharding import PartitionSpec as P

NEAR = 6
RIM = 64
GROUPS = 5
HALF = jnp.bfloat16
SINGLE = jnp.float32


def silu_slope(values):
    sigma = jax.nn.sigmoid(values)
    return sigma * (1.0 + values * (1.0 - sigma))


def matmul(left, right):
    return jnp.dot(left, right, preferred_element_type=SINGLE)


def outer_sum(left, right):
    return lax.dot_general(
        left, right, (((0,), (0,)), ((), ())), preferred_element_type=SINGLE
    )


def back_mul(left, right):
    return lax.dot_general(
        left, right, (((1,), (1,)), ((), ())), preferred_element_type=SINGLE
    )


def swap_on(value):
    count = lax.axis_size("dom")
    return lax.ppermute(value, "dom", [(i, i ^ 1) for i in range(count)])


def swap_off(value):
    count = lax.axis_size("dom")
    return lax.ppermute(
        value, "dom", [(i, (i + (1 if i % 2 else -1)) % count) for i in range(count)]
    )


def swap_band(value, first):
    count = lax.axis_size("band")
    pairs = []
    for low in range(first, count - 1, 2):
        pairs += [(low, low + 1), (low + 1, low)]
    return lax.ppermute(value, "band", pairs)


def swap_all(on, off, north, south):
    return swap_on(on), swap_off(off), swap_band(north, 0), swap_band(south, 1)


def by_partner(slots, odd_dom, odd_band, incoming):
    flip_dom = odd_dom != incoming
    flip_band = odd_band != incoming
    return [
        slots[0],
        jnp.where(flip_dom, slots[2], slots[1]),
        jnp.where(flip_dom, slots[1], slots[2]),
        jnp.where(flip_band, slots[4], slots[3]),
        jnp.where(flip_band, slots[3], slots[4]),
    ]


def pair_counts(rows, row_count, columns, column_count):
    row_hot = (jnp.arange(row_count, dtype=jnp.int32)[:, None] == rows[None, :]).astype(HALF)
    column_hot = (columns[:, None] == jnp.arange(column_count, dtype=jnp.int32)[None, :]).astype(HALF)
    return matmul(row_hot, column_hot).astype(HALF)


def reduce_all(stacked):
    rows = stacked.shape[0]
    odd = lax.axis_index("dom") % 2
    count = lax.axis_size("dom")
    groups = [list(range(c, count, 2)) for c in range(2)]
    halves = stacked.reshape(2, rows // 2, -1)
    mine = jnp.where(odd == 1, halves[1], halves[0])
    other = jnp.where(odd == 1, halves[0], halves[1])
    part = (mine.astype(SINGLE) + swap_on(other).astype(SINGLE)).astype(HALF)
    pieces = lax.all_to_all(
        part.reshape(count // 2, -1, part.shape[1]), "dom", 0, 0, axis_index_groups=groups
    )
    piece = jnp.sum(pieces.astype(SINGLE), 0).astype(HALF)
    pieces = lax.all_gather(piece, "band", axis=0)
    piece = jnp.sum(pieces.astype(SINGLE), 0).astype(HALF)
    part = lax.all_gather(piece, "dom", axis=0, tiled=True, axis_index_groups=groups)
    other = swap_on(part)
    return jnp.concatenate(
        [jnp.where(odd == 1, other, part), jnp.where(odd == 1, part, other)], 0
    )


def shards(
    grid_vars,
    cotangent,
    mesh_static,
    embed_weight,
    encode_weight,
    self_weight,
    neighbor_weight,
    decode_weight,
    output_weight,
    grid_sender,
    mesh_receiver,
    neighbors,
    mesh_sender,
    grid_receiver,
):
    grid_count, variables = grid_vars.shape
    mesh_count, width = mesh_static.shape
    rim = RIM
    odd_dom = lax.axis_index("dom") % 2 == 1
    odd_band = lax.axis_index("band") % 2 == 1

    def sides_out(first, last):
        return jnp.where(odd_dom, first, last), jnp.where(odd_dom, last, first)

    def sides_in(on, off):
        return jnp.where(odd_dom, on, off), jnp.where(odd_dom, off, on)

    grid_send = by_partner(grid_sender.reshape(GROUPS, -1), odd_dom, odd_band, False)
    mesh_recv = by_partner(mesh_receiver.reshape(GROUPS, -1), odd_dom, odd_band, True)
    mesh_send = by_partner(mesh_sender.reshape(GROUPS, -1), odd_dom, odd_band, False)
    grid_recv = by_partner(grid_receiver.reshape(GROUPS, -1), odd_dom, odd_band, True)
    near_on, near_off = sides_out(
        neighbors[: 2 * rim].reshape(-1), neighbors[mesh_count - 2 * rim :].reshape(-1)
    )
    near_out = [near_on, near_off, near_off[:0], near_off[:0]]
    packed = [
        jnp.concatenate([mesh_recv[p], mesh_send[p], near_out[p - 1]]) for p in range(1, GROUPS)
    ]
    packed = swap_all(*packed)
    cap = mesh_recv[0].shape[0]
    far_recv = [mesh_recv[0]] + [block[:cap] for block in packed]
    far_send = [mesh_send[0]] + [block[cap : 2 * cap] for block in packed]
    near_left, near_right = sides_in(packed[0][2 * cap :], packed[1][2 * cap :])
    wide = mesh_count + 4 * rim
    near_rows = jnp.concatenate(
        [
            near_left.reshape(-1, NEAR) + (rim - mesh_count),
            neighbors + rim,
            near_right.reshape(-1, NEAR) + (rim + mesh_count),
        ],
        0,
    )
    columns = jnp.arange(wide, dtype=jnp.int32)[None, :]
    counts = jnp.zeros((wide, wide), SINGLE)
    for column in range(NEAR):
        counts = counts + (near_rows[:, column][:, None] == columns).astype(SINGLE)
    counts = counts.astype(HALF)
    own = slice(2 * rim, 2 * rim + mesh_count)
    rims = slice(rim, 3 * rim + mesh_count)
    inner = slice(rim, rim + mesh_count)

    embed_pre = matmul(grid_vars, embed_weight)
    latent = jax.nn.silu(embed_pre).astype(HALF)
    to_mesh = [
        pair_counts(far_recv[p], mesh_count, grid_send[p], grid_count) for p in range(GROUPS)
    ]
    to_grid = [
        pair_counts(grid_recv[p], grid_count, far_send[p], mesh_count) for p in range(GROUPS)
    ]
    sums = [matmul(to_mesh[p], latent) for p in range(GROUPS)]
    arrived = swap_all(*[block.astype(HALF) for block in sums[1:]])
    encode_sum = sums[0]
    for block in arrived:
        encode_sum = encode_sum + block.astype(SINGLE)
    encode_in = encode_sum.astype(HALF)
    encode_pre = matmul(encode_in, encode_weight)
    state = mesh_static.astype(SINGLE) + jax.nn.silu(encode_pre)

    half = state.astype(HALF)
    left, right = sides_in(
        *[
            swap(block)
            for swap, block in zip(
                (swap_on, swap_off),
                sides_out(half[: 2 * rim], half[mesh_count - 2 * rim :]),
                strict=True,
            )
        ]
    )
    half_0 = jnp.concatenate([left, half, right], 0)
    state_0 = jnp.concatenate(
        [left[rim:].astype(SINGLE), state, right[:rim].astype(SINGLE)], 0
    )
    nearby_0 = (matmul(counts[rims], half_0) * (1.0 / NEAR)).astype(HALF)
    pre_0 = matmul(half_0[rims], self_weight[0]) + matmul(nearby_0, neighbor_weight[0])
    state_1 = state_0 + jax.nn.silu(pre_0)
    half_1 = state_1.astype(HALF)
    nearby_1 = (matmul(counts[own, rims], half_1) * (1.0 / NEAR)).astype(HALF)
    pre_1 = matmul(half_1[inner], self_weight[1]) + matmul(nearby_1, neighbor_weight[1])
    state_2 = state_1[inner] + jax.nn.silu(pre_1)
    final_half = state_2.astype(HALF)

    finals = (final_half,) + swap_all(*[final_half] * 4)
    decode_sum = matmul(to_grid[0], finals[0])
    for p in range(1, GROUPS):
        decode_sum = decode_sum + matmul(to_grid[p], finals[p])
    decode_in = decode_sum.astype(HALF)
    decode_pre = matmul(decode_in, decode_weight)
    hidden = jax.nn.silu(decode_pre).astype(HALF)
    prediction = (grid_vars.astype(SINGLE) + matmul(hidden, output_weight)).astype(HALF)
    grad_output = outer_sum(cotangent, hidden)
    hidden_grad = back_mul(cotangent, output_weight)
    decode_grad = (hidden_grad * silu_slope(decode_pre)).astype(HALF)
    grad_decode = outer_sum(decode_in, decode_grad)
    decode_in_grad = back_mul(decode_grad, decode_weight).astype(HALF)
    sums = [outer_sum(to_grid[p], decode_in_grad) for p in range(GROUPS)]
    arrived = swap_all(*[block.astype(HALF) for block in sums[1:]])
    state_grad = sums[0]
    for block in arrived:
        state_grad = state_grad + block.astype(SINGLE)

    layer_grad = (state_grad * silu_slope(pre_1)).astype(HALF)
    grad_self_1 = outer_sum(half_1[inner], layer_grad)
    grad_near_1 = outer_sum(nearby_1, layer_grad)
    state_grad_half = state_grad.astype(HALF)
    heads = jnp.concatenate([layer_grad[: 2 * rim], state_grad_half[:rim]], 0)
    tails = jnp.concatenate(
        [layer_grad[mesh_count - 2 * rim :], state_grad_half[mesh_count - rim :]], 0
    )
    left, right = sides_in(
        *[
            swap(block)
            for swap, block in zip((swap_on, swap_off), sides_out(heads, tails), strict=True)
        ]
    )
    layer_grad = jnp.concatenate([left[: 2 * rim], layer_grad, right[: 2 * rim]], 0)
    state_grad = jnp.concatenate(
        [left[2 * rim :].astype(SINGLE), state_grad, right[2 * rim :].astype(SINGLE)], 0
    )
    spread = (outer_sum(counts[:, rims], layer_grad) * (1.0 / NEAR)).astype(HALF)
    state_grad = (
        state_grad
        + back_mul(layer_grad[rims], self_weight[1])
        + back_mul(spread, neighbor_weight[1])
    )
    layer_grad = (state_grad * silu_slope(pre_0)).astype(HALF)
    grad_self_0 = outer_sum(half, layer_grad[inner])
    grad_near_0 = outer_sum(nearby_0[inner], layer_grad[inner])
    spread = (outer_sum(counts[rims, own], layer_grad) * (1.0 / NEAR)).astype(HALF)
    state_grad = (
        state_grad[inner]
        + back_mul(layer_grad[inner], self_weight[0])
        + back_mul(spread, neighbor_weight[0])
    )
    encode_grad = (state_grad * silu_slope(encode_pre)).astype(HALF)
    grad_encode = outer_sum(encode_in, encode_grad)
    encode_in_grad = back_mul(encode_grad, encode_weight).astype(HALF)
    returned = (encode_in_grad,) + swap_all(*[encode_in_grad] * 4)
    latent_grad = outer_sum(to_mesh[0], returned[0])
    for p in range(1, GROUPS):
        latent_grad = latent_grad + outer_sum(to_mesh[p], returned[p])
    embed_grad = (latent_grad * silu_slope(embed_pre)).astype(HALF)
    grad_embed = outer_sum(grid_vars, embed_grad)

    filler = jnp.zeros((-variables % 32, width), HALF)
    pieces = [
        grad_self_0,
        grad_self_1,
        grad_near_0,
        grad_near_1,
        grad_encode,
        grad_decode,
        grad_output,
        filler,
        grad_embed,
        filler,
    ]
    total = reduce_all(jnp.concatenate([piece.astype(HALF) for piece in pieces], 0))
    total = total.astype(SINGLE)
    square = total[: 6 * width].reshape(6, width, width)
    rest = total[6 * width :].reshape(2, -1, width)[:, :variables]
    return (
        prediction,
        state_grad,
        rest[1],
        square[4],
        square[0:2],
        square[2:4],
        square[5],
        rest[0].T,
    )


def solution(mesh):
    placed = (
        P(("band", "dom"), None),
        P(("band", "dom"), None),
        P(("band", "dom"), None),
        P(),
        P(),
        P(),
        P(),
        P(),
        P(),
        P(("band", "dom")),
        P(("band", "dom")),
        P(("band", "dom"), None),
        P(("band", "dom")),
        P(("band", "dom")),
    )
    return jax.shard_map(
        shards,
        mesh=mesh,
        in_specs=placed,
        out_specs=(
            P(("band", "dom"), None),
            P(("band", "dom"), None),
            P(),
            P(),
            P(),
            P(),
            P(),
            P(),
        ),
        check_vma=False,
    )
```

```python
import jax
import jax.numpy as jnp
from jax import lax
from jax.experimental import pallas as pl
from jax.experimental.pallas import tpu as pltpu
from jax.sharding import PartitionSpec as P

NEAR = 6
RIM = 64
GROUPS = 5
LANES = 128
HALF = jnp.bfloat16
SINGLE = jnp.float32
MIB = 1024 * 1024


def silu_slope(values):
    sigma = jax.nn.sigmoid(values)
    return sigma * (1.0 + values * (1.0 - sigma))


def matmul(left, right):
    return jnp.dot(left, right, preferred_element_type=SINGLE)


def outer_sum(left, right):
    return lax.dot_general(
        left, right, (((0,), (0,)), ((), ())), preferred_element_type=SINGLE
    )


def back_mul(left, right):
    return lax.dot_general(
        left, right, (((1,), (1,)), ((), ())), preferred_element_type=SINGLE
    )


def swap_on(value):
    count = lax.axis_size("dom")
    return lax.ppermute(value, "dom", [(i, i ^ 1) for i in range(count)])


def swap_off(value):
    count = lax.axis_size("dom")
    return lax.ppermute(
        value, "dom", [(i, (i + (1 if i % 2 else -1)) % count) for i in range(count)]
    )


def swap_band(value, first):
    count = lax.axis_size("band")
    pairs = []
    for low in range(first, count - 1, 2):
        pairs += [(low, low + 1), (low + 1, low)]
    return lax.ppermute(value, "band", pairs)


def swap_all(on, off, north, south):
    return swap_on(on), swap_off(off), swap_band(north, 0), swap_band(south, 1)


def by_partner(slots, odd_dom, odd_band, incoming):
    flip_dom = odd_dom != incoming
    flip_band = odd_band != incoming
    return [
        slots[0],
        jnp.where(flip_dom, slots[2], slots[1]),
        jnp.where(flip_dom, slots[1], slots[2]),
        jnp.where(flip_band, slots[4], slots[3]),
        jnp.where(flip_band, slots[3], slots[4]),
    ]


def whole(body, outs, macs, *args, limit=32):
    moved = sum(a.size * a.dtype.itemsize for a in (*args, *outs))
    return pl.pallas_call(
        body,
        out_shape=outs,
        compiler_params=pltpu.CompilerParams(vmem_limit_bytes=limit * MIB),
        cost_estimate=pl.CostEstimate(flops=2 * macs, bytes_accessed=moved, transcendentals=0),
    )(*args)


def shape(rows, columns, kind):
    return jax.ShapeDtypeStruct((rows, columns), kind)


def odd_along(axis):
    return lax.axis_index(axis) % 2 == 1


def hot(rows, index):
    spots = lax.broadcasted_iota(jnp.int32, (rows, LANES), 0)
    one = [
        jnp.where(spots == index[j : j + 1], 1.0, 0.0).astype(HALF) for j in range(index.shape[0])
    ]
    return jnp.concatenate(one, 1)


def pair_counts(rows, row_count, columns, column_count):
    return back_mul(hot(row_count, rows), hot(column_count, columns)).astype(HALF)


def slots_of(index):
    step = index.shape[0] // GROUPS
    return [index[k * step : (k + 1) * step] for k in range(GROUPS)]


def parcels(grid_ref, grid_send_ref, mesh_recv_ref, mesh_send_ref, near_ref, *outs):
    odd_dom, odd_band = odd_along("dom"), odd_along("band")
    grid_send = by_partner(slots_of(grid_send_ref[...]), odd_dom, odd_band, False)
    mesh_recv = by_partner(slots_of(mesh_recv_ref[...]), odd_dom, odd_band, True)
    mesh_send = by_partner(slots_of(mesh_send_ref[...]), odd_dom, odd_band, False)
    near = near_ref[...]
    near = [near[:, j : j + LANES] for j in range(0, near.shape[1], LANES)]
    rows, variables = grid_ref.shape
    width = outs[0].shape[1]
    grid = grid_ref[...]
    spare = jnp.zeros((rows, width - variables), HALF)
    for p, out in enumerate(outs):
        parts = [mesh_recv[p + 1], mesh_send[p + 1], grid_send[p + 1], *near]
        used = sum(part.shape[0] for part in parts)
        parts.append(jnp.zeros((out.shape[0] - rows - used, LANES), jnp.int32))
        index = jnp.concatenate(parts, 0)
        out[:rows, :variables] = grid
        out[:rows, variables:] = spare
        out[rows:, :LANES] = (index >> 1).astype(SINGLE).astype(HALF)
        out[rows:, LANES:] = (index & 1).astype(SINGLE).astype(HALF)


def embed_own(grid_ref, weight_ref, send_ref, recv_ref, slope_ref, counts_ref, sum_ref):
    step = send_ref.shape[0] // GROUPS
    counts = pair_counts(
        recv_ref[:step], sum_ref.shape[0], send_ref[:step], grid_ref.shape[0]
    )
    pre = matmul(grid_ref[...], weight_ref[...])
    sigma = jax.nn.sigmoid(pre)
    slope_ref[...] = sigma * (1.0 + pre * (1.0 - sigma))
    counts_ref[...] = counts
    sum_ref[...] = matmul(counts, (pre * sigma).astype(HALF))


def embed_far(p, parcel_ref, weight_ref, recv_ref, sum_ref, index_ref, out_ref):
    rows = parcel_ref.shape[0] - index_ref.shape[0]
    packed = parcel_ref[rows:].astype(SINGLE)
    index = (packed[:, :LANES] * 2.0 + packed[:, LANES:]).astype(jnp.int32)
    index_ref[...] = index
    step = recv_ref.shape[0] // GROUPS
    recv = by_partner(slots_of(recv_ref[...]), odd_along("dom"), odd_along("band"), True)[p]
    counts = pair_counts(recv, out_ref.shape[0], index[2 * step : 3 * step], rows)
    pre = matmul(parcel_ref[:rows], weight_ref[...])
    latent = (pre * jax.nn.sigmoid(pre)).astype(HALF)
    out_ref[...] = sum_ref[...] + matmul(counts, latent)


def near_counts(near_ref, on_ref, off_ref, out_ref):
    step = near_ref.shape[0]
    mesh_count = near_ref.shape[1]
    first = on_ref.shape[0] - 2 - 2 * step
    odd_dom = odd_along("dom")
    on, off = on_ref[...], off_ref[...]
    left = jnp.where(odd_dom, on, off)[first + step : first + 2 * step] + (RIM - mesh_count)
    right = jnp.where(odd_dom, off, on)[first : first + step] + (RIM + mesh_count)
    own = near_ref[...] + RIM
    index = jnp.concatenate([left, own, right], 1)
    spots = lax.broadcasted_iota(jnp.int32, out_ref.shape, 0)
    counts = jnp.zeros(out_ref.shape, SINGLE)
    for j in range(step):
        counts = counts + jnp.where(spots == index[j : j + 1], 1.0, 0.0)
    out_ref[...] = counts.astype(HALF)


def grid_counts(send_ref, recv_ref, *refs):
    far, outs = refs[: GROUPS - 1], refs[GROUPS - 1 :]
    odd_dom, odd_band = odd_along("dom"), odd_along("band")
    step = send_ref.shape[0] // GROUPS
    recv = by_partner(slots_of(recv_ref[...]), odd_dom, odd_band, True)
    send = [send_ref[:step]] + [ref[step : 2 * step] for ref in far]
    for p, out in enumerate(outs):
        out[...] = pair_counts(recv[p], out.shape[0], send[p], out.shape[1])


def mesh_counts(send_ref, *refs):
    far, outs = refs[: GROUPS - 1], refs[GROUPS - 1 :]
    step = send_ref.shape[0] // GROUPS
    send = by_partner(slots_of(send_ref[...]), odd_along("dom"), odd_along("band"), False)
    for p, out in enumerate(outs):
        out[...] = pair_counts(far[p][:step], out.shape[0], send[p + 1], out.shape[1])


def gradient_halves(*refs):
    mine_ref, other_ref, wide_ref = refs[-3:]
    odd = lax.axis_index("dom") % 2
    at = 0
    for left, right in zip(refs[:-3:2], refs[1:-3:2], strict=True):
        columns = left.shape[1]
        rows = -(-columns // (2 * LANES)) * LANES
        wide_ref[:columns] = outer_sum(left[...], right[...])
        if columns < 2 * rows:
            wide_ref[columns : 2 * rows] = jnp.zeros((2 * rows - columns, right.shape[1]), SINGLE)
        mine_ref[at : at + rows] = wide_ref[pl.ds(pl.multiple_of(odd * rows, rows), rows)].astype(HALF)
        other_ref[at : at + rows] = wide_ref[
            pl.ds(pl.multiple_of((1 - odd) * rows, rows), rows)
        ].astype(HALF)
        at += rows


def split_gradients(*pairs):
    rows = sum(-(-left.shape[1] // (2 * LANES)) * LANES for left, _ in pairs)
    width = pairs[0][1].shape[1]
    flat = [array for pair in pairs for array in pair]
    macs = sum(left.size * right.shape[1] for left, right in pairs)
    outs = [shape(rows, width, HALF)] * 2
    moved = sum(a.size * a.dtype.itemsize for a in (*flat, *outs))
    mine, other = pl.pallas_call(
        gradient_halves,
        out_shape=outs,
        scratch_shapes=[pltpu.VMEM((width, width), SINGLE)],
        compiler_params=pltpu.CompilerParams(vmem_limit_bytes=32 * MIB),
        cost_estimate=pl.CostEstimate(flops=2 * macs, bytes_accessed=moved, transcendentals=0),
    )(*flat)
    return mine, swap_on(other)


def add_halves(*refs):
    out_ref = refs[-1]
    at = 0
    for mine, other in zip(refs[:-1:2], refs[1:-1:2], strict=True):
        rows = mine.shape[0]
        out_ref[at : at + rows] = (
            mine[...].astype(SINGLE) + other[...].astype(SINGLE)
        ).astype(HALF)
        at += rows


def unpack(part_ref, other_ref, *outs):
    odd = odd_along("dom")
    at = 0
    for out, which, rows in outs_of(outs):
        own = part_ref[at : at + rows].astype(SINGLE)
        far = other_ref[at : at + rows].astype(SINGLE)
        top, bottom = jnp.where(odd, far, own), jnp.where(odd, own, far)
        if which is None:
            out[:rows] = top
            out[rows:] = bottom[: out.shape[0] - rows]
        else:
            out[which, :rows] = top
            out[which, rows:] = bottom
        at += rows


def outs_of(outs):
    embed, encode, self_, near, decode, output = outs
    half = encode.shape[0] // 2
    narrow = -(-embed.shape[0] // (2 * LANES)) * LANES
    return [
        (output, None, narrow),
        (decode, None, half),
        (self_, 1, half),
        (near, 1, half),
        (self_, 0, half),
        (near, 0, half),
        (encode, None, half),
        (embed, None, narrow),
    ]


def reduce_all(part):
    count = lax.axis_size("dom")
    groups = [list(range(c, count, 2)) for c in range(2)]
    chips = count // 2
    width = part.shape[1]
    pieces = lax.all_to_all(
        part.reshape(chips, -1, width), "dom", 0, 0, axis_index_groups=groups
    )
    piece = jnp.sum(pieces.astype(SINGLE), 0).astype(HALF)
    pieces = lax.all_gather(piece, "band", axis=0)
    piece = jnp.sum(pieces.astype(SINGLE), 0).astype(HALF)
    copies = jnp.broadcast_to(piece[None], (chips, *piece.shape))
    return lax.all_to_all(copies, "dom", 0, 0, axis_index_groups=groups).reshape(part.shape)


def shards(
    grid_vars,
    cotangent,
    mesh_static,
    embed_weight,
    encode_weight,
    self_weight,
    neighbor_weight,
    decode_weight,
    output_weight,
    grid_sender,
    mesh_receiver,
    neighbors,
    mesh_sender,
    grid_receiver,
):
    grid_count, variables = grid_vars.shape
    mesh_count, width = mesh_static.shape
    rim = RIM
    odd_dom = odd_along("dom")
    cap = grid_sender.shape[0] // GROUPS

    def sides_out(first, last):
        return jnp.where(odd_dom, first, last), jnp.where(odd_dom, last, first)

    def sides_in(on, off):
        return jnp.where(odd_dom, on, off), jnp.where(odd_dom, off, on)

    grid_send, mesh_recv, mesh_send, grid_recv = (
        index.reshape(-1, LANES) for index in (grid_sender, mesh_receiver, mesh_sender, grid_receiver)
    )
    near = neighbors.T
    index_rows = 3 * (cap // LANES) + NEAR * mesh_count // LANES
    index_rows += -index_rows % 16
    columns = 2 * LANES
    sent = whole(
        parcels,
        [shape(grid_count + index_rows, columns, HALF)] * (GROUPS - 1),
        0,
        grid_vars,
        grid_send,
        mesh_recv,
        mesh_send,
        near,
    )
    arrived = swap_all(*sent)
    slope_embed, to_mesh_own, total = whole(
        embed_own,
        [
            shape(grid_count, width, SINGLE),
            shape(mesh_count, grid_count, HALF),
            shape(mesh_count, width, SINGLE),
        ],
        grid_vars.size * width + mesh_count * grid_count * (cap + width),
        grid_vars,
        embed_weight,
        grid_send,
        mesh_recv,
    )
    wide_weight = jnp.pad(embed_weight, ((0, columns - variables), (0, 0)))
    index = [None] * GROUPS
    for p in range(1, GROUPS):
        index[p], total = whole(
            lambda *refs, p=p: embed_far(p, *refs),
            [shape(index_rows, LANES, jnp.int32), shape(mesh_count, width, SINGLE)],
            grid_count * columns * width + mesh_count * grid_count * (cap + width),
            arrived[p - 1],
            wide_weight,
            mesh_recv,
            total,
        )
    ext = mesh_count + 4 * rim
    (counts,) = whole(
        near_counts, [shape(ext, ext, HALF)], ext * ext * 64, near, index[1], index[2]
    )
    own = slice(2 * rim, 2 * rim + mesh_count)
    to_grid = whole(
        grid_counts,
        [shape(grid_count, mesh_count, HALF)] * GROUPS,
        GROUPS * grid_count * mesh_count * cap,
        mesh_send,
        grid_recv,
        *index[1:],
    )
    to_mesh = to_mesh_own, *whole(
        mesh_counts,
        [shape(mesh_count, grid_count, HALF)] * (GROUPS - 1),
        (GROUPS - 1) * grid_count * mesh_count * cap,
        grid_send,
        *index[1:],
    )

    encode_in = total.astype(HALF)
    encode_pre = matmul(encode_in, encode_weight)
    state = mesh_static.astype(SINGLE) + jax.nn.silu(encode_pre)

    half = state.astype(HALF)
    on, off = sides_out(half[: 2 * rim], half[mesh_count - 2 * rim :])
    left, right = sides_in(swap_on(on), swap_off(off))
    half_0 = jnp.concatenate([left, half, right], 0)
    state_0 = jnp.concatenate([left.astype(SINGLE), state, right.astype(SINGLE)], 0)
    nearby_0 = (outer_sum(counts, half_0) * (1.0 / NEAR)).astype(HALF)
    pre_0 = matmul(half_0, self_weight[0]) + matmul(nearby_0, neighbor_weight[0])
    state_1 = state_0 + jax.nn.silu(pre_0)
    half_1 = state_1.astype(HALF)
    nearby_1 = (outer_sum(counts[:, own], half_1) * (1.0 / NEAR)).astype(HALF)
    pre_1 = matmul(half_1[own], self_weight[1]) + matmul(nearby_1, neighbor_weight[1])
    state_2 = state_1[own] + jax.nn.silu(pre_1)
    final_half = state_2.astype(HALF)

    finals = (final_half,) + swap_all(*[final_half] * 4)
    decode_sum = matmul(to_grid[0], finals[0])
    for p in range(1, GROUPS):
        decode_sum = decode_sum + matmul(to_grid[p], finals[p])
    decode_in = decode_sum.astype(HALF)
    decode_pre = matmul(decode_in, decode_weight)
    hidden = jax.nn.silu(decode_pre).astype(HALF)
    prediction = (grid_vars.astype(SINGLE) + matmul(hidden, output_weight)).astype(HALF)
    hidden_grad = back_mul(cotangent, output_weight)
    decode_grad = (hidden_grad * silu_slope(decode_pre)).astype(HALF)
    decode_in_grad = back_mul(decode_grad, decode_weight).astype(HALF)
    sums = [outer_sum(to_grid[p], decode_in_grad) for p in range(GROUPS)]
    arrived = swap_all(*[block.astype(HALF) for block in sums[1:]])
    halves = [*split_gradients((cotangent, hidden), (decode_in, decode_grad))]
    state_grad = sums[0]
    for block in arrived:
        state_grad = state_grad + block.astype(SINGLE)

    layer_grad_1 = (state_grad * silu_slope(pre_1)).astype(HALF)
    state_grad_half = state_grad.astype(HALF)
    heads = jnp.concatenate([layer_grad_1[: 2 * rim], state_grad_half[:rim]], 0)
    tails = jnp.concatenate(
        [layer_grad_1[mesh_count - 2 * rim :], state_grad_half[mesh_count - rim :]], 0
    )
    on, off = sides_out(heads, tails)
    left, right = sides_in(swap_on(on), swap_off(off))
    halves += split_gradients((half_1[own], layer_grad_1), (nearby_1, layer_grad_1))
    layer_grad = jnp.concatenate([left[: 2 * rim], layer_grad_1, right[: 2 * rim]], 0)
    outside = jnp.zeros((rim, width), SINGLE)
    state_grad = jnp.concatenate(
        [
            outside,
            left[2 * rim :].astype(SINGLE),
            state_grad,
            right[2 * rim :].astype(SINGLE),
            outside,
        ],
        0,
    )
    spread = (matmul(counts, layer_grad) * (1.0 / NEAR)).astype(HALF)
    state_grad = (
        state_grad
        + back_mul(layer_grad, self_weight[1])
        + back_mul(spread, neighbor_weight[1])
    )
    layer_grad = (state_grad * silu_slope(pre_0)).astype(HALF)
    layer_grad_0 = layer_grad[own]
    spread = (matmul(counts[own], layer_grad) * (1.0 / NEAR)).astype(HALF)
    state_grad = (
        state_grad[own]
        + back_mul(layer_grad_0, self_weight[0])
        + back_mul(spread, neighbor_weight[0])
    )
    encode_grad = (state_grad * silu_slope(encode_pre)).astype(HALF)
    encode_in_grad = back_mul(encode_grad, encode_weight).astype(HALF)
    returned = (encode_in_grad,) + swap_all(*[encode_in_grad] * 4)
    halves += split_gradients(
        (half, layer_grad_0), (nearby_0[own], layer_grad_0), (encode_in, encode_grad)
    )
    latent_grad = outer_sum(to_mesh[0], returned[0])
    for p in range(1, GROUPS):
        latent_grad = latent_grad + outer_sum(to_mesh[p], returned[p])
    embed_grad = (latent_grad * slope_embed).astype(HALF)
    halves += split_gradients((grid_vars, embed_grad))

    rows = sum(block.shape[0] for block in halves[::2])
    (part,) = whole(add_halves, [shape(rows, width, HALF)], 0, *halves)
    part = reduce_all(part)
    other = swap_on(part)
    square = shape(width, width, SINGLE)
    pair = jax.ShapeDtypeStruct((2, width, width), SINGLE)
    narrow = shape(variables, width, SINGLE)
    grad_embed, grad_encode, grad_self, grad_near, grad_decode, grad_output = whole(
        unpack, [narrow, square, pair, pair, square, narrow], 0, part, other
    )
    return (
        prediction,
        state_grad,
        grad_embed,
        grad_encode,
        grad_self,
        grad_near,
        grad_decode,
        grad_output.T,
    )


def solution(mesh):
    placed = (
        P(("band", "dom"), None),
        P(("band", "dom"), None),
        P(("band", "dom"), None),
        P(),
        P(),
        P(),
        P(),
        P(),
        P(),
        P(("band", "dom")),
        P(("band", "dom")),
        P(("band", "dom"), None),
        P(("band", "dom")),
        P(("band", "dom")),
    )
    return jax.shard_map(
        shards,
        mesh=mesh,
        in_specs=placed,
        out_specs=(
            P(("band", "dom"), None),
            P(("band", "dom"), None),
            P(),
            P(),
            P(),
            P(),
            P(),
            P(),
        ),
        check_vma=False,
    )
```

```python
import jax
import jax.numpy as jnp
from jax import lax
from jax.experimental import pallas as pl
from jax.experimental.pallas import tpu as pltpu
from jax.sharding import PartitionSpec as P

NEAR = 6
RIM = 64
GROUPS = 5
LANES = 128
HALF = jnp.bfloat16
SINGLE = jnp.float32
MIB = 1024 * 1024
SLOT_ROWS = 6
INDEX_ROWS = 32


def silu_slope(values):
    sigma = jax.nn.sigmoid(values)
    return sigma * (1.0 + values * (1.0 - sigma))


def matmul(left, right):
    return jnp.dot(left, right, preferred_element_type=SINGLE)


def outer_sum(left, right):
    return lax.dot_general(
        left, right, (((0,), (0,)), ((), ())), preferred_element_type=SINGLE
    )


def back_mul(left, right):
    return lax.dot_general(
        left, right, (((1,), (1,)), ((), ())), preferred_element_type=SINGLE
    )


def swap_on(value):
    count = lax.axis_size("dom")
    return lax.ppermute(value, "dom", [(i, i ^ 1) for i in range(count)])


def swap_off(value):
    count = lax.axis_size("dom")
    return lax.ppermute(
        value, "dom", [(i, (i + (1 if i % 2 else -1)) % count) for i in range(count)]
    )


def swap_band(value, first):
    count = lax.axis_size("band")
    pairs = []
    for low in range(first, count - 1, 2):
        pairs += [(low, low + 1), (low + 1, low)]
    return lax.ppermute(value, "band", pairs)


def swap_all(on, off, north, south):
    return swap_on(on), swap_off(off), swap_band(north, 0), swap_band(south, 1)


def by_partner(slots, odd_dom, odd_band, incoming):
    flip_dom = odd_dom != incoming
    flip_band = odd_band != incoming
    return [
        slots[0],
        jnp.where(flip_dom, slots[2], slots[1]),
        jnp.where(flip_dom, slots[1], slots[2]),
        jnp.where(flip_band, slots[4], slots[3]),
        jnp.where(flip_band, slots[3], slots[4]),
    ]


def whole(body, outs, macs, *args, limit=32, scratch=()):
    moved = sum(a.size * a.dtype.itemsize for a in (*args, *outs))
    return pl.pallas_call(
        body,
        out_shape=outs,
        scratch_shapes=scratch,
        compiler_params=pltpu.CompilerParams(vmem_limit_bytes=limit * MIB),
        cost_estimate=pl.CostEstimate(flops=2 * macs, bytes_accessed=moved, transcendentals=0),
    )(*args)


def shape(rows, columns, kind):
    return jax.ShapeDtypeStruct((rows, columns), kind)


def odd_along(axis):
    return lax.axis_index(axis) % 2 == 1


def hot(rows, index):
    spots = lax.broadcasted_iota(jnp.int32, (rows, LANES), 0)
    one = [
        jnp.where(spots == index[j : j + 1], 1.0, 0.0).astype(HALF) for j in range(index.shape[0])
    ]
    return jnp.concatenate(one, 1)


def pair_counts(rows, row_count, columns, column_count):
    return back_mul(hot(row_count, rows), hot(column_count, columns)).astype(HALF)


def slots_of(index):
    step = index.shape[0] // GROUPS
    return [index[k * step : (k + 1) * step] for k in range(GROUPS)]


def fetch(sources, buffers, sems):
    copies = [
        pltpu.make_async_copy(source, buffer, sems.at[i])
        for i, (source, buffer) in enumerate(zip(sources, buffers, strict=True))
    ]
    for copy in copies:
        copy.start()
    for copy in copies:
        copy.wait()


def fetching(body, outs, macs, *args):
    moved = sum(a.size * a.dtype.itemsize for a in (*args, *outs))
    return pl.pallas_call(
        body,
        out_shape=outs,
        in_specs=[pl.BlockSpec(memory_space=pl.ANY)] * len(args),
        scratch_shapes=[pltpu.VMEM(a.shape, a.dtype) for a in args]
        + [pltpu.SemaphoreType.DMA((len(args),))],
        compiler_params=pltpu.CompilerParams(vmem_limit_bytes=32 * MIB),
        cost_estimate=pl.CostEstimate(flops=2 * macs, bytes_accessed=moved, transcendentals=0),
    )(*args)


def parcels(*refs):
    inputs, rest = refs[:5], refs[5:]
    outs, buffers, sems = rest[: GROUPS - 1], rest[GROUPS - 1 : -1], rest[-1]
    fetch(inputs, buffers, sems)
    grid_ref, grid_send_ref, mesh_recv_ref, mesh_send_ref, near_ref = buffers
    odd_dom, odd_band = odd_along("dom"), odd_along("band")
    grid_send = by_partner(slots_of(grid_send_ref[...]), odd_dom, odd_band, False)
    mesh_recv = by_partner(slots_of(mesh_recv_ref[...]), odd_dom, odd_band, True)
    mesh_send = by_partner(slots_of(mesh_send_ref[...]), odd_dom, odd_band, False)
    near = near_ref[...]
    near = [near[:, j : j + LANES] for j in range(0, near.shape[1], LANES)]
    variables, count = grid_ref.shape
    first = outs[0].shape[0] - INDEX_ROWS // 2
    grid = grid_ref[...]
    for p, out in enumerate(outs):
        parts = [mesh_recv[p + 1], mesh_send[p + 1], grid_send[p + 1], *near]
        used = sum(part.shape[0] for part in parts)
        parts.append(jnp.zeros((INDEX_ROWS - used, LANES), jnp.int32))
        index = jnp.concatenate(parts, 0)
        high = (index >> 1).astype(SINGLE)
        low = (index & 1).astype(SINGLE)
        cut = INDEX_ROWS // 2
        out[:variables] = grid
        out[variables:first] = jnp.zeros((first - variables, count), HALF)
        out[first:] = jnp.concatenate([high[:cut], low[:cut], high[cut:], low[cut:]], 1).astype(HALF)


def index_of(packed):
    packed = packed.astype(SINGLE)
    halves = [
        packed[:, j : j + LANES] * 2.0 + packed[:, j + LANES : j + 2 * LANES]
        for j in (0, 2 * LANES)
    ]
    return jnp.concatenate(halves, 0).astype(jnp.int32)


def embed_own(*refs):
    inputs, (slope_ref, sum_ref), buffers, sems = refs[:4], refs[4:6], refs[6:-1], refs[-1]
    fetch(inputs, buffers, sems)
    grid_ref, weight_ref, send_ref, recv_ref = buffers
    step = send_ref.shape[0] // GROUPS
    counts = pair_counts(
        recv_ref[:step], sum_ref.shape[0], send_ref[:step], grid_ref.shape[1]
    )
    pre = outer_sum(grid_ref[...], weight_ref[...])
    sigma = jax.nn.sigmoid(pre)
    slope_ref[...] = sigma * (1.0 + pre * (1.0 - sigma))
    sum_ref[...] = matmul(counts, (pre * sigma).astype(HALF))


def embed_far(p, parcel_ref, weight_ref, recv_ref, sum_ref, index_ref, out_ref):
    index = index_of(parcel_ref[parcel_ref.shape[0] - INDEX_ROWS // 2 :])
    index_ref[...] = index
    step = recv_ref.shape[0] // GROUPS
    recv = by_partner(slots_of(recv_ref[...]), odd_along("dom"), odd_along("band"), True)[p]
    counts = pair_counts(
        recv, out_ref.shape[0], index[2 * step : 3 * step], parcel_ref.shape[1]
    )
    pre = outer_sum(parcel_ref[: weight_ref.shape[0]], weight_ref[...])
    latent = (pre * jax.nn.sigmoid(pre)).astype(HALF)
    out_ref[...] = sum_ref[...] + matmul(counts, latent)


def encode(sum_ref, weight_ref, static_ref, in_ref, slope_ref, state_ref, half_ref, on_ref, off_ref):
    encode_in = sum_ref[...].astype(HALF)
    pre = matmul(encode_in, weight_ref[...])
    sigma = jax.nn.sigmoid(pre)
    state = static_ref[...].astype(SINGLE) + pre * sigma
    half = state.astype(HALF)
    in_ref[...] = encode_in
    slope_ref[...] = sigma * (1.0 + pre * (1.0 - sigma))
    state_ref[...] = state
    half_ref[...] = half
    rows = on_ref.shape[0]
    odd = odd_along("dom")
    head, tail = half[:rows], half[half.shape[0] - rows :]
    on_ref[...] = jnp.where(odd, head, tail)
    off_ref[...] = jnp.where(odd, tail, head)


def near_counts(near_ref, on_ref, off_ref, out_ref, turned_ref):
    step = near_ref.shape[0]
    mesh_count = near_ref.shape[1]
    first = 3 * SLOT_ROWS
    odd_dom = odd_along("dom")
    on, off = on_ref[...], off_ref[...]
    left = jnp.where(odd_dom, on, off)[first + step : first + 2 * step] + (RIM - mesh_count)
    right = jnp.where(odd_dom, off, on)[first : first + step] + (RIM + mesh_count)
    own = near_ref[...] + RIM
    index = jnp.concatenate([left, own, right], 1)
    spots = lax.broadcasted_iota(jnp.int32, out_ref.shape, 0)
    counts = jnp.zeros(out_ref.shape, SINGLE)
    for j in range(step):
        counts = counts + jnp.where(spots == index[j : j + 1], 1.0, 0.0)
    turned_ref[...] = counts.astype(HALF)
    out_ref[...] = counts.T.astype(HALF)


def process(
    half_ref, state_ref, on_ref, off_ref, counts_ref, self_ref, near_ref,
    final_ref, pre_0_ref, pre_1_ref, half_1_ref, nearby_0_ref, nearby_1_ref, whole_ref,
):
    rim = on_ref.shape[0]
    count = half_ref.shape[0]
    own = slice(rim, rim + count)
    odd = odd_along("dom")
    left = jnp.where(odd, on_ref[...], off_ref[...])
    right = jnp.where(odd, off_ref[...], on_ref[...])
    whole_ref[:rim] = left
    whole_ref[own] = half_ref[...]
    whole_ref[rim + count :] = right
    half_0 = whole_ref[...]
    nearby_0 = (matmul(counts_ref[...], half_0) * (1.0 / NEAR)).astype(HALF)
    nearby_0_ref[...] = nearby_0[own]
    pre_0 = matmul(half_0, self_ref[0]) + matmul(nearby_0, near_ref[0])
    pre_0_ref[...] = pre_0
    grown = pre_0 * jax.nn.sigmoid(pre_0)
    state_1 = state_ref[...] + grown[own]
    half_1 = state_1.astype(HALF)
    whole_ref[:rim] = (left.astype(SINGLE) + grown[:rim]).astype(HALF)
    whole_ref[own] = half_1
    whole_ref[rim + count :] = (right.astype(SINGLE) + grown[rim + count :]).astype(HALF)
    half_1_ref[...] = half_1
    nearby_1 = (matmul(counts_ref[own], whole_ref[...]) * (1.0 / NEAR)).astype(HALF)
    nearby_1_ref[...] = nearby_1
    pre_1 = matmul(half_1, self_ref[1]) + matmul(nearby_1, near_ref[1])
    pre_1_ref[...] = pre_1
    final_ref[...] = (state_1 + pre_1 * jax.nn.sigmoid(pre_1)).astype(HALF)


def grid_counts(send_ref, recv_ref, *refs):
    far, (out_ref, turned_ref) = refs[: GROUPS - 1], refs[GROUPS - 1 :]
    odd_dom, odd_band = odd_along("dom"), odd_along("band")
    step = send_ref.shape[0] // GROUPS
    recv = by_partner(slots_of(recv_ref[...]), odd_dom, odd_band, True)
    send = [send_ref[:step]] + [ref[step : 2 * step] for ref in far]
    grids, nodes = out_ref.shape[0], turned_ref.shape[0] // GROUPS
    for p in range(GROUPS):
        at = slice(p * nodes, (p + 1) * nodes)
        to, of = hot(grids, recv[p]), hot(nodes, send[p])
        out_ref[:, at] = back_mul(to, of).astype(HALF)
        turned_ref[at] = back_mul(of, to).astype(HALF)


def mesh_counts(send_ref, recv_ref, *refs):
    far, out_ref = refs[: GROUPS - 1], refs[GROUPS - 1]
    step = send_ref.shape[0] // GROUPS
    send = by_partner(slots_of(send_ref[...]), odd_along("dom"), odd_along("band"), False)
    recv = [recv_ref[:step]] + [ref[:step] for ref in far]
    grids, nodes = out_ref.shape[0], out_ref.shape[1] // GROUPS
    for p in range(GROUPS):
        out_ref[:, p * nodes : (p + 1) * nodes] = pair_counts(send[p], grids, recv[p], nodes)


def decode(*refs):
    finals = refs[:GROUPS]
    counts_ref, turned_ref, weight_ref, back_ref = refs[GROUPS : GROUPS + 4]
    in_ref, hidden_ref, grad_ref, own_ref, *outs = refs[GROUPS + 4 :]
    nodes = own_ref.shape[0]
    total = matmul(counts_ref[:, :nodes], finals[0][...])
    for p in range(1, GROUPS):
        total = total + matmul(counts_ref[:, p * nodes : (p + 1) * nodes], finals[p][...])
    decode_in = total.astype(HALF)
    in_ref[...] = decode_in
    pre = matmul(decode_in, weight_ref[...])
    sigma = jax.nn.sigmoid(pre)
    hidden_ref[...] = (pre * sigma).astype(HALF)
    grad = (back_ref[...] * (sigma * (1.0 + pre * (1.0 - sigma)))).astype(HALF)
    grad_ref[...] = grad
    in_grad = back_mul(grad, weight_ref[...]).astype(HALF)
    own_ref[...] = matmul(turned_ref[:nodes], in_grad)
    for p, out in enumerate(outs):
        out[...] = matmul(turned_ref[(p + 1) * nodes : (p + 2) * nodes], in_grad).astype(HALF)


def gather_back(*refs):
    total = refs[0][...]
    for ref in refs[1:GROUPS]:
        total = total + ref[...].astype(SINGLE)
    slope_ref, state_ref, layer_ref, on_ref, off_ref = refs[GROUPS:]
    state_ref[...] = total
    layer = (total * slope_ref[...]).astype(HALF)
    layer_ref[...] = layer
    half = total.astype(HALF)
    odd = odd_along("dom")
    rim, count = RIM, total.shape[0]
    heads = jnp.concatenate([layer[: 2 * rim], half[:rim]], 0)
    tails = jnp.concatenate([layer[count - 2 * rim :], half[count - rim :]], 0)
    on_ref[...] = jnp.where(odd, heads, tails)
    off_ref[...] = jnp.where(odd, tails, heads)


def process_back(
    state_ref, layer_ref, on_ref, off_ref, turned_ref, slope_0_ref, slope_in_ref,
    self_ref, near_ref, encode_ref, static_ref, layer_0_ref, encode_grad_ref, back_ref, whole_ref,
):
    rim = RIM
    count = state_ref.shape[0]
    own = slice(2 * rim, 2 * rim + count)
    odd = odd_along("dom")
    on, off = on_ref[...], off_ref[...]
    left, right = jnp.where(odd, on, off), jnp.where(odd, off, on)
    whole_ref[: 2 * rim] = left[: 2 * rim]
    whole_ref[own] = layer_ref[...]
    whole_ref[2 * rim + count :] = right[: 2 * rim]
    layer_1 = whole_ref[...]
    spread = (matmul(turned_ref[...], layer_1) * (1.0 / NEAR)).astype(HALF)
    back = back_mul(layer_1, self_ref[1]) + back_mul(spread, near_ref[1])
    state_own = state_ref[...] + back[own]
    first = left[2 * rim :].astype(SINGLE) + back[rim : 2 * rim]
    last = right[2 * rim :].astype(SINGLE) + back[2 * rim + count : 3 * rim + count]
    layer_0 = (state_own * slope_0_ref[own]).astype(HALF)
    layer_0_ref[...] = layer_0
    whole_ref[:rim] = jnp.zeros((rim, back.shape[1]), HALF)
    whole_ref[rim : 2 * rim] = (first * slope_0_ref[rim : 2 * rim]).astype(HALF)
    whole_ref[own] = layer_0
    whole_ref[2 * rim + count : 3 * rim + count] = (
        last * slope_0_ref[2 * rim + count : 3 * rim + count]
    ).astype(HALF)
    whole_ref[3 * rim + count :] = jnp.zeros((rim, back.shape[1]), HALF)
    spread = (matmul(turned_ref[own], whole_ref[...]) * (1.0 / NEAR)).astype(HALF)
    state = state_own + back_mul(layer_0, self_ref[0]) + back_mul(spread, near_ref[0])
    static_ref[...] = state
    grad = (state * slope_in_ref[...]).astype(HALF)
    encode_grad_ref[...] = grad
    back_ref[...] = back_mul(grad, encode_ref[...]).astype(HALF)


def split_rows(count):
    return -(-count // (2 * LANES)) * LANES


def store_halves(value, at, mine_ref, other_ref, wide_ref):
    odd = lax.axis_index("dom") % 2
    count, rows = value.shape[0], split_rows(value.shape[0])
    wide_ref[:count] = value
    if count < 2 * rows:
        wide_ref[count : 2 * rows] = jnp.zeros((2 * rows - count, value.shape[1]), SINGLE)
    mine = pl.ds(pl.multiple_of(odd * rows, rows), rows)
    other = pl.ds(pl.multiple_of((1 - odd) * rows, rows), rows)
    mine_ref[at : at + rows] = wide_ref[mine].astype(HALF)
    other_ref[at : at + rows] = wide_ref[other].astype(HALF)
    return at + rows


def gradient_halves(turned, *refs):
    mine_ref, other_ref, wide_ref = refs[-3:]
    at = 0
    for i, (left, right) in enumerate(zip(refs[:-3:2], refs[1:-3:2], strict=True)):
        product = matmul if i < turned else outer_sum
        value = product(left[...], right[...])
        at = store_halves(value, at, mine_ref, other_ref, wide_ref)


def embed_back(*refs):
    returned = refs[:GROUPS]
    counts_ref, slope_ref, grid_ref, mine_ref, other_ref, wide_ref = refs[GROUPS:]
    nodes = returned[0].shape[0]
    total = matmul(counts_ref[:, :nodes], returned[0][...])
    for p in range(1, GROUPS):
        total = total + matmul(counts_ref[:, p * nodes : (p + 1) * nodes], returned[p][...])
    grad = (total * slope_ref[...]).astype(HALF)
    store_halves(matmul(grid_ref[...], grad), 0, mine_ref, other_ref, wide_ref)


def split_gradients(body, rows, macs, *args):
    width = args[1].shape[1]
    outs = [shape(rows, width, HALF)] * 2
    mine, other = whole(body, outs, macs, *args, scratch=[pltpu.VMEM((width, width), SINGLE)])
    return mine, swap_on(other)


def add_halves(*refs):
    out_ref = refs[-1]
    at = 0
    for mine, other in zip(refs[:-1:2], refs[1:-1:2], strict=True):
        rows = mine.shape[0]
        out_ref[at : at + rows] = (
            mine[...].astype(SINGLE) + other[...].astype(SINGLE)
        ).astype(HALF)
        at += rows


def add_pieces(pieces_ref, out_ref):
    total = pieces_ref[0].astype(SINGLE)
    for i in range(1, pieces_ref.shape[0]):
        total = total + pieces_ref[i].astype(SINGLE)
    out_ref[...] = total.astype(HALF)


def add_bands(*refs):
    out_ref = refs[-1]
    total = refs[0][...].astype(SINGLE)
    for ref in refs[1:-1]:
        total = total + ref[...].astype(SINGLE)
    total = total.astype(HALF)
    for i in range(out_ref.shape[0]):
        out_ref[i] = total


def unpack(part_ref, other_ref, *outs):
    odd = odd_along("dom")
    at = 0
    for out, which, rows in outs_of(outs):
        own = part_ref[at : at + rows].astype(SINGLE)
        far = other_ref[at : at + rows].astype(SINGLE)
        top, bottom = jnp.where(odd, far, own), jnp.where(odd, own, far)
        if which is None:
            out[:rows] = top
            out[rows:] = bottom[: out.shape[0] - rows]
        else:
            out[which, :rows] = top
            out[which, rows:] = bottom
        at += rows


def outs_of(outs):
    embed, encode, self_, near, decode, output = outs
    half = encode.shape[0] // 2
    narrow = -(-embed.shape[0] // (2 * LANES)) * LANES
    return [
        (output, None, narrow),
        (decode, None, half),
        (self_, 1, half),
        (near, 1, half),
        (self_, 0, half),
        (near, 0, half),
        (encode, None, half),
        (embed, None, narrow),
    ]


def reduce_all(part):
    count = lax.axis_size("dom")
    bands = lax.axis_size("band")
    groups = [list(range(c, count, 2)) for c in range(2)]
    chips = count // 2
    rows, width = part.shape[0] // chips, part.shape[1]
    pieces = lax.all_to_all(
        part.reshape(chips, rows, width), "dom", 0, 0, axis_index_groups=groups
    )
    (piece,) = whole(add_pieces, [shape(rows, width, HALF)], 0, pieces)
    others = [
        lax.ppermute(piece, "band", [(i, (i + step) % bands) for i in range(bands)])
        for step in range(1, bands)
    ]
    copies = jax.ShapeDtypeStruct((chips, rows, width), HALF)
    (copies,) = whole(add_bands, [copies], 0, piece, *others)
    return lax.all_to_all(copies, "dom", 0, 0, axis_index_groups=groups).reshape(part.shape)


def shards(
    grid_vars,
    cotangent,
    mesh_static,
    embed_weight,
    encode_weight,
    self_weight,
    neighbor_weight,
    decode_weight,
    output_weight,
    grid_sender,
    mesh_receiver,
    neighbors,
    mesh_sender,
    grid_receiver,
):
    grid_count, variables = grid_vars.shape
    mesh_count, width = mesh_static.shape
    rim = 2 * RIM
    ext = mesh_count + 2 * rim
    grid, cot, near, out_weight = grid_vars.T, cotangent.T, neighbors.T, output_weight.T
    grid_send, mesh_recv, mesh_send, grid_recv = (
        index.reshape(-1, LANES) for index in (grid_sender, mesh_receiver, mesh_sender, grid_receiver)
    )
    step = grid_send.shape[0] // GROUPS * LANES
    nodes = GROUPS * mesh_count
    mesh_rows = shape(mesh_count, width, HALF)
    mesh_full = shape(mesh_count, width, SINGLE)
    grid_rows = shape(grid_count, width, HALF)
    grid_full = shape(grid_count, width, SINGLE)
    parcel = shape(variables + -variables % 16 + INDEX_ROWS // 2, grid_count, HALF)
    sent = fetching(
        parcels, [parcel] * (GROUPS - 1), 0, grid, grid_send, mesh_recv, mesh_send, near
    )
    arrived = swap_all(*sent)
    embed_macs = grid_count * variables * width + mesh_count * grid_count * (step + width)
    slope_embed, total = fetching(
        embed_own, [grid_full, mesh_full], embed_macs, grid, embed_weight, grid_send, mesh_recv
    )
    index = [None] * GROUPS
    for p in range(1, GROUPS):
        index[p], total = whole(
            lambda *refs, p=p: embed_far(p, *refs),
            [shape(INDEX_ROWS, LANES, jnp.int32), mesh_full],
            embed_macs,
            arrived[p - 1],
            embed_weight,
            mesh_recv,
            total,
        )
    encode_in, slope_encode, state, half, on, off = whole(
        encode,
        [mesh_rows, mesh_full, mesh_full, mesh_rows] + [shape(rim, width, HALF)] * 2,
        mesh_count * width * width,
        total,
        encode_weight,
        mesh_static,
    )
    on, off = swap_on(on), swap_off(off)
    counts, turned = whole(
        near_counts, [shape(ext, ext, HALF)] * 2, ext * ext * 64, near, index[1], index[2]
    )
    final_half, pre_0, pre_1, half_1, nearby_0, nearby_1 = whole(
        process,
        [mesh_rows, shape(ext, width, SINGLE), mesh_full, mesh_rows, mesh_rows, mesh_rows],
        (ext + mesh_count) * (ext + 2 * width) * width,
        half,
        state,
        on,
        off,
        counts,
        self_weight,
        neighbor_weight,
        scratch=[pltpu.VMEM((ext, width), HALF)],
    )
    finals = (final_half,) + swap_all(*[final_half] * 4)
    to_grid, from_grid = whole(
        grid_counts,
        [shape(grid_count, nodes, HALF), shape(nodes, grid_count, HALF)],
        2 * nodes * grid_count * step,
        mesh_send,
        grid_recv,
        *index[1:],
    )
    hidden_grad = outer_sum(cot, out_weight)
    decode_in, hidden, decode_grad, state_grad, *sums = whole(
        decode,
        [grid_rows] * 3 + [mesh_full] + [mesh_rows] * (GROUPS - 1),
        2 * grid_count * width * (nodes + width),
        *finals,
        to_grid,
        from_grid,
        decode_weight,
        hidden_grad,
    )
    arrived = swap_all(*sums)
    prediction = (grid.astype(SINGLE) + back_mul(out_weight, hidden)).astype(HALF)
    half_rows = split_rows(width)
    narrow_rows = split_rows(variables)
    square = width * width
    halves = [
        *split_gradients(
            lambda *refs: gradient_halves(1, *refs),
            narrow_rows + half_rows,
            2 * grid_count * square,
            cot,
            hidden,
            decode_in,
            decode_grad,
        )
    ]
    state_grad, layer_1, on, off = whole(
        gather_back,
        [mesh_full, mesh_rows] + [shape(rim + RIM, width, HALF)] * 2,
        0,
        state_grad,
        *arrived,
        silu_slope(pre_1),
    )
    on, off = swap_on(on), swap_off(off)
    state_grad, layer_0, encode_grad, encode_in_grad = whole(
        process_back,
        [mesh_full, mesh_rows, mesh_rows, mesh_rows],
        (ext + mesh_count) * (ext + 2 * width) * width,
        state_grad,
        layer_1,
        on,
        off,
        turned,
        silu_slope(pre_0),
        slope_encode,
        self_weight,
        neighbor_weight,
        encode_weight,
        scratch=[pltpu.VMEM((ext, width), HALF)],
    )
    returned = (encode_in_grad,) + swap_all(*[encode_in_grad] * 4)
    to_mesh = whole(
        mesh_counts,
        [shape(grid_count, nodes, HALF)],
        nodes * grid_count * step,
        grid_send,
        mesh_recv,
        *index[1:],
    )[0]
    layer_1, encode_grad = lax.optimization_barrier((layer_1, encode_grad))
    halves += split_gradients(
        lambda *refs: gradient_halves(0, *refs),
        5 * half_rows,
        5 * mesh_count * square,
        half_1,
        layer_1,
        nearby_1,
        layer_1,
        half,
        layer_0,
        nearby_0,
        layer_0,
        encode_in,
        encode_grad,
    )
    halves += split_gradients(
        embed_back,
        narrow_rows,
        grid_count * width * (nodes + variables),
        *returned,
        to_mesh,
        slope_embed,
        grid,
    )
    rows = sum(block.shape[0] for block in halves[::2])
    (part,) = whole(add_halves, [shape(rows, width, HALF)], 0, *halves)
    part = reduce_all(part)
    other = swap_on(part)
    full = shape(width, width, SINGLE)
    pair = jax.ShapeDtypeStruct((2, width, width), SINGLE)
    narrow = shape(variables, width, SINGLE)
    grad_embed, grad_encode, grad_self, grad_near, grad_decode, grad_output = whole(
        unpack, [narrow, full, pair, pair, full, narrow], 0, part, other
    )
    return (
        prediction.T,
        state_grad,
        grad_embed,
        grad_encode,
        grad_self,
        grad_near,
        grad_decode,
        grad_output.T,
    )


def solution(mesh):
    placed = (
        P(("band", "dom"), None),
        P(("band", "dom"), None),
        P(("band", "dom"), None),
        P(),
        P(),
        P(),
        P(),
        P(),
        P(),
        P(("band", "dom")),
        P(("band", "dom")),
        P(("band", "dom"), None),
        P(("band", "dom")),
        P(("band", "dom")),
    )
    return jax.shard_map(
        shards,
        mesh=mesh,
        in_specs=placed,
        out_specs=(
            P(("band", "dom"), None),
            P(("band", "dom"), None),
            P(),
            P(),
            P(),
            P(),
            P(),
            P(),
        ),
        check_vma=False,
    )
```

```python
import jax
import jax.numpy as jnp
from jax import lax
from jax.experimental import pallas as pl
from jax.experimental.pallas import tpu as pltpu
from jax.sharding import PartitionSpec as P

NEAR = 6
RIM = 64
GROUPS = 5
LANES = 128
HALF = jnp.bfloat16
SINGLE = jnp.float32
MIB = 1024 * 1024
SLOT_ROWS = 6
INDEX_ROWS = 32


def silu_slope(values):
    sigma = jax.nn.sigmoid(values)
    return sigma * (1.0 + values * (1.0 - sigma))


def matmul(left, right):
    return jnp.dot(left, right, preferred_element_type=SINGLE)


def outer_sum(left, right):
    return lax.dot_general(
        left, right, (((0,), (0,)), ((), ())), preferred_element_type=SINGLE
    )


def back_mul(left, right):
    return lax.dot_general(
        left, right, (((1,), (1,)), ((), ())), preferred_element_type=SINGLE
    )


def swap_on(value):
    count = lax.axis_size("dom")
    return lax.ppermute(value, "dom", [(i, i ^ 1) for i in range(count)])


def swap_off(value):
    count = lax.axis_size("dom")
    return lax.ppermute(
        value, "dom", [(i, (i + (1 if i % 2 else -1)) % count) for i in range(count)]
    )


def swap_band(value, first):
    count = lax.axis_size("band")
    pairs = []
    for low in range(first, count - 1, 2):
        pairs += [(low, low + 1), (low + 1, low)]
    return lax.ppermute(value, "band", pairs)


def swap_all(on, off, north, south):
    south = swap_band(south, 1)
    north = swap_band(north, 0)
    off = swap_off(off)
    return swap_on(on), off, north, south


def by_partner(slots, odd_dom, odd_band, incoming):
    flip_dom = odd_dom != incoming
    flip_band = odd_band != incoming
    return [
        slots[0],
        jnp.where(flip_dom, slots[2], slots[1]),
        jnp.where(flip_dom, slots[1], slots[2]),
        jnp.where(flip_band, slots[4], slots[3]),
        jnp.where(flip_band, slots[3], slots[4]),
    ]


def whole(body, outs, macs, *args, limit=32, scratch=()):
    moved = sum(a.size * a.dtype.itemsize for a in (*args, *outs))
    return pl.pallas_call(
        body,
        out_shape=outs,
        scratch_shapes=scratch,
        compiler_params=pltpu.CompilerParams(vmem_limit_bytes=limit * MIB),
        cost_estimate=pl.CostEstimate(flops=2 * macs, bytes_accessed=moved, transcendentals=0),
    )(*args)


def shape(rows, columns, kind):
    return jax.ShapeDtypeStruct((rows, columns), kind)


def odd_along(axis):
    return lax.axis_index(axis) % 2 == 1


def hot(rows, index):
    spots = lax.broadcasted_iota(jnp.int32, (rows, LANES), 0)
    one = [
        jnp.where(spots == index[j : j + 1], 1.0, 0.0).astype(HALF) for j in range(index.shape[0])
    ]
    return jnp.concatenate(one, 1)


def pair_counts(rows, row_count, columns, column_count):
    return back_mul(hot(row_count, rows), hot(column_count, columns)).astype(HALF)


def slots_of(index):
    step = index.shape[0] // GROUPS
    return [index[k * step : (k + 1) * step] for k in range(GROUPS)]


def fetch(sources, buffers, sems):
    copies = [
        pltpu.make_async_copy(source, buffer, sems.at[i])
        for i, (source, buffer) in enumerate(zip(sources, buffers, strict=True))
    ]
    for copy in copies:
        copy.start()
    for copy in copies:
        copy.wait()


def fetching(body, outs, macs, *args):
    moved = sum(a.size * a.dtype.itemsize for a in (*args, *outs))
    return pl.pallas_call(
        body,
        out_shape=outs,
        in_specs=[pl.BlockSpec(memory_space=pltpu.HBM)] * len(args),
        scratch_shapes=[pltpu.VMEM(a.shape, a.dtype) for a in args]
        + [pltpu.SemaphoreType.DMA((len(args),))],
        compiler_params=pltpu.CompilerParams(vmem_limit_bytes=32 * MIB),
        cost_estimate=pl.CostEstimate(flops=2 * macs, bytes_accessed=moved, transcendentals=0),
    )(*args)


def parcels(*refs):
    inputs, rest = refs[:4], refs[4:]
    outs, buffers, sems = rest[: GROUPS - 1], rest[GROUPS - 1 : -1], rest[-1]
    fetch(inputs, buffers, sems)
    grid_ref, grid_send_ref, mesh_send_ref, near_ref = buffers
    odd_dom, odd_band = odd_along("dom"), odd_along("band")
    grid_send = by_partner(slots_of(grid_send_ref[...]), odd_dom, odd_band, False)
    mesh_send = by_partner(slots_of(mesh_send_ref[...]), odd_dom, odd_band, False)
    near = near_ref[...]
    near = [near[:, j : j + LANES] for j in range(0, near.shape[1], LANES)]
    variables, count = grid_ref.shape
    first = outs[0].shape[0] - INDEX_ROWS // 2
    grid = grid_ref[...]
    for p, out in enumerate(outs):
        parts = [mesh_send[p + 1], grid_send[p + 1], *near]
        used = sum(part.shape[0] for part in parts)
        parts.append(jnp.zeros((INDEX_ROWS - used, LANES), jnp.int32))
        index = jnp.concatenate(parts, 0)
        high = (index >> 1).astype(SINGLE)
        low = (index & 1).astype(SINGLE)
        cut = INDEX_ROWS // 2
        out[:variables] = grid
        out[variables:first] = jnp.zeros((first - variables, count), HALF)
        out[first:] = jnp.concatenate([high[:cut], low[:cut], high[cut:], low[cut:]], 1).astype(HALF)


def index_of(packed):
    packed = packed.astype(SINGLE)
    halves = [
        packed[:, j : j + LANES] * 2.0 + packed[:, j + LANES : j + 2 * LANES]
        for j in (0, 2 * LANES)
    ]
    return jnp.concatenate(halves, 0).astype(jnp.int32)


def embed_own(*refs):
    inputs, (slope_ref, sum_ref), buffers, sems = refs[:4], refs[4:6], refs[6:-1], refs[-1]
    fetch(inputs, buffers, sems)
    grid_ref, weight_ref, send_ref, recv_ref = buffers
    step = send_ref.shape[0] // GROUPS
    counts = pair_counts(
        recv_ref[:step], sum_ref.shape[0], send_ref[:step], grid_ref.shape[1]
    )
    pre = outer_sum(grid_ref[...], weight_ref[...])
    sigma = jax.nn.sigmoid(pre)
    slope_ref[...] = sigma * (1.0 + pre * (1.0 - sigma))
    sum_ref[...] = matmul(counts, (pre * sigma).astype(HALF))


def embed_far(p, parcel_ref, weight_ref, recv_ref, sum_ref, index_ref, slope_ref, out_ref):
    index = index_of(parcel_ref[parcel_ref.shape[0] - INDEX_ROWS // 2 :])
    index_ref[...] = index
    step = recv_ref.shape[0] // GROUPS
    recv = by_partner(slots_of(recv_ref[...]), odd_along("dom"), odd_along("band"), True)[p]
    counts = pair_counts(
        recv, out_ref.shape[0], index[step : 2 * step], parcel_ref.shape[1]
    )
    pre = outer_sum(parcel_ref[: weight_ref.shape[0]], weight_ref[...])
    sigma = jax.nn.sigmoid(pre)
    slope_ref[...] = sigma * (1.0 + pre * (1.0 - sigma))
    out_ref[...] = sum_ref[...] + matmul(counts, (pre * sigma).astype(HALF))


def encode(sum_ref, weight_ref, static_ref, in_ref, slope_ref, state_ref, half_ref, on_ref, off_ref):
    encode_in = sum_ref[...].astype(HALF)
    pre = matmul(encode_in, weight_ref[...])
    sigma = jax.nn.sigmoid(pre)
    state = static_ref[...].astype(SINGLE) + pre * sigma
    half = state.astype(HALF)
    in_ref[...] = encode_in
    slope_ref[...] = sigma * (1.0 + pre * (1.0 - sigma))
    state_ref[...] = state
    half_ref[...] = half
    rows = on_ref.shape[0]
    odd = odd_along("dom")
    head, tail = half[:rows], half[half.shape[0] - rows :]
    on_ref[...] = jnp.where(odd, head, tail)
    off_ref[...] = jnp.where(odd, tail, head)


def near_counts(near_ref, on_ref, off_ref, out_ref, turned_ref):
    step = near_ref.shape[0]
    mesh_count = near_ref.shape[1]
    first = 2 * SLOT_ROWS
    odd_dom = odd_along("dom")
    on, off = on_ref[...], off_ref[...]
    left = jnp.where(odd_dom, on, off)[first + step : first + 2 * step] + (RIM - mesh_count)
    right = jnp.where(odd_dom, off, on)[first : first + step] + (RIM + mesh_count)
    own = near_ref[...] + RIM
    index = jnp.concatenate([left, own, right], 1)
    spots = lax.broadcasted_iota(jnp.int32, out_ref.shape, 0)
    counts = jnp.zeros(out_ref.shape, SINGLE)
    for j in range(step):
        counts = counts + jnp.where(spots == index[j : j + 1], 1.0, 0.0)
    turned_ref[...] = counts.astype(HALF)
    out_ref[...] = counts.T.astype(HALF)


def process(
    half_ref, state_ref, on_ref, off_ref, counts_ref, self_ref, near_ref,
    final_ref, pre_0_ref, pre_1_ref, half_1_ref, nearby_0_ref, nearby_1_ref, whole_ref,
):
    rim = on_ref.shape[0]
    count = half_ref.shape[0]
    own = slice(rim, rim + count)
    odd = odd_along("dom")
    left = jnp.where(odd, on_ref[...], off_ref[...])
    right = jnp.where(odd, off_ref[...], on_ref[...])
    whole_ref[:rim] = left
    whole_ref[own] = half_ref[...]
    whole_ref[rim + count :] = right
    half_0 = whole_ref[...]
    nearby_0 = (matmul(counts_ref[...], half_0) * (1.0 / NEAR)).astype(HALF)
    nearby_0_ref[...] = nearby_0[own]
    pre_0 = matmul(half_0, self_ref[0]) + matmul(nearby_0, near_ref[0])
    pre_0_ref[...] = pre_0
    grown = pre_0 * jax.nn.sigmoid(pre_0)
    state_1 = state_ref[...] + grown[own]
    half_1 = state_1.astype(HALF)
    whole_ref[:rim] = (left.astype(SINGLE) + grown[:rim]).astype(HALF)
    whole_ref[own] = half_1
    whole_ref[rim + count :] = (right.astype(SINGLE) + grown[rim + count :]).astype(HALF)
    half_1_ref[...] = half_1
    nearby_1 = (matmul(counts_ref[own], whole_ref[...]) * (1.0 / NEAR)).astype(HALF)
    nearby_1_ref[...] = nearby_1
    pre_1 = matmul(half_1, self_ref[1]) + matmul(nearby_1, near_ref[1])
    pre_1_ref[...] = pre_1
    final_ref[...] = (state_1 + pre_1 * jax.nn.sigmoid(pre_1)).astype(HALF)


def grid_counts(send_ref, recv_ref, *refs):
    far, (out_ref, turned_ref) = refs[: GROUPS - 1], refs[GROUPS - 1 :]
    odd_dom, odd_band = odd_along("dom"), odd_along("band")
    step = send_ref.shape[0] // GROUPS
    recv = by_partner(slots_of(recv_ref[...]), odd_dom, odd_band, True)
    send = [send_ref[:step]] + [ref[:step] for ref in far]
    grids, nodes = out_ref.shape[0], turned_ref.shape[0] // GROUPS
    for p in range(GROUPS):
        at = slice(p * nodes, (p + 1) * nodes)
        to, of = hot(grids, recv[p]), hot(nodes, send[p])
        out_ref[:, at] = back_mul(to, of).astype(HALF)
        turned_ref[at] = back_mul(of, to).astype(HALF)


def mesh_counts(send_ref, recv_ref, *refs):
    far, out_ref = refs[: GROUPS - 1], refs[GROUPS - 1]
    step = send_ref.shape[0] // GROUPS
    send = [send_ref[:step]] + [ref[step : 2 * step] for ref in far]
    recv = by_partner(slots_of(recv_ref[...]), odd_along("dom"), odd_along("band"), True)
    grids, nodes = out_ref.shape[0], out_ref.shape[1] // GROUPS
    for p in range(GROUPS):
        out_ref[:, p * nodes : (p + 1) * nodes] = pair_counts(send[p], grids, recv[p], nodes)


def decode(*refs):
    finals = refs[:GROUPS]
    counts_ref, turned_ref, weight_ref, back_ref = refs[GROUPS : GROUPS + 4]
    in_ref, hidden_ref, grad_ref, own_ref, *outs = refs[GROUPS + 4 :]
    nodes = own_ref.shape[0]
    total = matmul(counts_ref[:, :nodes], finals[0][...])
    for p in range(1, GROUPS):
        total = total + matmul(counts_ref[:, p * nodes : (p + 1) * nodes], finals[p][...])
    decode_in = total.astype(HALF)
    in_ref[...] = decode_in
    pre = matmul(decode_in, weight_ref[...])
    sigma = jax.nn.sigmoid(pre)
    hidden_ref[...] = (pre * sigma).astype(HALF)
    grad = (back_ref[...] * (sigma * (1.0 + pre * (1.0 - sigma)))).astype(HALF)
    grad_ref[...] = grad
    in_grad = back_mul(grad, weight_ref[...]).astype(HALF)
    own_ref[...] = matmul(turned_ref[:nodes], in_grad)
    for p, out in enumerate(outs):
        out[...] = matmul(turned_ref[(p + 1) * nodes : (p + 2) * nodes], in_grad).astype(HALF)


def gather_back(*refs):
    total = refs[0][...]
    for ref in refs[1:GROUPS]:
        total = total + ref[...].astype(SINGLE)
    slope_ref, state_ref, layer_ref, on_ref, off_ref = refs[GROUPS:]
    state_ref[...] = total
    layer = (total * slope_ref[...]).astype(HALF)
    layer_ref[...] = layer
    half = total.astype(HALF)
    odd = odd_along("dom")
    rim, count = RIM, total.shape[0]
    heads = jnp.concatenate([layer[: 2 * rim], half[:rim]], 0)
    tails = jnp.concatenate([layer[count - 2 * rim :], half[count - rim :]], 0)
    on_ref[...] = jnp.where(odd, heads, tails)
    off_ref[...] = jnp.where(odd, tails, heads)


def process_back(
    state_ref, layer_ref, on_ref, off_ref, turned_ref, slope_0_ref, slope_in_ref,
    self_ref, near_ref, encode_ref, static_ref, layer_0_ref, encode_grad_ref, back_ref, whole_ref,
):
    rim = RIM
    count = state_ref.shape[0]
    own = slice(2 * rim, 2 * rim + count)
    odd = odd_along("dom")
    on, off = on_ref[...], off_ref[...]
    left, right = jnp.where(odd, on, off), jnp.where(odd, off, on)
    whole_ref[: 2 * rim] = left[: 2 * rim]
    whole_ref[own] = layer_ref[...]
    whole_ref[2 * rim + count :] = right[: 2 * rim]
    layer_1 = whole_ref[...]
    spread = (matmul(turned_ref[...], layer_1) * (1.0 / NEAR)).astype(HALF)
    back = back_mul(layer_1, self_ref[1]) + back_mul(spread, near_ref[1])
    state_own = state_ref[...] + back[own]
    first = left[2 * rim :].astype(SINGLE) + back[rim : 2 * rim]
    last = right[2 * rim :].astype(SINGLE) + back[2 * rim + count : 3 * rim + count]
    layer_0 = (state_own * slope_0_ref[own]).astype(HALF)
    layer_0_ref[...] = layer_0
    whole_ref[:rim] = jnp.zeros((rim, back.shape[1]), HALF)
    whole_ref[rim : 2 * rim] = (first * slope_0_ref[rim : 2 * rim]).astype(HALF)
    whole_ref[own] = layer_0
    whole_ref[2 * rim + count : 3 * rim + count] = (
        last * slope_0_ref[2 * rim + count : 3 * rim + count]
    ).astype(HALF)
    whole_ref[3 * rim + count :] = jnp.zeros((rim, back.shape[1]), HALF)
    spread = (matmul(turned_ref[own], whole_ref[...]) * (1.0 / NEAR)).astype(HALF)
    state = state_own + back_mul(layer_0, self_ref[0]) + back_mul(spread, near_ref[0])
    static_ref[...] = state
    grad = (state * slope_in_ref[...]).astype(HALF)
    encode_grad_ref[...] = grad
    back_ref[...] = back_mul(grad, encode_ref[...]).astype(HALF)


def split_rows(count):
    return -(-count // (2 * LANES)) * LANES


def store_halves(value, at, mine_ref, other_ref, wide_ref):
    odd = lax.axis_index("dom") % 2
    count, rows = value.shape[0], split_rows(value.shape[0])
    wide_ref[:count] = value
    if count < 2 * rows:
        wide_ref[count : 2 * rows] = jnp.zeros((2 * rows - count, value.shape[1]), SINGLE)
    mine = pl.ds(pl.multiple_of(odd * rows, rows), rows)
    other = pl.ds(pl.multiple_of((1 - odd) * rows, rows), rows)
    mine_ref[at : at + rows] = wide_ref[mine].astype(HALF)
    other_ref[at : at + rows] = wide_ref[other].astype(HALF)
    return at + rows


def gradient_halves(turned, *refs):
    mine_ref, other_ref, wide_ref = refs[-3:]
    at = 0
    for i, (left, right) in enumerate(zip(refs[:-3:2], refs[1:-3:2], strict=True)):
        product = matmul if i < turned else outer_sum
        value = product(left[...], right[...])
        at = store_halves(value, at, mine_ref, other_ref, wide_ref)


def embed_back(*refs):
    back_ref, counts_ref = refs[:2]
    slopes, grids = refs[2 : 2 + GROUPS], refs[2 + GROUPS : 2 + 2 * GROUPS]
    mine_ref, other_ref, wide_ref = refs[2 + 2 * GROUPS :]
    nodes = back_ref.shape[0]
    variables = grids[0].shape[0]
    total = None
    for p in range(GROUPS):
        latent = matmul(counts_ref[:, p * nodes : (p + 1) * nodes], back_ref[...])
        grad = (latent * slopes[p][...]).astype(HALF)
        term = matmul(grids[p][:variables], grad)
        total = term if total is None else total + term
    store_halves(total, 0, mine_ref, other_ref, wide_ref)


def split_gradients(body, rows, width, macs, *args):
    outs = [shape(rows, width, HALF)] * 2
    return whole(body, outs, macs, *args, scratch=[pltpu.VMEM((width, width), SINGLE)])


def add_halves(*refs):
    out_ref = refs[-1]
    at = 0
    for mine, other in zip(refs[:-1:2], refs[1:-1:2], strict=True):
        rows = mine.shape[0]
        out_ref[at : at + rows] = (
            mine[...].astype(SINGLE) + other[...].astype(SINGLE)
        ).astype(HALF)
        at += rows


def add_pieces(pieces_ref, out_ref):
    total = pieces_ref[0].astype(SINGLE)
    for i in range(1, pieces_ref.shape[0]):
        total = total + pieces_ref[i].astype(SINGLE)
    out_ref[...] = total.astype(HALF)


def add_bands(*refs):
    out_ref = refs[-1]
    total = refs[0][...].astype(SINGLE)
    for ref in refs[1:-1]:
        total = total + ref[...].astype(SINGLE)
    total = total.astype(HALF)
    for i in range(out_ref.shape[0]):
        out_ref[i] = total


def unpack(part_ref, other_ref, *outs):
    odd = odd_along("dom")
    at = 0
    for out, which, rows in outs_of(outs):
        own = part_ref[at : at + rows].astype(SINGLE)
        far = other_ref[at : at + rows].astype(SINGLE)
        top, bottom = jnp.where(odd, far, own), jnp.where(odd, own, far)
        if which is None:
            out[:rows] = top
            out[rows:] = bottom[: out.shape[0] - rows]
        else:
            out[which, :rows] = top
            out[which, rows:] = bottom
        at += rows


def outs_of(outs):
    embed, encode, self_, near, decode, output = outs
    half = encode.shape[0] // 2
    narrow = -(-embed.shape[0] // (2 * LANES)) * LANES
    return [
        (output, None, narrow),
        (decode, None, half),
        (self_, 1, half),
        (near, 1, half),
        (self_, 0, half),
        (near, 0, half),
        (encode, None, half),
        (embed, None, narrow),
    ]


def reduce_all(part):
    count = lax.axis_size("dom")
    bands = lax.axis_size("band")
    groups = [list(range(c, count, 2)) for c in range(2)]
    chips = count // 2
    rows, width = part.shape[0] // chips, part.shape[1]
    pieces = lax.all_to_all(
        part.reshape(chips, rows, width), "dom", 0, 0, axis_index_groups=groups
    )
    (piece,) = whole(add_pieces, [shape(rows, width, HALF)], 0, pieces)
    others = [
        lax.ppermute(piece, "band", [(i, (i + step) % bands) for i in range(bands)])
        for step in range(1, bands)
    ]
    copies = jax.ShapeDtypeStruct((chips, rows, width), HALF)
    (copies,) = whole(add_bands, [copies], 0, piece, *others)
    return lax.all_to_all(copies, "dom", 0, 0, axis_index_groups=groups).reshape(part.shape)


def shards(
    grid_vars,
    cotangent,
    mesh_static,
    embed_weight,
    encode_weight,
    self_weight,
    neighbor_weight,
    decode_weight,
    output_weight,
    grid_sender,
    mesh_receiver,
    neighbors,
    mesh_sender,
    grid_receiver,
):
    grid_count, variables = grid_vars.shape
    mesh_count, width = mesh_static.shape
    rim = 2 * RIM
    ext = mesh_count + 2 * rim
    grid, cot, near, out_weight = grid_vars.T, cotangent.T, neighbors.T, output_weight.T
    grid_send, mesh_recv, mesh_send, grid_recv = (
        index.reshape(-1, LANES) for index in (grid_sender, mesh_receiver, mesh_sender, grid_receiver)
    )
    step = grid_send.shape[0] // GROUPS * LANES
    nodes = GROUPS * mesh_count
    mesh_rows = shape(mesh_count, width, HALF)
    mesh_full = shape(mesh_count, width, SINGLE)
    grid_rows = shape(grid_count, width, HALF)
    grid_full = shape(grid_count, width, SINGLE)
    parcel = shape(variables + -variables % 16 + INDEX_ROWS // 2, grid_count, HALF)
    sent = fetching(
        parcels, [parcel] * (GROUPS - 1), 0, grid, grid_send, mesh_send, near
    )
    arrived = swap_all(*sent)
    embed_macs = grid_count * variables * width + mesh_count * grid_count * (step + width)
    slope_embed, total = fetching(
        embed_own, [grid_full, mesh_full], embed_macs, grid, embed_weight, grid_send, mesh_recv
    )
    index = [None] * GROUPS
    slopes = [slope_embed] + [None] * (GROUPS - 1)
    grids = [grid, *arrived]
    for p in range(1, GROUPS):
        index[p], slopes[p], total = whole(
            lambda *refs, p=p: embed_far(p, *refs),
            [shape(INDEX_ROWS, LANES, jnp.int32), grid_full, mesh_full],
            embed_macs,
            arrived[p - 1],
            embed_weight,
            mesh_recv,
            total,
        )
    encode_in, slope_encode, state, half, on, off = whole(
        encode,
        [mesh_rows, mesh_full, mesh_full, mesh_rows] + [shape(rim, width, HALF)] * 2,
        mesh_count * width * width,
        total,
        encode_weight,
        mesh_static,
    )
    off = swap_off(off)
    on = swap_on(on)
    counts, turned = whole(
        near_counts, [shape(ext, ext, HALF)] * 2, ext * ext * 64, near, index[1], index[2]
    )
    final_half, pre_0, pre_1, half_1, nearby_0, nearby_1 = whole(
        process,
        [mesh_rows, shape(ext, width, SINGLE), mesh_full, mesh_rows, mesh_rows, mesh_rows],
        (ext + mesh_count) * (ext + 2 * width) * width,
        half,
        state,
        on,
        off,
        counts,
        self_weight,
        neighbor_weight,
        scratch=[pltpu.VMEM((ext, width), HALF)],
    )
    finals = (final_half,) + swap_all(*[final_half] * 4)
    to_grid, from_grid = whole(
        grid_counts,
        [shape(grid_count, nodes, HALF), shape(nodes, grid_count, HALF)],
        2 * nodes * grid_count * step,
        mesh_send,
        grid_recv,
        *index[1:],
    )
    hidden_grad = outer_sum(cot, out_weight)
    decode_in, hidden, decode_grad, state_grad, *sums = whole(
        decode,
        [grid_rows] * 3 + [mesh_full] + [mesh_rows] * (GROUPS - 1),
        2 * grid_count * width * (nodes + width),
        *finals,
        to_grid,
        from_grid,
        decode_weight,
        hidden_grad,
    )
    arrived = swap_all(*sums)
    prediction = (grid.astype(SINGLE) + back_mul(out_weight, hidden)).astype(HALF)
    half_rows = split_rows(width)
    narrow_rows = split_rows(variables)
    square = width * width
    decode_halves = split_gradients(
        lambda *refs: gradient_halves(1, *refs),
        narrow_rows + half_rows,
        width,
        2 * grid_count * square,
        cot,
        hidden,
        decode_in,
        decode_grad,
    )
    state_grad, *decode_halves = lax.optimization_barrier((state_grad, *decode_halves))
    state_grad, layer_1, on, off = whole(
        gather_back,
        [mesh_full, mesh_rows] + [shape(rim + RIM, width, HALF)] * 2,
        0,
        state_grad,
        *arrived,
        silu_slope(pre_1),
    )
    off = swap_off(off)
    on = swap_on(on)
    layer_halves = split_gradients(
        lambda *refs: gradient_halves(0, *refs),
        2 * half_rows,
        width,
        2 * mesh_count * square,
        half_1,
        layer_1,
        nearby_1,
        layer_1,
    )
    state_grad, *layer_halves = lax.optimization_barrier((state_grad, *layer_halves))
    state_grad, layer_0, encode_grad, encode_in_grad = whole(
        process_back,
        [mesh_full, mesh_rows, mesh_rows, mesh_rows],
        (ext + mesh_count) * (ext + 2 * width) * width,
        state_grad,
        layer_1,
        on,
        off,
        turned,
        silu_slope(pre_0),
        slope_encode,
        self_weight,
        neighbor_weight,
        encode_weight,
        scratch=[pltpu.VMEM((ext, width), HALF)],
    )
    to_mesh = whole(
        mesh_counts,
        [shape(grid_count, nodes, HALF)],
        nodes * grid_count * step,
        grid_send,
        mesh_recv,
        *index[1:],
    )[0]
    rest_halves = split_gradients(
        lambda *refs: gradient_halves(0, *refs),
        3 * half_rows,
        width,
        3 * mesh_count * square,
        half,
        layer_0,
        nearby_0,
        layer_0,
        encode_in,
        encode_grad,
    )
    embed_halves = split_gradients(
        embed_back,
        narrow_rows,
        width,
        grid_count * width * (nodes + GROUPS * variables),
        encode_in_grad,
        to_mesh,
        *slopes,
        *grids,
    )
    halves = []
    for mine, other in (decode_halves, layer_halves, rest_halves, embed_halves):
        halves += [mine, swap_on(other)]
    rows = sum(block.shape[0] for block in halves[::2])
    (part,) = whole(add_halves, [shape(rows, width, HALF)], 0, *halves)
    part = reduce_all(part)
    other = swap_on(part)
    full = shape(width, width, SINGLE)
    pair = jax.ShapeDtypeStruct((2, width, width), SINGLE)
    narrow = shape(variables, width, SINGLE)
    grad_embed, grad_encode, grad_self, grad_near, grad_decode, grad_output = whole(
        unpack, [narrow, full, pair, pair, full, narrow], 0, part, other
    )
    return (
        prediction.T,
        state_grad,
        grad_embed,
        grad_encode,
        grad_self,
        grad_near,
        grad_decode,
        grad_output.T,
    )


def solution(mesh):
    placed = (
        P(("band", "dom"), None),
        P(("band", "dom"), None),
        P(("band", "dom"), None),
        P(),
        P(),
        P(),
        P(),
        P(),
        P(),
        P(("band", "dom")),
        P(("band", "dom")),
        P(("band", "dom"), None),
        P(("band", "dom")),
        P(("band", "dom")),
    )
    return jax.shard_map(
        shards,
        mesh=mesh,
        in_specs=placed,
        out_specs=(
            P(("band", "dom"), None),
            P(("band", "dom"), None),
            P(),
            P(),
            P(),
            P(),
            P(),
            P(),
        ),
        check_vma=False,
    )
```

```python
import jax
import jax.numpy as jnp
from jax import lax
from jax.experimental import pallas as pl
from jax.experimental.pallas import tpu as pltpu
from jax.sharding import PartitionSpec as P

NEAR = 6
RIM = 64
GROUPS = 5
LANES = 128
HALF = jnp.bfloat16
SINGLE = jnp.float32
MIB = 1024 * 1024
SLOT_ROWS = 6
INDEX_ROWS = 32


def silu_slope(values):
    sigma = jax.nn.sigmoid(values)
    return sigma * (1.0 + values * (1.0 - sigma))


def matmul(left, right):
    return jnp.dot(left, right, preferred_element_type=SINGLE)


def outer_sum(left, right):
    return lax.dot_general(
        left, right, (((0,), (0,)), ((), ())), preferred_element_type=SINGLE
    )


def back_mul(left, right):
    return lax.dot_general(
        left, right, (((1,), (1,)), ((), ())), preferred_element_type=SINGLE
    )


def swap_on(value):
    count = lax.axis_size("dom")
    return lax.ppermute(value, "dom", [(i, i ^ 1) for i in range(count)])


def swap_off(value):
    count = lax.axis_size("dom")
    return lax.ppermute(
        value, "dom", [(i, (i + (1 if i % 2 else -1)) % count) for i in range(count)]
    )


def swap_band(value, first):
    count = lax.axis_size("band")
    pairs = []
    for low in range(first, count - 1, 2):
        pairs += [(low, low + 1), (low + 1, low)]
    return lax.ppermute(value, "band", pairs)


def swap_all(on, off, north, south):
    south = swap_band(south, 1)
    north = swap_band(north, 0)
    off = swap_off(off)
    return swap_on(on), off, north, south


def by_partner(slots, odd_dom, odd_band, incoming):
    flip_dom = odd_dom != incoming
    flip_band = odd_band != incoming
    return [
        slots[0],
        jnp.where(flip_dom, slots[2], slots[1]),
        jnp.where(flip_dom, slots[1], slots[2]),
        jnp.where(flip_band, slots[4], slots[3]),
        jnp.where(flip_band, slots[3], slots[4]),
    ]


def whole(body, outs, macs, *args, limit=32, scratch=()):
    moved = sum(a.size * a.dtype.itemsize for a in (*args, *outs))
    return pl.pallas_call(
        body,
        out_shape=outs,
        scratch_shapes=scratch,
        compiler_params=pltpu.CompilerParams(vmem_limit_bytes=limit * MIB),
        cost_estimate=pl.CostEstimate(flops=2 * macs, bytes_accessed=moved, transcendentals=0),
    )(*args)


def shape(rows, columns, kind):
    return jax.ShapeDtypeStruct((rows, columns), kind)


def odd_along(axis):
    return lax.axis_index(axis) % 2 == 1


def hot(rows, index):
    spots = lax.broadcasted_iota(jnp.int32, (rows, LANES), 0)
    one = [
        jnp.where(spots == index[j : j + 1], 1.0, 0.0).astype(HALF) for j in range(index.shape[0])
    ]
    return jnp.concatenate(one, 1)


def pair_counts(rows, row_count, columns, column_count):
    return back_mul(hot(row_count, rows), hot(column_count, columns)).astype(HALF)


def slots_of(index):
    step = index.shape[0] // GROUPS
    return [index[k * step : (k + 1) * step] for k in range(GROUPS)]


def fetch(sources, buffers, sems):
    copies = [
        pltpu.make_async_copy(source, buffer, sems.at[i])
        for i, (source, buffer) in enumerate(zip(sources, buffers, strict=True))
    ]
    for copy in copies:
        copy.start()
    for copy in copies:
        copy.wait()


def fetching(body, outs, macs, *args, limit):
    moved = sum(a.size * a.dtype.itemsize for a in (*args, *outs))
    return pl.pallas_call(
        body,
        out_shape=outs,
        in_specs=[pl.BlockSpec(memory_space=pltpu.HBM)] * len(args),
        scratch_shapes=[pltpu.VMEM(a.shape, a.dtype) for a in args]
        + [pltpu.SemaphoreType.DMA((len(args),))],
        compiler_params=pltpu.CompilerParams(vmem_limit_bytes=limit * MIB),
        cost_estimate=pl.CostEstimate(flops=2 * macs, bytes_accessed=moved, transcendentals=0),
    )(*args)


def parcels(*refs):
    inputs, rest = refs[:4], refs[4:]
    outs, buffers, sems = rest[: GROUPS - 1], rest[GROUPS - 1 : -1], rest[-1]
    fetch(inputs, buffers, sems)
    grid_ref, grid_send_ref, mesh_send_ref, near_ref = buffers
    odd_dom, odd_band = odd_along("dom"), odd_along("band")
    grid_send = by_partner(slots_of(grid_send_ref[...]), odd_dom, odd_band, False)
    mesh_send = by_partner(slots_of(mesh_send_ref[...]), odd_dom, odd_band, False)
    near = near_ref[...]
    near = [near[:, j : j + LANES] for j in range(0, near.shape[1], LANES)]
    variables, count = grid_ref.shape
    first = outs[0].shape[0] - INDEX_ROWS // 2
    grid = grid_ref[...]
    for p, out in enumerate(outs):
        parts = [mesh_send[p + 1], grid_send[p + 1], *near]
        used = sum(part.shape[0] for part in parts)
        parts.append(jnp.zeros((INDEX_ROWS - used, LANES), jnp.int32))
        index = jnp.concatenate(parts, 0)
        high = (index >> 1).astype(SINGLE)
        low = (index & 1).astype(SINGLE)
        cut = INDEX_ROWS // 2
        out[:variables] = grid
        out[variables:first] = jnp.zeros((first - variables, count), HALF)
        out[first:] = jnp.concatenate([high[:cut], low[:cut], high[cut:], low[cut:]], 1).astype(HALF)


def index_of(packed):
    packed = packed.astype(SINGLE)
    halves = [
        packed[:, j : j + LANES] * 2.0 + packed[:, j + LANES : j + 2 * LANES]
        for j in (0, 2 * LANES)
    ]
    return jnp.concatenate(halves, 0).astype(jnp.int32)


def embed_own(*refs):
    inputs, (slope_ref, sum_ref, held_ref), buffers, sems = refs[:4], refs[4:7], refs[7:-1], refs[-1]
    fetch(inputs, buffers, sems)
    grid_ref, weight_ref, send_ref, recv_ref = buffers
    step = send_ref.shape[0] // GROUPS
    counts = pair_counts(
        recv_ref[:step], sum_ref.shape[0], send_ref[:step], grid_ref.shape[1]
    )
    pre = outer_sum(grid_ref[...], weight_ref[...])
    sigma = jax.nn.sigmoid(pre)
    slope_ref[...] = sigma * (1.0 + pre * (1.0 - sigma))
    sum_ref[...] = matmul(counts, (pre * sigma).astype(HALF))
    held_ref[...] = weight_ref[...]


def embed_far(p, parcel_ref, weight_ref, recv_ref, sum_ref, index_ref, slope_ref, out_ref):
    index = index_of(parcel_ref[parcel_ref.shape[0] - INDEX_ROWS // 2 :])
    index_ref[...] = index
    step = recv_ref.shape[0] // GROUPS
    recv = by_partner(slots_of(recv_ref[...]), odd_along("dom"), odd_along("band"), True)[p]
    counts = pair_counts(
        recv, out_ref.shape[0], index[step : 2 * step], parcel_ref.shape[1]
    )
    pre = outer_sum(parcel_ref[: weight_ref.shape[0]], weight_ref[...])
    sigma = jax.nn.sigmoid(pre)
    slope_ref[...] = sigma * (1.0 + pre * (1.0 - sigma))
    out_ref[...] = sum_ref[...] + matmul(counts, (pre * sigma).astype(HALF))


def encode(sum_ref, weight_ref, static_ref, in_ref, slope_ref, state_ref, half_ref, on_ref, off_ref):
    encode_in = sum_ref[...].astype(HALF)
    pre = matmul(encode_in, weight_ref[...])
    sigma = jax.nn.sigmoid(pre)
    state = static_ref[...].astype(SINGLE) + pre * sigma
    half = state.astype(HALF)
    in_ref[...] = encode_in
    slope_ref[...] = sigma * (1.0 + pre * (1.0 - sigma))
    state_ref[...] = state
    half_ref[...] = half
    rows = on_ref.shape[0]
    odd = odd_along("dom")
    head, tail = half[:rows], half[half.shape[0] - rows :]
    on_ref[...] = jnp.where(odd, head, tail)
    off_ref[...] = jnp.where(odd, tail, head)


def near_counts(near_ref, on_ref, off_ref, out_ref, turned_ref):
    step = near_ref.shape[0]
    mesh_count = near_ref.shape[1]
    first = 2 * SLOT_ROWS
    odd_dom = odd_along("dom")
    on, off = on_ref[...], off_ref[...]
    left = jnp.where(odd_dom, on, off)[first + step : first + 2 * step] + (RIM - mesh_count)
    right = jnp.where(odd_dom, off, on)[first : first + step] + (RIM + mesh_count)
    own = near_ref[...] + RIM
    index = jnp.concatenate([left, own, right], 1)
    spots = lax.broadcasted_iota(jnp.int32, out_ref.shape, 0)
    counts = jnp.zeros(out_ref.shape, SINGLE)
    for j in range(step):
        counts = counts + jnp.where(spots == index[j : j + 1], 1.0, 0.0)
    turned_ref[...] = counts.astype(HALF)
    out_ref[...] = counts.T.astype(HALF)


def process(
    half_ref, state_ref, on_ref, off_ref, counts_ref, self_ref, near_ref,
    final_ref, pre_0_ref, pre_1_ref, half_1_ref, nearby_0_ref, nearby_1_ref, whole_ref,
):
    rim = on_ref.shape[0]
    count = half_ref.shape[0]
    own = slice(rim, rim + count)
    odd = odd_along("dom")
    left = jnp.where(odd, on_ref[...], off_ref[...])
    right = jnp.where(odd, off_ref[...], on_ref[...])
    whole_ref[:rim] = left
    whole_ref[own] = half_ref[...]
    whole_ref[rim + count :] = right
    half_0 = whole_ref[...]
    nearby_0 = (matmul(counts_ref[...], half_0) * (1.0 / NEAR)).astype(HALF)
    nearby_0_ref[...] = nearby_0[own]
    pre_0 = matmul(half_0, self_ref[0]) + matmul(nearby_0, near_ref[0])
    pre_0_ref[...] = pre_0
    grown = pre_0 * jax.nn.sigmoid(pre_0)
    state_1 = state_ref[...] + grown[own]
    half_1 = state_1.astype(HALF)
    whole_ref[:rim] = (left.astype(SINGLE) + grown[:rim]).astype(HALF)
    whole_ref[own] = half_1
    whole_ref[rim + count :] = (right.astype(SINGLE) + grown[rim + count :]).astype(HALF)
    half_1_ref[...] = half_1
    nearby_1 = (matmul(counts_ref[own], whole_ref[...]) * (1.0 / NEAR)).astype(HALF)
    nearby_1_ref[...] = nearby_1
    pre_1 = matmul(half_1, self_ref[1]) + matmul(nearby_1, near_ref[1])
    pre_1_ref[...] = pre_1
    final_ref[...] = (state_1 + pre_1 * jax.nn.sigmoid(pre_1)).astype(HALF)


def grid_counts(send_ref, recv_ref, *refs):
    far, (out_ref, turned_ref) = refs[: GROUPS - 1], refs[GROUPS - 1 :]
    odd_dom, odd_band = odd_along("dom"), odd_along("band")
    step = send_ref.shape[0] // GROUPS
    recv = by_partner(slots_of(recv_ref[...]), odd_dom, odd_band, True)
    send = [send_ref[:step]] + [ref[:step] for ref in far]
    grids, nodes = out_ref.shape[0], turned_ref.shape[0] // GROUPS
    for p in range(GROUPS):
        at = slice(p * nodes, (p + 1) * nodes)
        to, of = hot(grids, recv[p]), hot(nodes, send[p])
        out_ref[:, at] = back_mul(to, of).astype(HALF)
        turned_ref[at] = back_mul(of, to).astype(HALF)


def mesh_counts(send_ref, recv_ref, *refs):
    far, out_ref = refs[: GROUPS - 1], refs[GROUPS - 1]
    step = send_ref.shape[0] // GROUPS
    send = [send_ref[:step]] + [ref[step : 2 * step] for ref in far]
    recv = by_partner(slots_of(recv_ref[...]), odd_along("dom"), odd_along("band"), True)
    grids, nodes = out_ref.shape[0], out_ref.shape[1] // GROUPS
    for p in range(GROUPS):
        out_ref[:, p * nodes : (p + 1) * nodes] = pair_counts(send[p], grids, recv[p], nodes)


def decode(*refs):
    finals = refs[:GROUPS]
    counts_ref, turned_ref, weight_ref, back_ref = refs[GROUPS : GROUPS + 4]
    in_ref, hidden_ref, grad_ref, own_ref, *outs = refs[GROUPS + 4 :]
    nodes = own_ref.shape[0]
    total = matmul(counts_ref[:, :nodes], finals[0][...])
    for p in range(1, GROUPS):
        total = total + matmul(counts_ref[:, p * nodes : (p + 1) * nodes], finals[p][...])
    decode_in = total.astype(HALF)
    in_ref[...] = decode_in
    pre = matmul(decode_in, weight_ref[...])
    sigma = jax.nn.sigmoid(pre)
    hidden_ref[...] = (pre * sigma).astype(HALF)
    grad = (back_ref[...] * (sigma * (1.0 + pre * (1.0 - sigma)))).astype(HALF)
    grad_ref[...] = grad
    in_grad = back_mul(grad, weight_ref[...]).astype(HALF)
    own_ref[...] = matmul(turned_ref[:nodes], in_grad)
    for p, out in enumerate(outs):
        out[...] = matmul(turned_ref[(p + 1) * nodes : (p + 2) * nodes], in_grad).astype(HALF)


def gather_back(*refs):
    total = refs[0][...]
    for ref in refs[1:GROUPS]:
        total = total + ref[...].astype(SINGLE)
    slope_ref, state_ref, layer_ref, on_ref, off_ref = refs[GROUPS:]
    state_ref[...] = total
    layer = (total * slope_ref[...]).astype(HALF)
    layer_ref[...] = layer
    half = total.astype(HALF)
    odd = odd_along("dom")
    rim, count = RIM, total.shape[0]
    heads = jnp.concatenate([layer[: 2 * rim], half[:rim]], 0)
    tails = jnp.concatenate([layer[count - 2 * rim :], half[count - rim :]], 0)
    on_ref[...] = jnp.where(odd, heads, tails)
    off_ref[...] = jnp.where(odd, tails, heads)


def process_back(
    state_ref, layer_ref, on_ref, off_ref, turned_ref, slope_0_ref, slope_in_ref,
    self_ref, near_ref, encode_ref, static_ref, layer_0_ref, encode_grad_ref, back_ref, whole_ref,
):
    rim = RIM
    count = state_ref.shape[0]
    own = slice(2 * rim, 2 * rim + count)
    odd = odd_along("dom")
    on, off = on_ref[...], off_ref[...]
    left, right = jnp.where(odd, on, off), jnp.where(odd, off, on)
    whole_ref[: 2 * rim] = left[: 2 * rim]
    whole_ref[own] = layer_ref[...]
    whole_ref[2 * rim + count :] = right[: 2 * rim]
    layer_1 = whole_ref[...]
    spread = (matmul(turned_ref[...], layer_1) * (1.0 / NEAR)).astype(HALF)
    back = back_mul(layer_1, self_ref[1]) + back_mul(spread, near_ref[1])
    state_own = state_ref[...] + back[own]
    first = left[2 * rim :].astype(SINGLE) + back[rim : 2 * rim]
    last = right[2 * rim :].astype(SINGLE) + back[2 * rim + count : 3 * rim + count]
    layer_0 = (state_own * slope_0_ref[own]).astype(HALF)
    layer_0_ref[...] = layer_0
    whole_ref[:rim] = jnp.zeros((rim, back.shape[1]), HALF)
    whole_ref[rim : 2 * rim] = (first * slope_0_ref[rim : 2 * rim]).astype(HALF)
    whole_ref[own] = layer_0
    whole_ref[2 * rim + count : 3 * rim + count] = (
        last * slope_0_ref[2 * rim + count : 3 * rim + count]
    ).astype(HALF)
    whole_ref[3 * rim + count :] = jnp.zeros((rim, back.shape[1]), HALF)
    spread = (matmul(turned_ref[own], whole_ref[...]) * (1.0 / NEAR)).astype(HALF)
    state = state_own + back_mul(layer_0, self_ref[0]) + back_mul(spread, near_ref[0])
    static_ref[...] = state
    grad = (state * slope_in_ref[...]).astype(HALF)
    encode_grad_ref[...] = grad
    back_ref[...] = back_mul(grad, encode_ref[...]).astype(HALF)


def split_rows(count):
    return -(-count // (2 * LANES)) * LANES


def store_halves(value, at, mine_ref, other_ref, wide_ref):
    odd = lax.axis_index("dom") % 2
    count, rows = value.shape[0], split_rows(value.shape[0])
    wide_ref[:count] = value
    if count < 2 * rows:
        wide_ref[count : 2 * rows] = jnp.zeros((2 * rows - count, value.shape[1]), SINGLE)
    mine = pl.ds(pl.multiple_of(odd * rows, rows), rows)
    other = pl.ds(pl.multiple_of((1 - odd) * rows, rows), rows)
    mine_ref[at : at + rows] = wide_ref[mine].astype(HALF)
    other_ref[at : at + rows] = wide_ref[other].astype(HALF)
    return at + rows


def gradient_halves(turned, *refs):
    mine_ref, other_ref, wide_ref = refs[-3:]
    at = 0
    for i, (left, right) in enumerate(zip(refs[:-3:2], refs[1:-3:2], strict=True)):
        product = matmul if i < turned else outer_sum
        value = product(left[...], right[...])
        at = store_halves(value, at, mine_ref, other_ref, wide_ref)


def embed_back(*refs):
    back_ref, counts_ref = refs[:2]
    slopes, grids = refs[2 : 2 + GROUPS], refs[2 + GROUPS : 2 + 2 * GROUPS]
    mine_ref, other_ref, wide_ref = refs[2 + 2 * GROUPS :]
    nodes = back_ref.shape[0]
    variables = grids[0].shape[0]
    total = None
    for p in range(GROUPS):
        latent = matmul(counts_ref[:, p * nodes : (p + 1) * nodes], back_ref[...])
        grad = (latent * slopes[p][...]).astype(HALF)
        term = matmul(grids[p][:variables], grad)
        total = term if total is None else total + term
    store_halves(total, 0, mine_ref, other_ref, wide_ref)


def split_gradients(body, rows, width, macs, *args):
    outs = [shape(rows, width, HALF)] * 2
    return whole(body, outs, macs, *args, scratch=[pltpu.VMEM((width, width), SINGLE)])


def add_halves(*refs):
    out_ref = refs[-1]
    at = 0
    for mine, other in zip(refs[:-1:2], refs[1:-1:2], strict=True):
        rows = mine.shape[0]
        out_ref[at : at + rows] = (
            mine[...].astype(SINGLE) + other[...].astype(SINGLE)
        ).astype(HALF)
        at += rows


def add_pieces(pieces_ref, out_ref):
    total = pieces_ref[0].astype(SINGLE)
    for i in range(1, pieces_ref.shape[0]):
        total = total + pieces_ref[i].astype(SINGLE)
    out_ref[...] = total.astype(HALF)


def add_bands(*refs):
    out_ref = refs[-1]
    total = refs[0][...].astype(SINGLE)
    for ref in refs[1:-1]:
        total = total + ref[...].astype(SINGLE)
    total = total.astype(HALF)
    for i in range(out_ref.shape[0]):
        out_ref[i] = total


def places(outs):
    encode, self_, near, decode = outs
    return [(decode, None), (self_, 1), (near, 1), (self_, 0), (near, 0), (encode, None)]


def store_squares(first, half, value_ref, outs, buffer_ref, sems):
    rows = outs[0].shape[0] // 2
    spot = pl.ds(pl.multiple_of(half * rows, rows), rows)
    copies = []
    for i, (out, which) in enumerate(places(outs)):
        at = i * rows
        buffer_ref[at : at + rows] = value_ref[first + at : first + at + rows].astype(SINGLE)
        target = out.at[spot] if which is None else out.at[which, spot]
        copies.append(
            pltpu.make_async_copy(buffer_ref.at[at : at + rows], target, sems.at[i])
        )
        copies[-1].start()
    return copies


def unpack_own(part_ref, *refs):
    outs, (buffer_ref, sems) = refs[:4], refs[4:]
    first = (part_ref.shape[0] - buffer_ref.shape[0]) // 2
    half = lax.axis_index("dom") % 2
    for copy in store_squares(first, half, part_ref, outs, buffer_ref, sems):
        copy.wait()


def unpack_other(part_ref, other_ref, *refs):
    outs, (embed, output), (buffer_ref, sems) = refs[4:8], refs[8:10], refs[10:]
    rows = (part_ref.shape[0] - buffer_ref.shape[0]) // 2
    half = lax.axis_index("dom") % 2
    copies = store_squares(rows, 1 - half, other_ref, outs, buffer_ref, sems)
    odd = odd_along("dom")
    for out, at in ((output, 0), (embed, part_ref.shape[0] - rows)):
        own = part_ref[at : at + rows].astype(SINGLE)
        far = other_ref[at : at + rows].astype(SINGLE)
        out[:rows] = jnp.where(odd, far, own)
        out[rows:] = jnp.where(odd, own, far)[: out.shape[0] - rows]
    for copy in copies:
        copy.wait()


def unpack(part, other, width, variables):
    full = shape(width, width, SINGLE)
    pair = jax.ShapeDtypeStruct((2, width, width), SINGLE)
    narrow = shape(variables, width, SINGLE)
    squares = [full, pair, pair, full]
    hbm = pl.BlockSpec(memory_space=pltpu.HBM)
    vmem = pl.BlockSpec(memory_space=pltpu.VMEM)
    scratch = [
        pltpu.VMEM((6 * split_rows(width), width), SINGLE),
        pltpu.SemaphoreType.DMA((6,)),
    ]
    params = pltpu.CompilerParams(vmem_limit_bytes=32 * MIB)
    size = part.size * 6
    cost = pl.CostEstimate(flops=0, bytes_accessed=size, transcendentals=0)
    grads = pl.pallas_call(
        unpack_own,
        out_shape=squares,
        in_specs=[vmem],
        out_specs=[hbm] * 4,
        scratch_shapes=scratch,
        compiler_params=params,
        cost_estimate=cost,
    )(part)
    return pl.pallas_call(
        unpack_other,
        out_shape=[*squares, narrow, narrow],
        in_specs=[vmem, vmem] + [hbm] * 4,
        out_specs=[hbm] * 4 + [vmem] * 2,
        input_output_aliases={2: 0, 3: 1, 4: 2, 5: 3},
        scratch_shapes=scratch,
        compiler_params=params,
        cost_estimate=cost,
    )(part, other, *grads)


def reduce_all(part):
    count = lax.axis_size("dom")
    bands = lax.axis_size("band")
    groups = [list(range(c, count, 2)) for c in range(2)]
    chips = count // 2
    rows, width = part.shape[0] // chips, part.shape[1]
    pieces = lax.all_to_all(
        part.reshape(chips, rows, width), "dom", 0, 0, axis_index_groups=groups
    )
    (piece,) = whole(add_pieces, [shape(rows, width, HALF)], 0, pieces)
    others = [
        lax.ppermute(piece, "band", [(i, (i + step) % bands) for i in range(bands)])
        for step in range(1, bands)
    ]
    copies = jax.ShapeDtypeStruct((chips, rows, width), HALF)
    (copies,) = whole(add_bands, [copies], 0, piece, *others)
    return lax.all_to_all(copies, "dom", 0, 0, axis_index_groups=groups).reshape(part.shape)


def shards(
    grid_vars,
    cotangent,
    mesh_static,
    embed_weight,
    encode_weight,
    self_weight,
    neighbor_weight,
    decode_weight,
    output_weight,
    grid_sender,
    mesh_receiver,
    neighbors,
    mesh_sender,
    grid_receiver,
):
    grid_count, variables = grid_vars.shape
    mesh_count, width = mesh_static.shape
    rim = 2 * RIM
    ext = mesh_count + 2 * rim
    grid, cot, near, out_weight = grid_vars.T, cotangent.T, neighbors.T, output_weight.T
    grid_send, mesh_recv, mesh_send, grid_recv = (
        index.reshape(-1, LANES) for index in (grid_sender, mesh_receiver, mesh_sender, grid_receiver)
    )
    step = grid_send.shape[0] // GROUPS * LANES
    nodes = GROUPS * mesh_count
    mesh_rows = shape(mesh_count, width, HALF)
    mesh_full = shape(mesh_count, width, SINGLE)
    grid_rows = shape(grid_count, width, HALF)
    grid_full = shape(grid_count, width, SINGLE)
    parcel = shape(variables + -variables % 16 + INDEX_ROWS // 2, grid_count, HALF)
    sent = fetching(
        parcels, [parcel] * (GROUPS - 1), 0, grid, grid_send, mesh_send, near, limit=58
    )
    arrived = swap_all(*sent)
    embed_macs = grid_count * variables * width + mesh_count * grid_count * (step + width)
    slope_embed, total, held_weight = fetching(
        embed_own,
        [grid_full, mesh_full, shape(variables, width, HALF)],
        embed_macs,
        grid,
        embed_weight,
        grid_send,
        mesh_recv,
        limit=32,
    )
    index = [None] * GROUPS
    slopes = [slope_embed] + [None] * (GROUPS - 1)
    grids = [grid, *arrived]
    for p in range(1, GROUPS):
        index[p], slopes[p], total = whole(
            lambda *refs, p=p: embed_far(p, *refs),
            [shape(INDEX_ROWS, LANES, jnp.int32), grid_full, mesh_full],
            embed_macs,
            arrived[p - 1],
            held_weight,
            mesh_recv,
            total,
        )
    encode_in, slope_encode, state, half, on, off = whole(
        encode,
        [mesh_rows, mesh_full, mesh_full, mesh_rows] + [shape(rim, width, HALF)] * 2,
        mesh_count * width * width,
        total,
        encode_weight,
        mesh_static,
    )
    off = swap_off(off)
    on = swap_on(on)
    counts, turned = whole(
        near_counts, [shape(ext, ext, HALF)] * 2, ext * ext * 64, near, index[1], index[2]
    )
    final_half, pre_0, pre_1, half_1, nearby_0, nearby_1 = whole(
        process,
        [mesh_rows, shape(ext, width, SINGLE), mesh_full, mesh_rows, mesh_rows, mesh_rows],
        (ext + mesh_count) * (ext + 2 * width) * width,
        half,
        state,
        on,
        off,
        counts,
        self_weight,
        neighbor_weight,
        scratch=[pltpu.VMEM((ext, width), HALF)],
    )
    finals = (final_half,) + swap_all(*[final_half] * 4)
    to_grid, from_grid = whole(
        grid_counts,
        [shape(grid_count, nodes, HALF), shape(nodes, grid_count, HALF)],
        2 * nodes * grid_count * step,
        mesh_send,
        grid_recv,
        *index[1:],
    )
    hidden_grad = outer_sum(cot, out_weight)
    decode_in, hidden, decode_grad, state_grad, *sums = whole(
        decode,
        [grid_rows] * 3 + [mesh_full] + [mesh_rows] * (GROUPS - 1),
        2 * grid_count * width * (nodes + width),
        *finals,
        to_grid,
        from_grid,
        decode_weight,
        hidden_grad,
    )
    arrived = swap_all(*sums)
    prediction = (grid.astype(SINGLE) + back_mul(out_weight, hidden)).astype(HALF)
    half_rows = split_rows(width)
    narrow_rows = split_rows(variables)
    square = width * width
    decode_halves = split_gradients(
        lambda *refs: gradient_halves(1, *refs),
        narrow_rows + half_rows,
        width,
        2 * grid_count * square,
        cot,
        hidden,
        decode_in,
        decode_grad,
    )
    to_mesh = whole(
        mesh_counts,
        [shape(grid_count, nodes, HALF)],
        nodes * grid_count * step,
        grid_send,
        mesh_recv,
        *index[1:],
    )[0]
    state_grad, to_mesh, *decode_halves = lax.optimization_barrier(
        (state_grad, to_mesh, *decode_halves)
    )
    state_grad, layer_1, on, off = whole(
        gather_back,
        [mesh_full, mesh_rows] + [shape(rim + RIM, width, HALF)] * 2,
        0,
        state_grad,
        *arrived,
        silu_slope(pre_1),
    )
    off = swap_off(off)
    on = swap_on(on)
    layer_halves = split_gradients(
        lambda *refs: gradient_halves(0, *refs),
        2 * half_rows,
        width,
        2 * mesh_count * square,
        half_1,
        layer_1,
        nearby_1,
        layer_1,
    )
    halves = [decode_halves[0], swap_on(decode_halves[1])]
    state_grad, *layer_halves, halves[1] = lax.optimization_barrier(
        (state_grad, *layer_halves, halves[1])
    )
    state_grad, layer_0, encode_grad, encode_in_grad = whole(
        process_back,
        [mesh_full, mesh_rows, mesh_rows, mesh_rows],
        (ext + mesh_count) * (ext + 2 * width) * width,
        state_grad,
        layer_1,
        on,
        off,
        turned,
        silu_slope(pre_0),
        slope_encode,
        self_weight,
        neighbor_weight,
        encode_weight,
        scratch=[pltpu.VMEM((ext, width), HALF)],
    )
    rest_halves = split_gradients(
        lambda *refs: gradient_halves(0, *refs),
        3 * half_rows,
        width,
        3 * mesh_count * square,
        half,
        layer_0,
        nearby_0,
        layer_0,
        encode_in,
        encode_grad,
    )
    embed_halves = split_gradients(
        embed_back,
        narrow_rows,
        width,
        grid_count * width * (nodes + GROUPS * variables),
        encode_in_grad,
        to_mesh,
        *slopes,
        *grids,
    )
    for mine, other in (layer_halves, rest_halves, embed_halves):
        halves += [mine, swap_on(other)]
    rows = sum(block.shape[0] for block in halves[::2])
    (part,) = whole(add_halves, [shape(rows, width, HALF)], 0, *halves)
    part = reduce_all(part)
    other = swap_on(part)
    grad_encode, grad_self, grad_near, grad_decode, grad_embed, grad_output = unpack(
        part, other, width, variables
    )
    return (
        prediction.T,
        state_grad,
        grad_embed,
        grad_encode,
        grad_self,
        grad_near,
        grad_decode,
        grad_output.T,
    )


def solution(mesh):
    placed = (
        P(("band", "dom"), None),
        P(("band", "dom"), None),
        P(("band", "dom"), None),
        P(),
        P(),
        P(),
        P(),
        P(),
        P(),
        P(("band", "dom")),
        P(("band", "dom")),
        P(("band", "dom"), None),
        P(("band", "dom")),
        P(("band", "dom")),
    )
    return jax.shard_map(
        shards,
        mesh=mesh,
        in_specs=placed,
        out_specs=(
            P(("band", "dom"), None),
            P(("band", "dom"), None),
            P(),
            P(),
            P(),
            P(),
            P(),
            P(),
        ),
        check_vma=False,
    )
```

```python
import jax
import jax.numpy as jnp
from jax import lax
from jax.experimental import pallas as pl
from jax.experimental.pallas import tpu as pltpu
from jax.sharding import PartitionSpec as P

NEAR = 6
RIM = 64
GROUPS = 5
LANES = 128
HALF = jnp.bfloat16
SINGLE = jnp.float32
MIB = 1024 * 1024
SLOT_ROWS = 6
INDEX_ROWS = 32


def silu_slope(values):
    sigma = jax.nn.sigmoid(values)
    return sigma * (1.0 + values * (1.0 - sigma))


def matmul(left, right):
    return jnp.dot(left, right, preferred_element_type=SINGLE)


def outer_sum(left, right):
    return lax.dot_general(
        left, right, (((0,), (0,)), ((), ())), preferred_element_type=SINGLE
    )


def back_mul(left, right):
    return lax.dot_general(
        left, right, (((1,), (1,)), ((), ())), preferred_element_type=SINGLE
    )


def swap_on(value):
    count = lax.axis_size("dom")
    return lax.ppermute(value, "dom", [(i, i ^ 1) for i in range(count)])


def swap_off(value):
    count = lax.axis_size("dom")
    return lax.ppermute(
        value, "dom", [(i, (i + (1 if i % 2 else -1)) % count) for i in range(count)]
    )


def swap_band(value, first):
    count = lax.axis_size("band")
    pairs = []
    for low in range(first, count - 1, 2):
        pairs += [(low, low + 1), (low + 1, low)]
    return lax.ppermute(value, "band", pairs)


def swap_all(on, off, north, south):
    south = swap_band(south, 1)
    north = swap_band(north, 0)
    off = swap_off(off)
    return swap_on(on), off, north, south


def by_partner(slots, odd_dom, odd_band, incoming):
    flip_dom = odd_dom != incoming
    flip_band = odd_band != incoming
    return [
        slots[0],
        jnp.where(flip_dom, slots[2], slots[1]),
        jnp.where(flip_dom, slots[1], slots[2]),
        jnp.where(flip_band, slots[4], slots[3]),
        jnp.where(flip_band, slots[3], slots[4]),
    ]


def whole(body, outs, macs, *args, limit=32, scratch=()):
    moved = sum(a.size * a.dtype.itemsize for a in (*args, *outs))
    return pl.pallas_call(
        body,
        out_shape=outs,
        scratch_shapes=scratch,
        compiler_params=pltpu.CompilerParams(vmem_limit_bytes=limit * MIB),
        cost_estimate=pl.CostEstimate(flops=2 * macs, bytes_accessed=moved, transcendentals=0),
    )(*args)


def shape(rows, columns, kind):
    return jax.ShapeDtypeStruct((rows, columns), kind)


def odd_along(axis):
    return lax.axis_index(axis) % 2 == 1


def hot(rows, index):
    spots = lax.broadcasted_iota(jnp.int32, (rows, LANES), 0)
    one = [
        jnp.where(spots == index[j : j + 1], 1.0, 0.0).astype(HALF) for j in range(index.shape[0])
    ]
    return jnp.concatenate(one, 1)


def pair_counts(rows, row_count, columns, column_count):
    return back_mul(hot(row_count, rows), hot(column_count, columns)).astype(HALF)


def slots_of(index):
    step = index.shape[0] // GROUPS
    return [index[k * step : (k + 1) * step] for k in range(GROUPS)]


def fetch(sources, buffers, sems):
    copies = [
        pltpu.make_async_copy(source, buffer, sems.at[i])
        for i, (source, buffer) in enumerate(zip(sources, buffers, strict=True))
    ]
    for copy in copies:
        copy.start()
    for copy in copies:
        copy.wait()


def fetching(body, outs, macs, *args, limit):
    moved = sum(a.size * a.dtype.itemsize for a in (*args, *outs))
    return pl.pallas_call(
        body,
        out_shape=outs,
        in_specs=[pl.BlockSpec(memory_space=pltpu.HBM)] * len(args),
        scratch_shapes=[pltpu.VMEM(a.shape, a.dtype) for a in args]
        + [pltpu.SemaphoreType.DMA((len(args),))],
        compiler_params=pltpu.CompilerParams(vmem_limit_bytes=limit * MIB),
        cost_estimate=pl.CostEstimate(flops=2 * macs, bytes_accessed=moved, transcendentals=0),
    )(*args)


def parcels(*refs):
    inputs, rest = refs[:4], refs[4:]
    outs, buffers, sems = rest[: GROUPS - 1], rest[GROUPS - 1 : -1], rest[-1]
    fetch(inputs, buffers, sems)
    grid_ref, grid_send_ref, mesh_send_ref, near_ref = buffers
    odd_dom, odd_band = odd_along("dom"), odd_along("band")
    grid_send = by_partner(slots_of(grid_send_ref[...]), odd_dom, odd_band, False)
    mesh_send = by_partner(slots_of(mesh_send_ref[...]), odd_dom, odd_band, False)
    near = near_ref[...]
    near = [near[:, j : j + LANES] for j in range(0, near.shape[1], LANES)]
    variables, count = grid_ref.shape
    first = outs[0].shape[0] - INDEX_ROWS // 2
    grid = grid_ref[...]
    for p, out in enumerate(outs):
        parts = [mesh_send[p + 1], grid_send[p + 1], *near]
        used = sum(part.shape[0] for part in parts)
        parts.append(jnp.zeros((INDEX_ROWS - used, LANES), jnp.int32))
        index = jnp.concatenate(parts, 0)
        high = (index >> 1).astype(SINGLE)
        low = (index & 1).astype(SINGLE)
        cut = INDEX_ROWS // 2
        out[:variables] = grid
        out[variables:first] = jnp.zeros((first - variables, count), HALF)
        out[first:] = jnp.concatenate([high[:cut], low[:cut], high[cut:], low[cut:]], 1).astype(HALF)


def index_of(packed):
    packed = packed.astype(SINGLE)
    halves = [
        packed[:, j : j + LANES] * 2.0 + packed[:, j + LANES : j + 2 * LANES]
        for j in (0, 2 * LANES)
    ]
    return jnp.concatenate(halves, 0).astype(jnp.int32)


def embed_own(*refs):
    inputs, (slope_ref, sum_ref, held_ref), buffers, sems = refs[:4], refs[4:7], refs[7:-1], refs[-1]
    fetch(inputs, buffers, sems)
    grid_ref, weight_ref, send_ref, recv_ref = buffers
    step = send_ref.shape[0] // GROUPS
    counts = pair_counts(
        recv_ref[:step], sum_ref.shape[0], send_ref[:step], grid_ref.shape[1]
    )
    pre = outer_sum(grid_ref[...], weight_ref[...])
    sigma = jax.nn.sigmoid(pre)
    slope_ref[...] = sigma * (1.0 + pre * (1.0 - sigma))
    sum_ref[...] = matmul(counts, (pre * sigma).astype(HALF))
    held_ref[...] = weight_ref[...]


def embed_far(p, parcel_ref, weight_ref, recv_ref, sum_ref, index_ref, slope_ref, out_ref):
    index = index_of(parcel_ref[parcel_ref.shape[0] - INDEX_ROWS // 2 :])
    index_ref[...] = index
    step = recv_ref.shape[0] // GROUPS
    recv = by_partner(slots_of(recv_ref[...]), odd_along("dom"), odd_along("band"), True)[p]
    counts = pair_counts(
        recv, out_ref.shape[0], index[step : 2 * step], parcel_ref.shape[1]
    )
    pre = outer_sum(parcel_ref[: weight_ref.shape[0]], weight_ref[...])
    sigma = jax.nn.sigmoid(pre)
    slope_ref[...] = sigma * (1.0 + pre * (1.0 - sigma))
    out_ref[...] = sum_ref[...] + matmul(counts, (pre * sigma).astype(HALF))


def encode(sum_ref, weight_ref, static_ref, in_ref, slope_ref, state_ref, half_ref, on_ref, off_ref):
    encode_in = sum_ref[...].astype(HALF)
    pre = matmul(encode_in, weight_ref[...])
    sigma = jax.nn.sigmoid(pre)
    state = static_ref[...].astype(SINGLE) + pre * sigma
    half = state.astype(HALF)
    in_ref[...] = encode_in
    slope_ref[...] = sigma * (1.0 + pre * (1.0 - sigma))
    state_ref[...] = state
    half_ref[...] = half
    rows = on_ref.shape[0]
    odd = odd_along("dom")
    head, tail = half[:rows], half[half.shape[0] - rows :]
    on_ref[...] = jnp.where(odd, head, tail)
    off_ref[...] = jnp.where(odd, tail, head)


def near_counts(near_ref, on_ref, off_ref, out_ref, turned_ref):
    step = near_ref.shape[0]
    mesh_count = near_ref.shape[1]
    first = 2 * SLOT_ROWS
    odd_dom = odd_along("dom")
    on, off = on_ref[...], off_ref[...]
    left = jnp.where(odd_dom, on, off)[first + step : first + 2 * step] + (RIM - mesh_count)
    right = jnp.where(odd_dom, off, on)[first : first + step] + (RIM + mesh_count)
    own = near_ref[...] + RIM
    index = jnp.concatenate([left, own, right], 1)
    spots = lax.broadcasted_iota(jnp.int32, out_ref.shape, 0)
    counts = jnp.zeros(out_ref.shape, SINGLE)
    for j in range(step):
        counts = counts + jnp.where(spots == index[j : j + 1], 1.0, 0.0)
    turned_ref[...] = counts.astype(HALF)
    out_ref[...] = counts.T.astype(HALF)


def process(
    half_ref, state_ref, on_ref, off_ref, counts_ref, self_ref, near_ref,
    final_ref, pre_0_ref, pre_1_ref, half_1_ref, nearby_0_ref, nearby_1_ref, whole_ref,
):
    rim = on_ref.shape[0]
    count = half_ref.shape[0]
    own = slice(rim, rim + count)
    odd = odd_along("dom")
    left = jnp.where(odd, on_ref[...], off_ref[...])
    right = jnp.where(odd, off_ref[...], on_ref[...])
    whole_ref[:rim] = left
    whole_ref[own] = half_ref[...]
    whole_ref[rim + count :] = right
    half_0 = whole_ref[...]
    used = slice(RIM, 3 * RIM + count)
    nearby_0 = (matmul(counts_ref[used], half_0) * (1.0 / NEAR)).astype(HALF)
    nearby_0_ref[...] = nearby_0[RIM : RIM + count]
    pre_0 = matmul(half_0[used], self_ref[0]) + matmul(nearby_0, near_ref[0])
    pre_0_ref[...] = pre_0
    grown = pre_0 * jax.nn.sigmoid(pre_0)
    state_1 = state_ref[...] + grown[RIM : RIM + count]
    half_1 = state_1.astype(HALF)
    whole_ref[RIM:rim] = (left[RIM:].astype(SINGLE) + grown[:RIM]).astype(HALF)
    whole_ref[own] = half_1
    whole_ref[rim + count : rim + count + RIM] = (
        right[:RIM].astype(SINGLE) + grown[RIM + count :]
    ).astype(HALF)
    half_1_ref[...] = half_1
    nearby_1 = (matmul(counts_ref[own], whole_ref[...]) * (1.0 / NEAR)).astype(HALF)
    nearby_1_ref[...] = nearby_1
    pre_1 = matmul(half_1, self_ref[1]) + matmul(nearby_1, near_ref[1])
    pre_1_ref[...] = pre_1
    final_ref[...] = (state_1 + pre_1 * jax.nn.sigmoid(pre_1)).astype(HALF)


def grid_counts(turned, send_ref, recv_ref, *refs):
    far, out_ref = refs[: GROUPS - 1], refs[GROUPS - 1]
    odd_dom, odd_band = odd_along("dom"), odd_along("band")
    step = send_ref.shape[0] // GROUPS
    recv = by_partner(slots_of(recv_ref[...]), odd_dom, odd_band, True)
    send = [send_ref[:step]] + [ref[:step] for ref in far]
    nodes = out_ref.shape[0 if turned else 1] // GROUPS
    grids = out_ref.shape[1 if turned else 0]
    for p in range(GROUPS):
        at = slice(p * nodes, (p + 1) * nodes)
        if turned:
            out_ref[at] = pair_counts(send[p], nodes, recv[p], grids)
        else:
            out_ref[:, at] = pair_counts(recv[p], grids, send[p], nodes)


def mesh_counts(send_ref, recv_ref, *refs):
    far, out_ref = refs[: GROUPS - 1], refs[GROUPS - 1]
    step = send_ref.shape[0] // GROUPS
    send = [send_ref[:step]] + [ref[step : 2 * step] for ref in far]
    recv = by_partner(slots_of(recv_ref[...]), odd_along("dom"), odd_along("band"), True)
    grids, nodes = out_ref.shape[0], out_ref.shape[1] // GROUPS
    for p in range(GROUPS):
        out_ref[:, p * nodes : (p + 1) * nodes] = pair_counts(send[p], grids, recv[p], nodes)


def decode(*refs):
    finals = [refs[i] for i in (0, 4, 3, 2, 1)]
    counts_ref, turned_ref, weight_ref, back_ref = refs[GROUPS : GROUPS + 4]
    in_ref, hidden_ref, grad_ref, own_ref, *outs = refs[GROUPS + 4 :]
    nodes = own_ref.shape[0]
    total = matmul(counts_ref[:, :nodes], finals[0][...])
    for p in range(1, GROUPS):
        total = total + matmul(counts_ref[:, p * nodes : (p + 1) * nodes], finals[p][...])
    decode_in = total.astype(HALF)
    in_ref[...] = decode_in
    pre = matmul(decode_in, weight_ref[...])
    sigma = jax.nn.sigmoid(pre)
    hidden_ref[...] = (pre * sigma).astype(HALF)
    grad = (back_ref[...] * (sigma * (1.0 + pre * (1.0 - sigma)))).astype(HALF)
    grad_ref[...] = grad
    in_grad = back_mul(grad, weight_ref[...]).astype(HALF)
    own_ref[...] = matmul(turned_ref[:nodes], in_grad)
    for p, out in enumerate(outs):
        out[...] = matmul(turned_ref[(p + 1) * nodes : (p + 2) * nodes], in_grad).astype(HALF)


def gather_back(*refs):
    total = refs[0][...]
    for ref in refs[1:GROUPS]:
        total = total + ref[...].astype(SINGLE)
    slope_ref, state_ref, layer_ref, on_ref, off_ref = refs[GROUPS:]
    state_ref[...] = total
    layer = (total * slope_ref[...]).astype(HALF)
    layer_ref[...] = layer
    half = total.astype(HALF)
    odd = odd_along("dom")
    rim, count = RIM, total.shape[0]
    heads = jnp.concatenate([layer[: 2 * rim], half[:rim]], 0)
    tails = jnp.concatenate([layer[count - 2 * rim :], half[count - rim :]], 0)
    on_ref[...] = jnp.where(odd, heads, tails)
    off_ref[...] = jnp.where(odd, tails, heads)


def process_back(
    state_ref, layer_ref, on_ref, off_ref, turned_ref, slope_0_ref, slope_in_ref,
    self_ref, near_ref, encode_ref, static_ref, layer_0_ref, encode_grad_ref, back_ref, whole_ref,
):
    rim = RIM
    count = state_ref.shape[0]
    own = slice(2 * rim, 2 * rim + count)
    odd = odd_along("dom")
    on, off = on_ref[...], off_ref[...]
    left, right = jnp.where(odd, on, off), jnp.where(odd, off, on)
    whole_ref[: 2 * rim] = left[: 2 * rim]
    whole_ref[own] = layer_ref[...]
    whole_ref[2 * rim + count :] = right[: 2 * rim]
    layer_1 = whole_ref[...]
    used = slice(rim, 3 * rim + count)
    inner = slice(rim, rim + count)
    spread = (matmul(turned_ref[used], layer_1) * (1.0 / NEAR)).astype(HALF)
    back = back_mul(layer_1[used], self_ref[1]) + back_mul(spread, near_ref[1])
    state_own = state_ref[...] + back[inner]
    first = left[2 * rim :].astype(SINGLE) + back[:rim]
    last = right[2 * rim :].astype(SINGLE) + back[rim + count :]
    layer_0 = (state_own * slope_0_ref[inner]).astype(HALF)
    layer_0_ref[...] = layer_0
    whole_ref[:rim] = jnp.zeros((rim, back.shape[1]), HALF)
    whole_ref[rim : 2 * rim] = (first * slope_0_ref[:rim]).astype(HALF)
    whole_ref[own] = layer_0
    whole_ref[2 * rim + count : 3 * rim + count] = (last * slope_0_ref[rim + count :]).astype(HALF)
    whole_ref[3 * rim + count :] = jnp.zeros((rim, back.shape[1]), HALF)
    spread = (matmul(turned_ref[own], whole_ref[...]) * (1.0 / NEAR)).astype(HALF)
    state = state_own + back_mul(layer_0, self_ref[0]) + back_mul(spread, near_ref[0])
    static_ref[...] = state
    grad = (state * slope_in_ref[...]).astype(HALF)
    encode_grad_ref[...] = grad
    back_ref[...] = back_mul(grad, encode_ref[...]).astype(HALF)


def split_rows(count):
    return -(-count // (2 * LANES)) * LANES


def store_halves(value, at, mine_ref, other_ref, wide_ref):
    odd = lax.axis_index("dom") % 2
    count, rows = value.shape[0], split_rows(value.shape[0])
    wide_ref[:count] = value
    if count < 2 * rows:
        wide_ref[count : 2 * rows] = jnp.zeros((2 * rows - count, value.shape[1]), SINGLE)
    mine = pl.ds(pl.multiple_of(odd * rows, rows), rows)
    other = pl.ds(pl.multiple_of((1 - odd) * rows, rows), rows)
    mine_ref[at : at + rows] = wide_ref[mine].astype(HALF)
    other_ref[at : at + rows] = wide_ref[other].astype(HALF)
    return at + rows


def gradient_halves(turned, *refs):
    mine_ref, other_ref, wide_ref = refs[-3:]
    at = 0
    for i, (left, right) in enumerate(zip(refs[:-3:2], refs[1:-3:2], strict=True)):
        product = matmul if i < turned else outer_sum
        value = product(left[...], right[...])
        at = store_halves(value, at, mine_ref, other_ref, wide_ref)


def embed_back(*refs):
    back_ref, counts_ref = refs[:2]
    slopes, grids = refs[2 : 2 + GROUPS], refs[2 + GROUPS : 2 + 2 * GROUPS]
    mine_ref, other_ref, wide_ref = refs[2 + 2 * GROUPS :]
    nodes = back_ref.shape[0]
    variables = grids[0].shape[0]
    grads = []
    for p in range(GROUPS):
        latent = matmul(counts_ref[:, p * nodes : (p + 1) * nodes], back_ref[...])
        grads.append((latent * slopes[p][...]).astype(HALF))
    total = matmul(
        jnp.concatenate([grid[:variables] for grid in grids], 1), jnp.concatenate(grads, 0)
    )
    store_halves(total, 0, mine_ref, other_ref, wide_ref)


def split_gradients(body, rows, width, macs, *args):
    outs = [shape(rows, width, HALF)] * 2
    return whole(body, outs, macs, *args, scratch=[pltpu.VMEM((width, width), SINGLE)])


def add_halves(*refs):
    out_ref = refs[-1]
    at = 0
    for mine, other in zip(refs[:-1:2], refs[1:-1:2], strict=True):
        rows = mine.shape[0]
        out_ref[at : at + rows] = (
            mine[...].astype(SINGLE) + other[...].astype(SINGLE)
        ).astype(HALF)
        at += rows


def add_pieces(pieces_ref, out_ref):
    total = pieces_ref[0].astype(SINGLE)
    for i in range(1, pieces_ref.shape[0]):
        total = total + pieces_ref[i].astype(SINGLE)
    out_ref[...] = total.astype(HALF)


def add_bands(*refs):
    out_ref = refs[-1]
    total = refs[0][...].astype(SINGLE)
    for ref in refs[1:-1]:
        total = total + ref[...].astype(SINGLE)
    total = total.astype(HALF)
    for i in range(out_ref.shape[0]):
        out_ref[i] = total


def places(outs):
    encode, self_, near, decode = outs
    return [(decode, None), (self_, 1), (near, 1), (self_, 0), (near, 0), (encode, None)]


def store_squares(first, half, value_ref, outs, buffer_ref, sems):
    rows = outs[0].shape[0] // 2
    spot = pl.ds(pl.multiple_of(half * rows, rows), rows)
    copies = []
    for i, (out, which) in enumerate(places(outs)):
        at = i * rows
        buffer_ref[at : at + rows] = value_ref[first + at : first + at + rows].astype(SINGLE)
        target = out.at[spot] if which is None else out.at[which, spot]
        copies.append(
            pltpu.make_async_copy(buffer_ref.at[at : at + rows], target, sems.at[i])
        )
        copies[-1].start()
    return copies


def unpack_own(part_ref, *refs):
    outs, (buffer_ref, sems) = refs[:4], refs[4:]
    first = (part_ref.shape[0] - buffer_ref.shape[0]) // 2
    half = lax.axis_index("dom") % 2
    for copy in store_squares(first, half, part_ref, outs, buffer_ref, sems):
        copy.wait()


def unpack_other(part_ref, other_ref, *refs):
    outs, narrow, (buffer_ref, sems, *held) = refs[4:8], refs[8:10], refs[10:]
    rows = (part_ref.shape[0] - buffer_ref.shape[0]) // 2
    half = lax.axis_index("dom") % 2
    copies = []
    odd = odd_along("dom")
    for i, at in enumerate((part_ref.shape[0] - rows, 0)):
        own = part_ref[at : at + rows].astype(SINGLE)
        far = other_ref[at : at + rows].astype(SINGLE)
        held[i][:rows] = jnp.where(odd, far, own)
        held[i][rows:] = jnp.where(odd, own, far)[: held[i].shape[0] - rows]
        copies.append(pltpu.make_async_copy(held[i], narrow[i], sems.at[6 + i]))
        copies[-1].start()
    copies += store_squares(rows, 1 - half, other_ref, outs, buffer_ref, sems)
    for copy in copies:
        copy.wait()


def unpack(part, other, width, variables):
    full = shape(width, width, SINGLE)
    pair = jax.ShapeDtypeStruct((2, width, width), SINGLE)
    narrow = shape(variables, width, SINGLE)
    squares = [full, pair, pair, full]
    hbm = pl.BlockSpec(memory_space=pltpu.HBM)
    vmem = pl.BlockSpec(memory_space=pltpu.VMEM)
    scratch = [
        pltpu.VMEM((6 * split_rows(width), width), SINGLE),
        pltpu.SemaphoreType.DMA((8,)),
    ]
    params = pltpu.CompilerParams(vmem_limit_bytes=32 * MIB)
    size = part.size * 6
    cost = pl.CostEstimate(flops=0, bytes_accessed=size, transcendentals=0)
    grads = pl.pallas_call(
        unpack_own,
        out_shape=squares,
        in_specs=[vmem],
        out_specs=[hbm] * 4,
        scratch_shapes=scratch,
        compiler_params=params,
        cost_estimate=cost,
    )(part)
    return pl.pallas_call(
        unpack_other,
        out_shape=[*squares, narrow, narrow],
        in_specs=[vmem, vmem] + [hbm] * 4,
        out_specs=[hbm] * 6,
        input_output_aliases={2: 0, 3: 1, 4: 2, 5: 3},
        scratch_shapes=scratch + [pltpu.VMEM((variables, width), SINGLE)] * 2,
        compiler_params=params,
        cost_estimate=cost,
    )(part, other, *grads)


def reduce_all(part):
    count = lax.axis_size("dom")
    bands = lax.axis_size("band")
    groups = [list(range(c, count, 2)) for c in range(2)]
    chips = count // 2
    rows, width = part.shape[0] // chips, part.shape[1]
    pieces = lax.all_to_all(
        part.reshape(chips, rows, width), "dom", 0, 0, axis_index_groups=groups
    )
    (piece,) = whole(add_pieces, [shape(rows, width, HALF)], 0, pieces)
    others = [
        lax.ppermute(piece, "band", [(i, (i + step) % bands) for i in range(bands)])
        for step in range(1, bands)
    ]
    copies = jax.ShapeDtypeStruct((chips, rows, width), HALF)
    (copies,) = whole(add_bands, [copies], 0, piece, *others)
    return lax.all_to_all(copies, "dom", 0, 0, axis_index_groups=groups).reshape(part.shape)


def shards(
    grid_vars,
    cotangent,
    mesh_static,
    embed_weight,
    encode_weight,
    self_weight,
    neighbor_weight,
    decode_weight,
    output_weight,
    grid_sender,
    mesh_receiver,
    neighbors,
    mesh_sender,
    grid_receiver,
):
    grid_count, variables = grid_vars.shape
    mesh_count, width = mesh_static.shape
    rim = 2 * RIM
    ext = mesh_count + 2 * rim
    grid, cot, near, out_weight = grid_vars.T, cotangent.T, neighbors.T, output_weight.T
    grid_send, mesh_recv, mesh_send, grid_recv = (
        index.reshape(-1, LANES) for index in (grid_sender, mesh_receiver, mesh_sender, grid_receiver)
    )
    step = grid_send.shape[0] // GROUPS * LANES
    nodes = GROUPS * mesh_count
    mesh_rows = shape(mesh_count, width, HALF)
    mesh_full = shape(mesh_count, width, SINGLE)
    grid_rows = shape(grid_count, width, HALF)
    grid_full = shape(grid_count, width, SINGLE)
    parcel = shape(variables + -variables % 16 + INDEX_ROWS // 2, grid_count, HALF)
    sent = fetching(
        parcels, [parcel] * (GROUPS - 1), 0, grid, grid_send, mesh_send, near, limit=58
    )
    arrived = swap_all(*sent)
    embed_macs = grid_count * variables * width + mesh_count * grid_count * (step + width)
    slope_embed, total, held_weight = fetching(
        embed_own,
        [grid_full, mesh_full, shape(variables, width, HALF)],
        embed_macs,
        grid,
        embed_weight,
        grid_send,
        mesh_recv,
        limit=32,
    )
    index = [None] * GROUPS
    slopes = [slope_embed] + [None] * (GROUPS - 1)
    grids = [grid, *arrived]
    for p in range(1, GROUPS):
        index[p], slopes[p], total = whole(
            lambda *refs, p=p: embed_far(p, *refs),
            [shape(INDEX_ROWS, LANES, jnp.int32), grid_full, mesh_full],
            embed_macs,
            arrived[p - 1],
            held_weight,
            mesh_recv,
            total,
        )
    encode_in, slope_encode, state, half, on, off = whole(
        encode,
        [mesh_rows, mesh_full, mesh_full, mesh_rows] + [shape(rim, width, HALF)] * 2,
        mesh_count * width * width,
        total,
        encode_weight,
        mesh_static,
    )
    off = swap_off(off)
    on = swap_on(on)
    counts, turned = whole(
        near_counts, [shape(ext, ext, HALF)] * 2, ext * ext * 64, near, index[1], index[2]
    )
    count_macs = nodes * grid_count * step
    (to_grid,) = whole(
        lambda *refs: grid_counts(False, *refs),
        [shape(grid_count, nodes, HALF)],
        count_macs,
        mesh_send,
        grid_recv,
        *index[1:],
    )
    state, to_grid = lax.optimization_barrier((state, to_grid))
    final_half, pre_0, pre_1, half_1, nearby_0, nearby_1 = whole(
        process,
        [mesh_rows, shape(ext - rim, width, SINGLE), mesh_full] + [mesh_rows] * 3,
        (ext + mesh_count) * (ext + 2 * width) * width,
        half,
        state,
        on,
        off,
        counts,
        self_weight,
        neighbor_weight,
        scratch=[pltpu.VMEM((ext, width), HALF)],
    )
    moved = swap_all(*[final_half] * 4)
    finals = [final_half] + [moved[p - 1] for p in (4, 3, 2, 1)]
    (from_grid,) = whole(
        lambda *refs: grid_counts(True, *refs),
        [shape(nodes, grid_count, HALF)],
        count_macs,
        lax.optimization_barrier((mesh_send, final_half))[0],
        grid_recv,
        *index[1:],
    )
    hidden_grad = outer_sum(cot, out_weight)
    decode_in, hidden, decode_grad, state_grad, *sums = whole(
        decode,
        [grid_rows] * 3 + [mesh_full] + [mesh_rows] * (GROUPS - 1),
        2 * grid_count * width * (nodes + width),
        *finals,
        to_grid,
        from_grid,
        decode_weight,
        hidden_grad,
    )
    moved = swap_all(*sums)
    arrived = [moved[p - 1] for p in (1, 2, 3, 4)]
    prediction = (grid.astype(SINGLE) + back_mul(out_weight, hidden)).astype(HALF)
    half_rows = split_rows(width)
    narrow_rows = split_rows(variables)
    square = width * width
    decode_halves = split_gradients(
        lambda *refs: gradient_halves(1, *refs),
        narrow_rows + half_rows,
        width,
        2 * grid_count * square,
        cot,
        hidden,
        decode_in,
        decode_grad,
    )
    to_mesh = whole(
        mesh_counts,
        [shape(grid_count, nodes, HALF)],
        count_macs,
        lax.optimization_barrier((grid_send, decode_in))[0],
        mesh_recv,
        *index[1:],
    )[0]
    state_grad, to_mesh, *decode_halves = lax.optimization_barrier(
        (state_grad, to_mesh, *decode_halves)
    )
    state_grad, layer_1, on, off = whole(
        gather_back,
        [mesh_full, mesh_rows] + [shape(rim + RIM, width, HALF)] * 2,
        0,
        state_grad,
        *arrived,
        silu_slope(pre_1),
    )
    off = swap_off(off)
    on = swap_on(on)
    layer_halves = split_gradients(
        lambda *refs: gradient_halves(0, *refs),
        2 * half_rows,
        width,
        2 * mesh_count * square,
        half_1,
        layer_1,
        nearby_1,
        layer_1,
    )
    halves = [decode_halves[0], swap_on(decode_halves[1])]
    state_grad, *layer_halves, halves[1] = lax.optimization_barrier(
        (state_grad, *layer_halves, halves[1])
    )
    state_grad, layer_0, encode_grad, encode_in_grad = whole(
        process_back,
        [mesh_full, mesh_rows, mesh_rows, mesh_rows],
        (ext + mesh_count) * (ext + 2 * width) * width,
        state_grad,
        layer_1,
        on,
        off,
        turned,
        silu_slope(pre_0),
        slope_encode,
        self_weight,
        neighbor_weight,
        encode_weight,
        scratch=[pltpu.VMEM((ext, width), HALF)],
    )
    rest_halves = split_gradients(
        lambda *refs: gradient_halves(0, *refs),
        3 * half_rows,
        width,
        3 * mesh_count * square,
        half,
        layer_0,
        nearby_0,
        layer_0,
        encode_in,
        encode_grad,
    )
    embed_halves = split_gradients(
        embed_back,
        narrow_rows,
        width,
        grid_count * width * (nodes + GROUPS * variables),
        encode_in_grad,
        to_mesh,
        *slopes,
        *grids,
    )
    for mine, other in (layer_halves, rest_halves, embed_halves):
        halves += [mine, swap_on(other)]
    rows = sum(block.shape[0] for block in halves[::2])
    (part,) = whole(add_halves, [shape(rows, width, HALF)], 0, *halves)
    part = reduce_all(part)
    other = swap_on(part)
    grad_encode, grad_self, grad_near, grad_decode, grad_embed, grad_output = unpack(
        part, other, width, variables
    )
    return (
        prediction.T,
        state_grad,
        grad_embed,
        grad_encode,
        grad_self,
        grad_near,
        grad_decode,
        grad_output.T,
    )


def solution(mesh):
    placed = (
        P(("band", "dom"), None),
        P(("band", "dom"), None),
        P(("band", "dom"), None),
        P(),
        P(),
        P(),
        P(),
        P(),
        P(),
        P(("band", "dom")),
        P(("band", "dom")),
        P(("band", "dom"), None),
        P(("band", "dom")),
        P(("band", "dom")),
    )
    return jax.shard_map(
        shards,
        mesh=mesh,
        in_specs=placed,
        out_specs=(
            P(("band", "dom"), None),
            P(("band", "dom"), None),
            P(),
            P(),
            P(),
            P(),
            P(),
            P(),
        ),
        check_vma=False,
    )
```

```python
import jax
import jax.numpy as jnp
from jax import lax
from jax.experimental import pallas as pl
from jax.experimental.pallas import tpu as pltpu
from jax.sharding import PartitionSpec as P

NEAR = 6
RIM = 64
GROUPS = 5
LANES = 128
HALF = jnp.bfloat16
SINGLE = jnp.float32
MIB = 1024 * 1024
SLOT_ROWS = 6
INDEX_ROWS = 32


def silu_slope(values):
    sigma = jax.nn.sigmoid(values)
    return sigma * (1.0 + values * (1.0 - sigma))


def matmul(left, right):
    return jnp.dot(left, right, preferred_element_type=SINGLE)


def outer_sum(left, right):
    return lax.dot_general(
        left, right, (((0,), (0,)), ((), ())), preferred_element_type=SINGLE
    )


def back_mul(left, right):
    return lax.dot_general(
        left, right, (((1,), (1,)), ((), ())), preferred_element_type=SINGLE
    )


def swap_on(value):
    count = lax.axis_size("dom")
    return lax.ppermute(value, "dom", [(i, i ^ 1) for i in range(count)])


def swap_off(value):
    count = lax.axis_size("dom")
    return lax.ppermute(
        value, "dom", [(i, (i + (1 if i % 2 else -1)) % count) for i in range(count)]
    )


def swap_band(value, first):
    count = lax.axis_size("band")
    pairs = []
    for low in range(first, count - 1, 2):
        pairs += [(low, low + 1), (low + 1, low)]
    return lax.ppermute(value, "band", pairs)


def swap_all(on, off, north, south):
    south = swap_band(south, 1)
    north = swap_band(north, 0)
    off = swap_off(off)
    return swap_on(on), off, north, south


def by_partner(slots, odd_dom, odd_band, incoming):
    flip_dom = odd_dom != incoming
    flip_band = odd_band != incoming
    return [
        slots[0],
        jnp.where(flip_dom, slots[2], slots[1]),
        jnp.where(flip_dom, slots[1], slots[2]),
        jnp.where(flip_band, slots[4], slots[3]),
        jnp.where(flip_band, slots[3], slots[4]),
    ]


def whole(body, outs, macs, *args, limit=32, scratch=()):
    moved = sum(a.size * a.dtype.itemsize for a in (*args, *outs))
    return pl.pallas_call(
        body,
        out_shape=outs,
        scratch_shapes=scratch,
        compiler_params=pltpu.CompilerParams(vmem_limit_bytes=limit * MIB),
        cost_estimate=pl.CostEstimate(flops=2 * macs, bytes_accessed=moved, transcendentals=0),
    )(*args)


def shape(rows, columns, kind):
    return jax.ShapeDtypeStruct((rows, columns), kind)


def odd_along(axis):
    return lax.axis_index(axis) % 2 == 1


def hot(rows, index):
    spots = lax.broadcasted_iota(jnp.int32, (rows, LANES), 0)
    one = [
        jnp.where(spots == index[j : j + 1], 1.0, 0.0).astype(HALF) for j in range(index.shape[0])
    ]
    return jnp.concatenate(one, 1)


def pair_counts(rows, row_count, columns, column_count):
    return back_mul(hot(row_count, rows), hot(column_count, columns)).astype(HALF)


def slots_of(index):
    step = index.shape[0] // GROUPS
    return [index[k * step : (k + 1) * step] for k in range(GROUPS)]


def fetch(sources, buffers, sems):
    copies = [
        pltpu.make_async_copy(source, buffer, sems.at[i])
        for i, (source, buffer) in enumerate(zip(sources, buffers, strict=True))
    ]
    for copy in copies:
        copy.start()
    for copy in copies:
        copy.wait()


def fetching(body, outs, macs, *args, limit):
    moved = sum(a.size * a.dtype.itemsize for a in (*args, *outs))
    return pl.pallas_call(
        body,
        out_shape=outs,
        in_specs=[pl.BlockSpec(memory_space=pltpu.HBM)] * len(args),
        scratch_shapes=[pltpu.VMEM(a.shape, a.dtype) for a in args]
        + [pltpu.SemaphoreType.DMA((len(args),))],
        compiler_params=pltpu.CompilerParams(vmem_limit_bytes=limit * MIB),
        cost_estimate=pl.CostEstimate(flops=2 * macs, bytes_accessed=moved, transcendentals=0),
    )(*args)


def parcels(*refs):
    inputs, rest = refs[:4], refs[4:]
    outs, buffers, sems = rest[: GROUPS - 1], rest[GROUPS - 1 : -1], rest[-1]
    fetch(inputs, buffers, sems)
    grid_ref, grid_send_ref, mesh_send_ref, near_ref = buffers
    odd_dom, odd_band = odd_along("dom"), odd_along("band")
    grid_send = by_partner(slots_of(grid_send_ref[...]), odd_dom, odd_band, False)
    mesh_send = by_partner(slots_of(mesh_send_ref[...]), odd_dom, odd_band, False)
    near = near_ref[...]
    near = [near[:, j : j + LANES] for j in range(0, near.shape[1], LANES)]
    variables, count = grid_ref.shape
    first = outs[0].shape[0] - INDEX_ROWS // 2
    grid = grid_ref[...]
    for p, out in enumerate(outs):
        parts = [mesh_send[p + 1], grid_send[p + 1], *near]
        used = sum(part.shape[0] for part in parts)
        parts.append(jnp.zeros((INDEX_ROWS - used, LANES), jnp.int32))
        index = jnp.concatenate(parts, 0)
        high = (index >> 1).astype(SINGLE)
        low = (index & 1).astype(SINGLE)
        cut = INDEX_ROWS // 2
        out[:variables] = grid
        out[variables:first] = jnp.zeros((first - variables, count), HALF)
        out[first:] = jnp.concatenate([high[:cut], low[:cut], high[cut:], low[cut:]], 1).astype(HALF)


def index_of(packed):
    packed = packed.astype(SINGLE)
    halves = [
        packed[:, j : j + LANES] * 2.0 + packed[:, j + LANES : j + 2 * LANES]
        for j in (0, 2 * LANES)
    ]
    return jnp.concatenate(halves, 0).astype(jnp.int32)


def embed_own(*refs):
    inputs, (slope_ref, sum_ref, held_ref), buffers, sems = refs[:4], refs[4:7], refs[7:-1], refs[-1]
    fetch(inputs, buffers, sems)
    grid_ref, weight_ref, send_ref, recv_ref = buffers
    step = send_ref.shape[0] // GROUPS
    counts = pair_counts(
        recv_ref[:step], sum_ref.shape[0], send_ref[:step], grid_ref.shape[1]
    )
    pre = outer_sum(grid_ref[...], weight_ref[...])
    sigma = jax.nn.sigmoid(pre)
    slope_ref[...] = sigma * (1.0 + pre * (1.0 - sigma))
    sum_ref[...] = matmul(counts, (pre * sigma).astype(HALF))
    held_ref[...] = weight_ref[...]


def embed_far(p, parcel_ref, weight_ref, recv_ref, sum_ref, index_ref, slope_ref, out_ref):
    index = index_of(parcel_ref[parcel_ref.shape[0] - INDEX_ROWS // 2 :])
    index_ref[...] = index
    step = recv_ref.shape[0] // GROUPS
    recv = by_partner(slots_of(recv_ref[...]), odd_along("dom"), odd_along("band"), True)[p]
    counts = pair_counts(
        recv, out_ref.shape[0], index[step : 2 * step], parcel_ref.shape[1]
    )
    pre = outer_sum(parcel_ref[: weight_ref.shape[0]], weight_ref[...])
    sigma = jax.nn.sigmoid(pre)
    slope_ref[...] = sigma * (1.0 + pre * (1.0 - sigma))
    out_ref[...] = sum_ref[...] + matmul(counts, (pre * sigma).astype(HALF))


def encode(sum_ref, weight_ref, static_ref, in_ref, slope_ref, state_ref, half_ref, on_ref, off_ref):
    encode_in = sum_ref[...].astype(HALF)
    pre = matmul(encode_in, weight_ref[...])
    sigma = jax.nn.sigmoid(pre)
    state = static_ref[...].astype(SINGLE) + pre * sigma
    half = state.astype(HALF)
    in_ref[...] = encode_in
    slope_ref[...] = sigma * (1.0 + pre * (1.0 - sigma))
    state_ref[...] = state
    half_ref[...] = half
    rows = on_ref.shape[0]
    odd = odd_along("dom")
    head, tail = half[:rows], half[half.shape[0] - rows :]
    on_ref[...] = jnp.where(odd, head, tail)
    off_ref[...] = jnp.where(odd, tail, head)


def near_counts(near_ref, on_ref, off_ref, out_ref, turned_ref):
    step = near_ref.shape[0]
    mesh_count = near_ref.shape[1]
    first = 2 * SLOT_ROWS
    odd_dom = odd_along("dom")
    on, off = on_ref[...], off_ref[...]
    left = jnp.where(odd_dom, on, off)[first + step : first + 2 * step] + (RIM - mesh_count)
    right = jnp.where(odd_dom, off, on)[first : first + step] + (RIM + mesh_count)
    own = near_ref[...] + RIM
    index = jnp.concatenate([left, own, right], 1)
    spots = lax.broadcasted_iota(jnp.int32, out_ref.shape, 0)
    counts = jnp.zeros(out_ref.shape, SINGLE)
    for j in range(step):
        counts = counts + jnp.where(spots == index[j : j + 1], 1.0, 0.0)
    turned_ref[...] = counts.astype(HALF)
    out_ref[...] = counts.T.astype(HALF)


def process(
    half_ref, state_ref, on_ref, off_ref, counts_ref, self_ref, near_ref,
    final_ref, pre_0_ref, pre_1_ref, half_1_ref, nearby_0_ref, nearby_1_ref, whole_ref,
):
    rim = on_ref.shape[0]
    count = half_ref.shape[0]
    own = slice(rim, rim + count)
    odd = odd_along("dom")
    left = jnp.where(odd, on_ref[...], off_ref[...])
    right = jnp.where(odd, off_ref[...], on_ref[...])
    whole_ref[:rim] = left
    whole_ref[own] = half_ref[...]
    whole_ref[rim + count :] = right
    half_0 = whole_ref[...]
    used = slice(RIM, 3 * RIM + count)
    nearby_0 = (matmul(counts_ref[used], half_0) * (1.0 / NEAR)).astype(HALF)
    nearby_0_ref[...] = nearby_0[RIM : RIM + count]
    pre_0 = matmul(half_0[used], self_ref[0]) + matmul(nearby_0, near_ref[0])
    pre_0_ref[...] = pre_0
    grown = pre_0 * jax.nn.sigmoid(pre_0)
    state_1 = state_ref[...] + grown[RIM : RIM + count]
    half_1 = state_1.astype(HALF)
    whole_ref[RIM:rim] = (left[RIM:].astype(SINGLE) + grown[:RIM]).astype(HALF)
    whole_ref[own] = half_1
    whole_ref[rim + count : rim + count + RIM] = (
        right[:RIM].astype(SINGLE) + grown[RIM + count :]
    ).astype(HALF)
    half_1_ref[...] = half_1
    nearby_1 = (matmul(counts_ref[own], whole_ref[...]) * (1.0 / NEAR)).astype(HALF)
    nearby_1_ref[...] = nearby_1
    pre_1 = matmul(half_1, self_ref[1]) + matmul(nearby_1, near_ref[1])
    pre_1_ref[...] = pre_1
    final_ref[...] = (state_1 + pre_1 * jax.nn.sigmoid(pre_1)).astype(HALF)


def grid_counts(turned, send_ref, recv_ref, *refs):
    far, out_ref = refs[: GROUPS - 1], refs[GROUPS - 1]
    odd_dom, odd_band = odd_along("dom"), odd_along("band")
    step = send_ref.shape[0] // GROUPS
    recv = by_partner(slots_of(recv_ref[...]), odd_dom, odd_band, True)
    send = [send_ref[:step]] + [ref[:step] for ref in far]
    nodes = out_ref.shape[0 if turned else 1] // GROUPS
    grids = out_ref.shape[1 if turned else 0]
    for p in range(GROUPS):
        at = slice(p * nodes, (p + 1) * nodes)
        if turned:
            out_ref[at] = pair_counts(send[p], nodes, recv[p], grids)
        else:
            out_ref[:, at] = pair_counts(recv[p], grids, send[p], nodes)


def mesh_counts(send_ref, recv_ref, *refs):
    far, out_ref = refs[: GROUPS - 1], refs[GROUPS - 1]
    step = send_ref.shape[0] // GROUPS
    send = [send_ref[:step]] + [ref[step : 2 * step] for ref in far]
    recv = by_partner(slots_of(recv_ref[...]), odd_along("dom"), odd_along("band"), True)
    grids, nodes = out_ref.shape[0], out_ref.shape[1] // GROUPS
    for p in range(GROUPS):
        out_ref[:, p * nodes : (p + 1) * nodes] = pair_counts(send[p], grids, recv[p], nodes)


def decode(*refs):
    finals = [refs[i] for i in (0, 4, 3, 2, 1)]
    counts_ref, turned_ref, weight_ref, back_ref = refs[GROUPS : GROUPS + 4]
    in_ref, hidden_ref, grad_ref, own_ref, *outs = refs[GROUPS + 4 :]
    nodes = own_ref.shape[0]
    total = matmul(counts_ref[:, :nodes], finals[0][...])
    for p in range(1, GROUPS):
        total = total + matmul(counts_ref[:, p * nodes : (p + 1) * nodes], finals[p][...])
    decode_in = total.astype(HALF)
    in_ref[...] = decode_in
    pre = matmul(decode_in, weight_ref[...])
    sigma = jax.nn.sigmoid(pre)
    hidden_ref[...] = (pre * sigma).astype(HALF)
    grad = (back_ref[...] * (sigma * (1.0 + pre * (1.0 - sigma)))).astype(HALF)
    grad_ref[...] = grad
    in_grad = back_mul(grad, weight_ref[...]).astype(HALF)
    own_ref[...] = matmul(turned_ref[:nodes], in_grad)
    for p, out in enumerate(outs):
        out[...] = matmul(turned_ref[(p + 1) * nodes : (p + 2) * nodes], in_grad).astype(HALF)


def gather_back(*refs):
    total = refs[0][...]
    for ref in refs[1:GROUPS]:
        total = total + ref[...].astype(SINGLE)
    slope_ref, state_ref, layer_ref, on_ref, off_ref = refs[GROUPS:]
    state_ref[...] = total
    layer = (total * slope_ref[...]).astype(HALF)
    layer_ref[...] = layer
    half = total.astype(HALF)
    odd = odd_along("dom")
    rim, count = RIM, total.shape[0]
    heads = jnp.concatenate([layer[: 2 * rim], half[:rim]], 0)
    tails = jnp.concatenate([layer[count - 2 * rim :], half[count - rim :]], 0)
    on_ref[...] = jnp.where(odd, heads, tails)
    off_ref[...] = jnp.where(odd, tails, heads)


def process_back(
    state_ref, layer_ref, on_ref, off_ref, turned_ref, slope_0_ref, slope_in_ref,
    self_ref, near_ref, encode_ref, static_ref, layer_0_ref, encode_grad_ref, back_ref, whole_ref,
):
    rim = RIM
    count = state_ref.shape[0]
    own = slice(2 * rim, 2 * rim + count)
    odd = odd_along("dom")
    on, off = on_ref[...], off_ref[...]
    left, right = jnp.where(odd, on, off), jnp.where(odd, off, on)
    whole_ref[: 2 * rim] = left[: 2 * rim]
    whole_ref[own] = layer_ref[...]
    whole_ref[2 * rim + count :] = right[: 2 * rim]
    layer_1 = whole_ref[...]
    used = slice(rim, 3 * rim + count)
    inner = slice(rim, rim + count)
    spread = (matmul(turned_ref[used], layer_1) * (1.0 / NEAR)).astype(HALF)
    back = back_mul(layer_1[used], self_ref[1]) + back_mul(spread, near_ref[1])
    state_own = state_ref[...] + back[inner]
    first = left[2 * rim :].astype(SINGLE) + back[:rim]
    last = right[2 * rim :].astype(SINGLE) + back[rim + count :]
    layer_0 = (state_own * slope_0_ref[inner]).astype(HALF)
    layer_0_ref[...] = layer_0
    whole_ref[:rim] = jnp.zeros((rim, back.shape[1]), HALF)
    whole_ref[rim : 2 * rim] = (first * slope_0_ref[:rim]).astype(HALF)
    whole_ref[own] = layer_0
    whole_ref[2 * rim + count : 3 * rim + count] = (last * slope_0_ref[rim + count :]).astype(HALF)
    whole_ref[3 * rim + count :] = jnp.zeros((rim, back.shape[1]), HALF)
    spread = (matmul(turned_ref[own], whole_ref[...]) * (1.0 / NEAR)).astype(HALF)
    state = state_own + back_mul(layer_0, self_ref[0]) + back_mul(spread, near_ref[0])
    static_ref[...] = state
    grad = (state * slope_in_ref[...]).astype(HALF)
    encode_grad_ref[...] = grad
    back_ref[...] = back_mul(grad, encode_ref[...]).astype(HALF)


def split_rows(count):
    return -(-count // (2 * LANES)) * LANES


def store_halves(value, at, mine_ref, other_ref, wide_ref):
    odd = lax.axis_index("dom") % 2
    count, rows = value.shape[0], split_rows(value.shape[0])
    wide_ref[:count] = value
    if count < 2 * rows:
        wide_ref[count : 2 * rows] = jnp.zeros((2 * rows - count, value.shape[1]), SINGLE)
    mine = pl.ds(pl.multiple_of(odd * rows, rows), rows)
    other = pl.ds(pl.multiple_of((1 - odd) * rows, rows), rows)
    mine_ref[at : at + rows] = wide_ref[mine].astype(HALF)
    other_ref[at : at + rows] = wide_ref[other].astype(HALF)
    return at + rows


def gradient_halves(turned, *refs):
    mine_ref, other_ref, wide_ref = refs[-3:]
    at = 0
    for i, (left, right) in enumerate(zip(refs[:-3:2], refs[1:-3:2], strict=True)):
        product = matmul if i < turned else outer_sum
        value = product(left[...], right[...])
        at = store_halves(value, at, mine_ref, other_ref, wide_ref)


def embed_back(*refs):
    back_ref, counts_ref = refs[:2]
    slopes, grids = refs[2 : 2 + GROUPS], refs[2 + GROUPS : 2 + 2 * GROUPS]
    mine_ref, other_ref, wide_ref = refs[2 + 2 * GROUPS :]
    nodes = back_ref.shape[0]
    variables = grids[0].shape[0]
    grads = []
    for p in range(GROUPS):
        latent = matmul(counts_ref[:, p * nodes : (p + 1) * nodes], back_ref[...])
        grads.append((latent * slopes[p][...]).astype(HALF))
    total = matmul(
        jnp.concatenate([grid[:variables] for grid in grids], 1), jnp.concatenate(grads, 0)
    )
    store_halves(total, 0, mine_ref, other_ref, wide_ref)


def split_gradients(body, rows, width, macs, *args):
    outs = [shape(rows, width, HALF)] * 2
    return whole(body, outs, macs, *args, scratch=[pltpu.VMEM((width, width), SINGLE)])


def add_halves(*refs):
    out_ref = refs[-1]
    at = 0
    for mine, other in zip(refs[:-1:2], refs[1:-1:2], strict=True):
        rows = mine.shape[0]
        out_ref[at : at + rows] = (
            mine[...].astype(SINGLE) + other[...].astype(SINGLE)
        ).astype(HALF)
        at += rows


def add_pieces(pieces_ref, out_ref):
    total = pieces_ref[0].astype(SINGLE)
    for i in range(1, pieces_ref.shape[0]):
        total = total + pieces_ref[i].astype(SINGLE)
    out_ref[...] = total.astype(HALF)


def add_bands(*refs):
    out_ref = refs[-1]
    total = refs[0][...].astype(SINGLE)
    for ref in refs[1:-1]:
        total = total + ref[...].astype(SINGLE)
    total = total.astype(HALF)
    for i in range(out_ref.shape[0]):
        out_ref[i] = total


def places(outs):
    encode, self_, near, decode = outs
    return [(decode, None), (self_, 1), (near, 1), (self_, 0), (near, 0), (encode, None)]


def store_squares(first, half, value_ref, outs, buffer_ref, sems):
    rows = outs[0].shape[0] // 2
    spot = pl.ds(pl.multiple_of(half * rows, rows), rows)
    copies = []
    for i, (out, which) in enumerate(places(outs)):
        at = i * rows
        buffer_ref[at : at + rows] = value_ref[first + at : first + at + rows].astype(SINGLE)
        target = out.at[spot] if which is None else out.at[which, spot]
        copies.append(
            pltpu.make_async_copy(buffer_ref.at[at : at + rows], target, sems.at[i])
        )
        copies[-1].start()
    return copies


def unpack_own(part_ref, *refs):
    outs, (buffer_ref, sems) = refs[:4], refs[4:]
    first = (part_ref.shape[0] - buffer_ref.shape[0]) // 2
    half = lax.axis_index("dom") % 2
    for copy in store_squares(first, half, part_ref, outs, buffer_ref, sems):
        copy.wait()


def unpack_other(part_ref, other_ref, *refs):
    outs, narrow, (buffer_ref, sems, *held) = refs[4:8], refs[8:10], refs[10:]
    rows = (part_ref.shape[0] - buffer_ref.shape[0]) // 2
    half = lax.axis_index("dom") % 2
    copies = []
    odd = odd_along("dom")
    for i, at in enumerate((part_ref.shape[0] - rows, 0)):
        own = part_ref[at : at + rows].astype(SINGLE)
        far = other_ref[at : at + rows].astype(SINGLE)
        held[i][:rows] = jnp.where(odd, far, own)
        held[i][rows:] = jnp.where(odd, own, far)[: held[i].shape[0] - rows]
        copies.append(pltpu.make_async_copy(held[i], narrow[i], sems.at[6 + i]))
        copies[-1].start()
    copies += store_squares(rows, 1 - half, other_ref, outs, buffer_ref, sems)
    for copy in copies:
        copy.wait()


def unpack(part, other, width, variables):
    full = shape(width, width, SINGLE)
    pair = jax.ShapeDtypeStruct((2, width, width), SINGLE)
    narrow = shape(variables, width, SINGLE)
    squares = [full, pair, pair, full]
    hbm = pl.BlockSpec(memory_space=pltpu.HBM)
    vmem = pl.BlockSpec(memory_space=pltpu.VMEM)
    scratch = [
        pltpu.VMEM((6 * split_rows(width), width), SINGLE),
        pltpu.SemaphoreType.DMA((8,)),
    ]
    params = pltpu.CompilerParams(vmem_limit_bytes=32 * MIB)
    size = part.size * 6
    cost = pl.CostEstimate(flops=0, bytes_accessed=size, transcendentals=0)
    grads = pl.pallas_call(
        unpack_own,
        out_shape=squares,
        in_specs=[vmem],
        out_specs=[hbm] * 4,
        scratch_shapes=scratch,
        compiler_params=params,
        cost_estimate=cost,
    )(part)
    return pl.pallas_call(
        unpack_other,
        out_shape=[*squares, narrow, narrow],
        in_specs=[vmem, vmem] + [hbm] * 4,
        out_specs=[hbm] * 6,
        input_output_aliases={2: 0, 3: 1, 4: 2, 5: 3},
        scratch_shapes=scratch + [pltpu.VMEM((variables, width), SINGLE)] * 2,
        compiler_params=params,
        cost_estimate=cost,
    )(part, other, *grads)


def reduce_all(part):
    count = lax.axis_size("dom")
    bands = lax.axis_size("band")
    groups = [list(range(c, count, 2)) for c in range(2)]
    chips = count // 2
    rows, width = part.shape[0] // chips, part.shape[1]
    pieces = lax.all_to_all(
        part.reshape(chips, rows, width), "dom", 0, 0, axis_index_groups=groups
    )
    (piece,) = whole(add_pieces, [shape(rows, width, HALF)], 0, pieces)
    others = [
        lax.ppermute(piece, "band", [(i, (i + step) % bands) for i in range(bands)])
        for step in range(1, bands)
    ]
    copies = jax.ShapeDtypeStruct((chips, rows, width), HALF)
    (copies,) = whole(add_bands, [copies], 0, piece, *others)
    return lax.all_to_all(copies, "dom", 0, 0, axis_index_groups=groups).reshape(part.shape)


def shards(
    grid_vars,
    cotangent,
    mesh_static,
    embed_weight,
    encode_weight,
    self_weight,
    neighbor_weight,
    decode_weight,
    output_weight,
    grid_sender,
    mesh_receiver,
    neighbors,
    mesh_sender,
    grid_receiver,
):
    grid_count, variables = grid_vars.shape
    mesh_count, width = mesh_static.shape
    rim = 2 * RIM
    ext = mesh_count + 2 * rim
    grid, cot, near, out_weight = grid_vars.T, cotangent.T, neighbors.T, output_weight.T
    grid_send, mesh_recv, mesh_send, grid_recv = (
        index.reshape(-1, LANES) for index in (grid_sender, mesh_receiver, mesh_sender, grid_receiver)
    )
    step = grid_send.shape[0] // GROUPS * LANES
    nodes = GROUPS * mesh_count
    mesh_rows = shape(mesh_count, width, HALF)
    mesh_full = shape(mesh_count, width, SINGLE)
    grid_rows = shape(grid_count, width, HALF)
    grid_full = shape(grid_count, width, SINGLE)
    parcel = shape(variables + -variables % 16 + INDEX_ROWS // 2, grid_count, HALF)
    sent = fetching(
        parcels, [parcel] * (GROUPS - 1), 0, grid, grid_send, mesh_send, near, limit=58
    )
    arrived = swap_all(*sent)
    embed_macs = grid_count * variables * width + mesh_count * grid_count * (step + width)
    slope_embed, total, held_weight = fetching(
        embed_own,
        [grid_full, mesh_full, shape(variables, width, HALF)],
        embed_macs,
        grid,
        embed_weight,
        grid_send,
        mesh_recv,
        limit=32,
    )
    index = [None] * GROUPS
    slopes = [slope_embed] + [None] * (GROUPS - 1)
    grids = [grid, *arrived]
    for p in (1, 3, 2, 4):
        index[p], slopes[p], total = whole(
            lambda *refs, p=p: embed_far(p, *refs),
            [shape(INDEX_ROWS, LANES, jnp.int32), grid_full, mesh_full],
            embed_macs,
            arrived[p - 1],
            held_weight,
            mesh_recv,
            total,
        )
    encode_in, slope_encode, state, half, on, off = whole(
        encode,
        [mesh_rows, mesh_full, mesh_full, mesh_rows] + [shape(rim, width, HALF)] * 2,
        mesh_count * width * width,
        total,
        encode_weight,
        mesh_static,
    )
    off = swap_off(off)
    on = swap_on(on)
    counts, turned = whole(
        near_counts, [shape(ext, ext, HALF)] * 2, ext * ext * 64, near, index[1], index[2]
    )
    count_macs = nodes * grid_count * step
    (to_grid,) = whole(
        lambda *refs: grid_counts(False, *refs),
        [shape(grid_count, nodes, HALF)],
        count_macs,
        mesh_send,
        grid_recv,
        *index[1:],
    )
    state, to_grid = lax.optimization_barrier((state, to_grid))
    final_half, pre_0, pre_1, half_1, nearby_0, nearby_1 = whole(
        process,
        [mesh_rows, shape(ext - rim, width, SINGLE), mesh_full] + [mesh_rows] * 3,
        (ext + mesh_count) * (ext + 2 * width) * width,
        half,
        state,
        on,
        off,
        counts,
        self_weight,
        neighbor_weight,
        scratch=[pltpu.VMEM((ext, width), HALF)],
    )
    moved = swap_all(*[final_half] * 4)
    finals = [final_half] + [moved[p - 1] for p in (4, 3, 2, 1)]
    (from_grid,) = whole(
        lambda *refs: grid_counts(True, *refs),
        [shape(nodes, grid_count, HALF)],
        count_macs,
        lax.optimization_barrier((mesh_send, final_half))[0],
        grid_recv,
        *index[1:],
    )
    hidden_grad = outer_sum(cot, out_weight)
    decode_in, hidden, decode_grad, state_grad, *sums = whole(
        decode,
        [grid_rows] * 3 + [mesh_full] + [mesh_rows] * (GROUPS - 1),
        2 * grid_count * width * (nodes + width),
        *finals,
        to_grid,
        from_grid,
        decode_weight,
        hidden_grad,
    )
    moved = swap_all(*sums)
    arrived = [moved[p - 1] for p in (1, 2, 3, 4)]
    prediction = (grid.astype(SINGLE) + back_mul(out_weight, hidden)).astype(HALF)
    half_rows = split_rows(width)
    narrow_rows = split_rows(variables)
    square = width * width
    decode_halves = split_gradients(
        lambda *refs: gradient_halves(1, *refs),
        narrow_rows + half_rows,
        width,
        2 * grid_count * square,
        cot,
        hidden,
        decode_in,
        decode_grad,
    )
    to_mesh = whole(
        mesh_counts,
        [shape(grid_count, nodes, HALF)],
        count_macs,
        lax.optimization_barrier((grid_send, decode_in))[0],
        mesh_recv,
        *index[1:],
    )[0]
    state_grad, to_mesh, *decode_halves = lax.optimization_barrier(
        (state_grad, to_mesh, *decode_halves)
    )
    state_grad, layer_1, on, off = whole(
        gather_back,
        [mesh_full, mesh_rows] + [shape(rim + RIM, width, HALF)] * 2,
        0,
        state_grad,
        *arrived,
        silu_slope(pre_1),
    )
    off = swap_off(off)
    on = swap_on(on)
    layer_halves = split_gradients(
        lambda *refs: gradient_halves(0, *refs),
        2 * half_rows,
        width,
        2 * mesh_count * square,
        half_1,
        layer_1,
        nearby_1,
        layer_1,
    )
    halves = [decode_halves[0], swap_on(decode_halves[1])]
    state_grad, *layer_halves, halves[1] = lax.optimization_barrier(
        (state_grad, *layer_halves, halves[1])
    )
    state_grad, layer_0, encode_grad, encode_in_grad = whole(
        process_back,
        [mesh_full, mesh_rows, mesh_rows, mesh_rows],
        (ext + mesh_count) * (ext + 2 * width) * width,
        state_grad,
        layer_1,
        on,
        off,
        turned,
        silu_slope(pre_0),
        slope_encode,
        self_weight,
        neighbor_weight,
        encode_weight,
        scratch=[pltpu.VMEM((ext, width), HALF)],
    )
    rest_halves = split_gradients(
        lambda *refs: gradient_halves(0, *refs),
        3 * half_rows,
        width,
        3 * mesh_count * square,
        half,
        layer_0,
        nearby_0,
        layer_0,
        encode_in,
        encode_grad,
    )
    embed_halves = split_gradients(
        embed_back,
        narrow_rows,
        width,
        grid_count * width * (nodes + GROUPS * variables),
        encode_in_grad,
        to_mesh,
        *slopes,
        *grids,
    )
    for mine, other in (layer_halves, rest_halves, embed_halves):
        halves += [mine, swap_on(other)]
    rows = sum(block.shape[0] for block in halves[::2])
    (part,) = whole(add_halves, [shape(rows, width, HALF)], 0, *halves)
    part = reduce_all(part)
    other = swap_on(part)
    grad_encode, grad_self, grad_near, grad_decode, grad_embed, grad_output = unpack(
        part, other, width, variables
    )
    return (
        prediction.T,
        state_grad,
        grad_embed,
        grad_encode,
        grad_self,
        grad_near,
        grad_decode,
        grad_output.T,
    )


def solution(mesh):
    placed = (
        P(("band", "dom"), None),
        P(("band", "dom"), None),
        P(("band", "dom"), None),
        P(),
        P(),
        P(),
        P(),
        P(),
        P(),
        P(("band", "dom")),
        P(("band", "dom")),
        P(("band", "dom"), None),
        P(("band", "dom")),
        P(("band", "dom")),
    )
    return jax.shard_map(
        shards,
        mesh=mesh,
        in_specs=placed,
        out_specs=(
            P(("band", "dom"), None),
            P(("band", "dom"), None),
            P(),
            P(),
            P(),
            P(),
            P(),
            P(),
        ),
        check_vma=False,
    )
```

```python
import jax
import jax.numpy as jnp
from jax import lax
from jax.experimental import pallas as pl
from jax.experimental.pallas import tpu as pltpu
from jax.sharding import PartitionSpec as P

NEAR = 6
RIM = 64
GROUPS = 5
LANES = 128
HALF = jnp.bfloat16
SINGLE = jnp.float32
MIB = 1024 * 1024
SLOT_ROWS = 6
INDEX_ROWS = 32


def silu_slope(values):
    sigma = jax.nn.sigmoid(values)
    return sigma * (1.0 + values * (1.0 - sigma))


def matmul(left, right):
    return jnp.dot(left, right, preferred_element_type=SINGLE)


def outer_sum(left, right):
    return lax.dot_general(
        left, right, (((0,), (0,)), ((), ())), preferred_element_type=SINGLE
    )


def back_mul(left, right):
    return lax.dot_general(
        left, right, (((1,), (1,)), ((), ())), preferred_element_type=SINGLE
    )


def swap_on(value):
    count = lax.axis_size("dom")
    return lax.ppermute(value, "dom", [(i, i ^ 1) for i in range(count)])


def swap_off(value):
    count = lax.axis_size("dom")
    return lax.ppermute(
        value, "dom", [(i, (i + (1 if i % 2 else -1)) % count) for i in range(count)]
    )


def swap_band(value, first):
    count = lax.axis_size("band")
    pairs = []
    for low in range(first, count - 1, 2):
        pairs += [(low, low + 1), (low + 1, low)]
    return lax.ppermute(value, "band", pairs)


def swap_all(on, off, north, south):
    south = swap_band(south, 1)
    north = swap_band(north, 0)
    off = swap_off(off)
    return swap_on(on), off, north, south


def by_partner(slots, odd_dom, odd_band, incoming):
    flip_dom = odd_dom != incoming
    flip_band = odd_band != incoming
    return [
        slots[0],
        jnp.where(flip_dom, slots[2], slots[1]),
        jnp.where(flip_dom, slots[1], slots[2]),
        jnp.where(flip_band, slots[4], slots[3]),
        jnp.where(flip_band, slots[3], slots[4]),
    ]


def whole(body, outs, macs, *args, limit=32, scratch=()):
    moved = sum(a.size * a.dtype.itemsize for a in (*args, *outs))
    return pl.pallas_call(
        body,
        out_shape=outs,
        scratch_shapes=scratch,
        compiler_params=pltpu.CompilerParams(vmem_limit_bytes=limit * MIB),
        cost_estimate=pl.CostEstimate(flops=2 * macs, bytes_accessed=moved, transcendentals=0),
    )(*args)


def shape(rows, columns, kind):
    return jax.ShapeDtypeStruct((rows, columns), kind)


def odd_along(axis):
    return lax.axis_index(axis) % 2 == 1


def hot(rows, index):
    spots = lax.broadcasted_iota(jnp.int32, (rows, LANES), 0)
    one = [
        jnp.where(spots == index[j : j + 1], 1.0, 0.0).astype(HALF) for j in range(index.shape[0])
    ]
    return jnp.concatenate(one, 1)


def pair_counts(rows, row_count, columns, column_count):
    return back_mul(hot(row_count, rows), hot(column_count, columns)).astype(HALF)


def slots_of(index):
    step = index.shape[0] // GROUPS
    return [index[k * step : (k + 1) * step] for k in range(GROUPS)]


def fetch(sources, buffers, sems):
    copies = [
        pltpu.make_async_copy(source, buffer, sems.at[i])
        for i, (source, buffer) in enumerate(zip(sources, buffers, strict=True))
    ]
    for copy in copies:
        copy.start()
    for copy in copies:
        copy.wait()


def fetching(body, outs, macs, *args, limit):
    moved = sum(a.size * a.dtype.itemsize for a in (*args, *outs))
    return pl.pallas_call(
        body,
        out_shape=outs,
        in_specs=[pl.BlockSpec(memory_space=pltpu.HBM)] * len(args),
        scratch_shapes=[pltpu.VMEM(a.shape, a.dtype) for a in args]
        + [pltpu.SemaphoreType.DMA((len(args),))],
        compiler_params=pltpu.CompilerParams(vmem_limit_bytes=limit * MIB),
        cost_estimate=pl.CostEstimate(flops=2 * macs, bytes_accessed=moved, transcendentals=0),
    )(*[pltpu.with_memory_space_constraint(a, pltpu.HBM) for a in args])


def parcels(*refs):
    inputs, rest = refs[:4], refs[4:]
    outs, buffers, sems = rest[: GROUPS - 1], rest[GROUPS - 1 : -1], rest[-1]
    fetch(inputs, buffers, sems)
    grid_ref, grid_send_ref, mesh_send_ref, near_ref = buffers
    odd_dom, odd_band = odd_along("dom"), odd_along("band")
    grid_send = by_partner(slots_of(grid_send_ref[...]), odd_dom, odd_band, False)
    mesh_send = by_partner(slots_of(mesh_send_ref[...]), odd_dom, odd_band, False)
    near = near_ref[...]
    near = [near[:, j : j + LANES] for j in range(0, near.shape[1], LANES)]
    variables, count = grid_ref.shape
    first = outs[0].shape[0] - INDEX_ROWS // 2
    grid = grid_ref[...]
    for p, out in enumerate(outs):
        parts = [mesh_send[p + 1], grid_send[p + 1], *near]
        used = sum(part.shape[0] for part in parts)
        parts.append(jnp.zeros((INDEX_ROWS - used, LANES), jnp.int32))
        index = jnp.concatenate(parts, 0)
        high = (index >> 1).astype(SINGLE)
        low = (index & 1).astype(SINGLE)
        cut = INDEX_ROWS // 2
        out[:variables] = grid
        out[variables:first] = jnp.zeros((first - variables, count), HALF)
        out[first:] = jnp.concatenate([high[:cut], low[:cut], high[cut:], low[cut:]], 1).astype(HALF)


def index_of(packed):
    packed = packed.astype(SINGLE)
    halves = [
        packed[:, j : j + LANES] * 2.0 + packed[:, j + LANES : j + 2 * LANES]
        for j in (0, 2 * LANES)
    ]
    return jnp.concatenate(halves, 0).astype(jnp.int32)


def embed_own(*refs):
    inputs, (slope_ref, sum_ref, held_ref), buffers, sems = refs[:4], refs[4:7], refs[7:-1], refs[-1]
    fetch(inputs, buffers, sems)
    grid_ref, weight_ref, send_ref, recv_ref = buffers
    step = send_ref.shape[0] // GROUPS
    counts = pair_counts(
        recv_ref[:step], sum_ref.shape[0], send_ref[:step], grid_ref.shape[1]
    )
    pre = outer_sum(grid_ref[...], weight_ref[...])
    sigma = jax.nn.sigmoid(pre)
    slope_ref[...] = sigma * (1.0 + pre * (1.0 - sigma))
    sum_ref[...] = matmul(counts, (pre * sigma).astype(HALF))
    held_ref[...] = weight_ref[...]


def embed_far(p, parcel_ref, weight_ref, recv_ref, sum_ref, index_ref, slope_ref, out_ref):
    index = index_of(parcel_ref[parcel_ref.shape[0] - INDEX_ROWS // 2 :])
    index_ref[...] = index
    step = recv_ref.shape[0] // GROUPS
    recv = by_partner(slots_of(recv_ref[...]), odd_along("dom"), odd_along("band"), True)[p]
    counts = pair_counts(
        recv, out_ref.shape[0], index[step : 2 * step], parcel_ref.shape[1]
    )
    pre = outer_sum(parcel_ref[: weight_ref.shape[0]], weight_ref[...])
    sigma = jax.nn.sigmoid(pre)
    slope_ref[...] = sigma * (1.0 + pre * (1.0 - sigma))
    out_ref[...] = sum_ref[...] + matmul(counts, (pre * sigma).astype(HALF))


def encode(sum_ref, weight_ref, static_ref, in_ref, slope_ref, state_ref, half_ref, on_ref, off_ref):
    encode_in = sum_ref[...].astype(HALF)
    pre = matmul(encode_in, weight_ref[...])
    sigma = jax.nn.sigmoid(pre)
    state = static_ref[...].astype(SINGLE) + pre * sigma
    half = state.astype(HALF)
    in_ref[...] = encode_in
    slope_ref[...] = sigma * (1.0 + pre * (1.0 - sigma))
    state_ref[...] = state
    half_ref[...] = half
    rows = on_ref.shape[0]
    odd = odd_along("dom")
    head, tail = half[:rows], half[half.shape[0] - rows :]
    on_ref[...] = jnp.where(odd, head, tail)
    off_ref[...] = jnp.where(odd, tail, head)


def near_counts(near_ref, on_ref, off_ref, out_ref, turned_ref):
    step = near_ref.shape[0]
    mesh_count = near_ref.shape[1]
    first = 2 * SLOT_ROWS
    odd_dom = odd_along("dom")
    on, off = on_ref[...], off_ref[...]
    left = jnp.where(odd_dom, on, off)[first + step : first + 2 * step] + (RIM - mesh_count)
    right = jnp.where(odd_dom, off, on)[first : first + step] + (RIM + mesh_count)
    own = near_ref[...] + RIM
    index = jnp.concatenate([left, own, right], 1)
    spots = lax.broadcasted_iota(jnp.int32, out_ref.shape, 0)
    counts = jnp.zeros(out_ref.shape, SINGLE)
    for j in range(step):
        counts = counts + jnp.where(spots == index[j : j + 1], 1.0, 0.0)
    turned_ref[...] = counts.astype(HALF)
    out_ref[...] = counts.T.astype(HALF)


def process(
    half_ref, state_ref, on_ref, off_ref, counts_ref, self_ref, near_ref,
    final_ref, pre_0_ref, pre_1_ref, half_1_ref, nearby_0_ref, nearby_1_ref, whole_ref,
):
    rim = on_ref.shape[0]
    count = half_ref.shape[0]
    own = slice(rim, rim + count)
    odd = odd_along("dom")
    left = jnp.where(odd, on_ref[...], off_ref[...])
    right = jnp.where(odd, off_ref[...], on_ref[...])
    whole_ref[:rim] = left
    whole_ref[own] = half_ref[...]
    whole_ref[rim + count :] = right
    half_0 = whole_ref[...]
    used = slice(RIM, 3 * RIM + count)
    nearby_0 = (matmul(counts_ref[used], half_0) * (1.0 / NEAR)).astype(HALF)
    nearby_0_ref[...] = nearby_0[RIM : RIM + count]
    pre_0 = matmul(half_0[used], self_ref[0]) + matmul(nearby_0, near_ref[0])
    pre_0_ref[...] = pre_0
    grown = pre_0 * jax.nn.sigmoid(pre_0)
    state_1 = state_ref[...] + grown[RIM : RIM + count]
    half_1 = state_1.astype(HALF)
    whole_ref[RIM:rim] = (left[RIM:].astype(SINGLE) + grown[:RIM]).astype(HALF)
    whole_ref[own] = half_1
    whole_ref[rim + count : rim + count + RIM] = (
        right[:RIM].astype(SINGLE) + grown[RIM + count :]
    ).astype(HALF)
    half_1_ref[...] = half_1
    nearby_1 = (matmul(counts_ref[own], whole_ref[...]) * (1.0 / NEAR)).astype(HALF)
    nearby_1_ref[...] = nearby_1
    pre_1 = matmul(half_1, self_ref[1]) + matmul(nearby_1, near_ref[1])
    pre_1_ref[...] = pre_1
    final_ref[...] = (state_1 + pre_1 * jax.nn.sigmoid(pre_1)).astype(HALF)


def grid_counts(turned, send_ref, recv_ref, *refs):
    far, out_ref = refs[: GROUPS - 1], refs[GROUPS - 1]
    odd_dom, odd_band = odd_along("dom"), odd_along("band")
    step = send_ref.shape[0] // GROUPS
    recv = by_partner(slots_of(recv_ref[...]), odd_dom, odd_band, True)
    send = [send_ref[:step]] + [ref[:step] for ref in far]
    nodes = out_ref.shape[0 if turned else 1] // GROUPS
    grids = out_ref.shape[1 if turned else 0]
    for p in range(GROUPS):
        at = slice(p * nodes, (p + 1) * nodes)
        if turned:
            out_ref[at] = pair_counts(send[p], nodes, recv[p], grids)
        else:
            out_ref[:, at] = pair_counts(recv[p], grids, send[p], nodes)


def mesh_counts(send_ref, recv_ref, *refs):
    far, out_ref = refs[: GROUPS - 1], refs[GROUPS - 1]
    step = send_ref.shape[0] // GROUPS
    send = [send_ref[:step]] + [ref[step : 2 * step] for ref in far]
    recv = by_partner(slots_of(recv_ref[...]), odd_along("dom"), odd_along("band"), True)
    grids, nodes = out_ref.shape[0], out_ref.shape[1] // GROUPS
    for p in range(GROUPS):
        out_ref[:, p * nodes : (p + 1) * nodes] = pair_counts(send[p], grids, recv[p], nodes)


def decode(*refs):
    finals = [refs[i] for i in (0, 4, 3, 2, 1)]
    counts_ref, turned_ref, weight_ref, back_ref = refs[GROUPS : GROUPS + 4]
    in_ref, hidden_ref, grad_ref, own_ref, *outs = refs[GROUPS + 4 :]
    nodes = own_ref.shape[0]
    total = matmul(counts_ref[:, :nodes], finals[0][...])
    for p in range(1, GROUPS):
        total = total + matmul(counts_ref[:, p * nodes : (p + 1) * nodes], finals[p][...])
    decode_in = total.astype(HALF)
    in_ref[...] = decode_in
    pre = matmul(decode_in, weight_ref[...])
    sigma = jax.nn.sigmoid(pre)
    hidden_ref[...] = (pre * sigma).astype(HALF)
    grad = (back_ref[...] * (sigma * (1.0 + pre * (1.0 - sigma)))).astype(HALF)
    grad_ref[...] = grad
    in_grad = back_mul(grad, weight_ref[...]).astype(HALF)
    own_ref[...] = matmul(turned_ref[:nodes], in_grad)
    for p, out in enumerate(outs):
        out[...] = matmul(turned_ref[(p + 1) * nodes : (p + 2) * nodes], in_grad).astype(HALF)


def gather_back(*refs):
    total = refs[0][...]
    for ref in refs[1:GROUPS]:
        total = total + ref[...].astype(SINGLE)
    slope_ref, state_ref, layer_ref, on_ref, off_ref = refs[GROUPS:]
    state_ref[...] = total
    layer = (total * slope_ref[...]).astype(HALF)
    layer_ref[...] = layer
    half = total.astype(HALF)
    odd = odd_along("dom")
    rim, count = RIM, total.shape[0]
    heads = jnp.concatenate([layer[: 2 * rim], half[:rim]], 0)
    tails = jnp.concatenate([layer[count - 2 * rim :], half[count - rim :]], 0)
    on_ref[...] = jnp.where(odd, heads, tails)
    off_ref[...] = jnp.where(odd, tails, heads)


def process_back(
    state_ref, layer_ref, on_ref, off_ref, turned_ref, slope_0_ref, slope_in_ref,
    self_ref, near_ref, encode_ref, static_ref, layer_0_ref, encode_grad_ref, back_ref, whole_ref,
):
    rim = RIM
    count = state_ref.shape[0]
    own = slice(2 * rim, 2 * rim + count)
    odd = odd_along("dom")
    on, off = on_ref[...], off_ref[...]
    left, right = jnp.where(odd, on, off), jnp.where(odd, off, on)
    whole_ref[: 2 * rim] = left[: 2 * rim]
    whole_ref[own] = layer_ref[...]
    whole_ref[2 * rim + count :] = right[: 2 * rim]
    layer_1 = whole_ref[...]
    used = slice(rim, 3 * rim + count)
    inner = slice(rim, rim + count)
    spread = (matmul(turned_ref[used], layer_1) * (1.0 / NEAR)).astype(HALF)
    back = back_mul(layer_1[used], self_ref[1]) + back_mul(spread, near_ref[1])
    state_own = state_ref[...] + back[inner]
    first = left[2 * rim :].astype(SINGLE) + back[:rim]
    last = right[2 * rim :].astype(SINGLE) + back[rim + count :]
    layer_0 = (state_own * slope_0_ref[inner]).astype(HALF)
    layer_0_ref[...] = layer_0
    whole_ref[:rim] = jnp.zeros((rim, back.shape[1]), HALF)
    whole_ref[rim : 2 * rim] = (first * slope_0_ref[:rim]).astype(HALF)
    whole_ref[own] = layer_0
    whole_ref[2 * rim + count : 3 * rim + count] = (last * slope_0_ref[rim + count :]).astype(HALF)
    whole_ref[3 * rim + count :] = jnp.zeros((rim, back.shape[1]), HALF)
    spread = (matmul(turned_ref[own], whole_ref[...]) * (1.0 / NEAR)).astype(HALF)
    state = state_own + back_mul(layer_0, self_ref[0]) + back_mul(spread, near_ref[0])
    static_ref[...] = state
    grad = (state * slope_in_ref[...]).astype(HALF)
    encode_grad_ref[...] = grad
    back_ref[...] = back_mul(grad, encode_ref[...]).astype(HALF)


def split_rows(count):
    return -(-count // (2 * LANES)) * LANES


def store_halves(value, at, mine_ref, other_ref, wide_ref):
    odd = lax.axis_index("dom") % 2
    count, rows = value.shape[0], split_rows(value.shape[0])
    wide_ref[:count] = value
    if count < 2 * rows:
        wide_ref[count : 2 * rows] = jnp.zeros((2 * rows - count, value.shape[1]), SINGLE)
    mine = pl.ds(pl.multiple_of(odd * rows, rows), rows)
    other = pl.ds(pl.multiple_of((1 - odd) * rows, rows), rows)
    mine_ref[at : at + rows] = wide_ref[mine].astype(HALF)
    other_ref[at : at + rows] = wide_ref[other].astype(HALF)
    return at + rows


def gradient_halves(turned, *refs):
    mine_ref, other_ref, wide_ref = refs[-3:]
    at = 0
    for i, (left, right) in enumerate(zip(refs[:-3:2], refs[1:-3:2], strict=True)):
        product = matmul if i < turned else outer_sum
        value = product(left[...], right[...])
        at = store_halves(value, at, mine_ref, other_ref, wide_ref)


def embed_back(*refs):
    back_ref, counts_ref = refs[:2]
    slopes, grids = refs[2 : 2 + GROUPS], refs[2 + GROUPS : 2 + 2 * GROUPS]
    mine_ref, other_ref, wide_ref = refs[2 + 2 * GROUPS :]
    nodes = back_ref.shape[0]
    variables = grids[0].shape[0]
    grads = []
    for p in range(GROUPS):
        latent = matmul(counts_ref[:, p * nodes : (p + 1) * nodes], back_ref[...])
        grads.append((latent * slopes[p][...]).astype(HALF))
    total = matmul(
        jnp.concatenate([grid[:variables] for grid in grids], 1), jnp.concatenate(grads, 0)
    )
    store_halves(total, 0, mine_ref, other_ref, wide_ref)


def split_gradients(body, rows, width, macs, *args):
    outs = [shape(rows, width, HALF)] * 2
    return whole(body, outs, macs, *args, scratch=[pltpu.VMEM((width, width), SINGLE)])


def add_halves(*refs):
    out_ref = refs[-1]
    at = 0
    for mine, other in zip(refs[:-1:2], refs[1:-1:2], strict=True):
        rows = mine.shape[0]
        out_ref[at : at + rows] = (
            mine[...].astype(SINGLE) + other[...].astype(SINGLE)
        ).astype(HALF)
        at += rows


def add_pieces(pieces_ref, out_ref):
    total = pieces_ref[0].astype(SINGLE)
    for i in range(1, pieces_ref.shape[0]):
        total = total + pieces_ref[i].astype(SINGLE)
    out_ref[...] = total.astype(HALF)


def add_bands(*refs):
    out_ref = refs[-1]
    total = refs[0][...].astype(SINGLE)
    for ref in refs[1:-1]:
        total = total + ref[...].astype(SINGLE)
    total = total.astype(HALF)
    for i in range(out_ref.shape[0]):
        out_ref[i] = total


def places(outs):
    encode, self_, near, decode = outs
    return [(decode, None), (self_, 1), (near, 1), (self_, 0), (near, 0), (encode, None)]


def store_squares(first, half, value_ref, outs, buffer_ref, sems):
    rows = outs[0].shape[0] // 2
    spot = pl.ds(pl.multiple_of(half * rows, rows), rows)
    copies = []
    for i, (out, which) in enumerate(places(outs)):
        at = i * rows
        buffer_ref[at : at + rows] = value_ref[first + at : first + at + rows].astype(SINGLE)
        target = out.at[spot] if which is None else out.at[which, spot]
        copies.append(
            pltpu.make_async_copy(buffer_ref.at[at : at + rows], target, sems.at[i])
        )
        copies[-1].start()
    return copies


def unpack_own(part_ref, *refs):
    outs, (buffer_ref, sems) = refs[:4], refs[4:]
    first = (part_ref.shape[0] - buffer_ref.shape[0]) // 2
    half = lax.axis_index("dom") % 2
    for copy in store_squares(first, half, part_ref, outs, buffer_ref, sems):
        copy.wait()


def unpack_other(part_ref, other_ref, *refs):
    outs, narrow, (buffer_ref, sems, *held) = refs[4:8], refs[8:10], refs[10:]
    rows = (part_ref.shape[0] - buffer_ref.shape[0]) // 2
    half = lax.axis_index("dom") % 2
    copies = []
    odd = odd_along("dom")
    for i, at in enumerate((part_ref.shape[0] - rows, 0)):
        own = part_ref[at : at + rows].astype(SINGLE)
        far = other_ref[at : at + rows].astype(SINGLE)
        held[i][:rows] = jnp.where(odd, far, own)
        held[i][rows:] = jnp.where(odd, own, far)[: held[i].shape[0] - rows]
        copies.append(pltpu.make_async_copy(held[i], narrow[i], sems.at[6 + i]))
        copies[-1].start()
    copies += store_squares(rows, 1 - half, other_ref, outs, buffer_ref, sems)
    for copy in copies:
        copy.wait()


def unpack(part, other, width, variables):
    full = shape(width, width, SINGLE)
    pair = jax.ShapeDtypeStruct((2, width, width), SINGLE)
    narrow = shape(variables, width, SINGLE)
    squares = [full, pair, pair, full]
    hbm = pl.BlockSpec(memory_space=pltpu.HBM)
    vmem = pl.BlockSpec(memory_space=pltpu.VMEM)
    scratch = [
        pltpu.VMEM((6 * split_rows(width), width), SINGLE),
        pltpu.SemaphoreType.DMA((8,)),
    ]
    params = pltpu.CompilerParams(vmem_limit_bytes=32 * MIB)
    size = part.size * 6
    cost = pl.CostEstimate(flops=0, bytes_accessed=size, transcendentals=0)
    grads = pl.pallas_call(
        unpack_own,
        out_shape=squares,
        in_specs=[vmem],
        out_specs=[hbm] * 4,
        scratch_shapes=scratch,
        compiler_params=params,
        cost_estimate=cost,
    )(part)
    return pl.pallas_call(
        unpack_other,
        out_shape=[*squares, narrow, narrow],
        in_specs=[vmem, vmem] + [hbm] * 4,
        out_specs=[hbm] * 6,
        input_output_aliases={2: 0, 3: 1, 4: 2, 5: 3},
        scratch_shapes=scratch + [pltpu.VMEM((variables, width), SINGLE)] * 2,
        compiler_params=params,
        cost_estimate=cost,
    )(part, other, *grads)


def reduce_all(part):
    count = lax.axis_size("dom")
    bands = lax.axis_size("band")
    groups = [list(range(c, count, 2)) for c in range(2)]
    chips = count // 2
    rows, width = part.shape[0] // chips, part.shape[1]
    pieces = lax.all_to_all(
        part.reshape(chips, rows, width), "dom", 0, 0, axis_index_groups=groups
    )
    (piece,) = whole(add_pieces, [shape(rows, width, HALF)], 0, pieces)
    others = [
        lax.ppermute(piece, "band", [(i, (i + step) % bands) for i in range(bands)])
        for step in range(1, bands)
    ]
    copies = jax.ShapeDtypeStruct((chips, rows, width), HALF)
    (copies,) = whole(add_bands, [copies], 0, piece, *others)
    return lax.all_to_all(copies, "dom", 0, 0, axis_index_groups=groups).reshape(part.shape)


def shards(
    grid_vars,
    cotangent,
    mesh_static,
    embed_weight,
    encode_weight,
    self_weight,
    neighbor_weight,
    decode_weight,
    output_weight,
    grid_sender,
    mesh_receiver,
    neighbors,
    mesh_sender,
    grid_receiver,
):
    grid_count, variables = grid_vars.shape
    mesh_count, width = mesh_static.shape
    rim = 2 * RIM
    ext = mesh_count + 2 * rim
    grid, cot, near, out_weight = grid_vars.T, cotangent.T, neighbors.T, output_weight.T
    grid_send, mesh_recv, mesh_send, grid_recv = (
        index.reshape(-1, LANES) for index in (grid_sender, mesh_receiver, mesh_sender, grid_receiver)
    )
    step = grid_send.shape[0] // GROUPS * LANES
    nodes = GROUPS * mesh_count
    mesh_rows = shape(mesh_count, width, HALF)
    mesh_full = shape(mesh_count, width, SINGLE)
    grid_rows = shape(grid_count, width, HALF)
    grid_full = shape(grid_count, width, SINGLE)
    parcel = shape(variables + -variables % 16 + INDEX_ROWS // 2, grid_count, HALF)
    sent = fetching(
        parcels, [parcel] * (GROUPS - 1), 0, grid, grid_send, mesh_send, near, limit=32
    )
    arrived = swap_all(*sent)
    embed_macs = grid_count * variables * width + mesh_count * grid_count * (step + width)
    slope_embed, total, held_weight = fetching(
        embed_own,
        [grid_full, mesh_full, shape(variables, width, HALF)],
        embed_macs,
        grid,
        embed_weight,
        grid_send,
        mesh_recv,
        limit=32,
    )
    index = [None] * GROUPS
    slopes = [slope_embed] + [None] * (GROUPS - 1)
    grids = [grid, *arrived]
    for p in (1, 3, 2, 4):
        index[p], slopes[p], total = whole(
            lambda *refs, p=p: embed_far(p, *refs),
            [shape(INDEX_ROWS, LANES, jnp.int32), grid_full, mesh_full],
            embed_macs,
            arrived[p - 1],
            held_weight,
            mesh_recv,
            total,
        )
    encode_in, slope_encode, state, half, on, off = whole(
        encode,
        [mesh_rows, mesh_full, mesh_full, mesh_rows] + [shape(rim, width, HALF)] * 2,
        mesh_count * width * width,
        total,
        encode_weight,
        mesh_static,
    )
    off = swap_off(off)
    on = swap_on(on)
    counts, turned = whole(
        near_counts, [shape(ext, ext, HALF)] * 2, ext * ext * 64, near, index[1], index[2]
    )
    count_macs = nodes * grid_count * step
    (to_grid,) = whole(
        lambda *refs: grid_counts(False, *refs),
        [shape(grid_count, nodes, HALF)],
        count_macs,
        mesh_send,
        grid_recv,
        *index[1:],
    )
    state, to_grid = lax.optimization_barrier((state, to_grid))
    final_half, pre_0, pre_1, half_1, nearby_0, nearby_1 = whole(
        process,
        [mesh_rows, shape(ext - rim, width, SINGLE), mesh_full] + [mesh_rows] * 3,
        (ext + mesh_count) * (ext + 2 * width) * width,
        half,
        state,
        on,
        off,
        counts,
        self_weight,
        neighbor_weight,
        scratch=[pltpu.VMEM((ext, width), HALF)],
    )
    moved = swap_all(*[final_half] * 4)
    finals = [final_half] + [moved[p - 1] for p in (4, 3, 2, 1)]
    (from_grid,) = whole(
        lambda *refs: grid_counts(True, *refs),
        [shape(nodes, grid_count, HALF)],
        count_macs,
        lax.optimization_barrier((mesh_send, final_half))[0],
        grid_recv,
        *index[1:],
    )
    hidden_grad = outer_sum(cot, out_weight)
    decode_in, hidden, decode_grad, state_grad, *sums = whole(
        decode,
        [grid_rows] * 3 + [mesh_full] + [mesh_rows] * (GROUPS - 1),
        2 * grid_count * width * (nodes + width),
        *finals,
        to_grid,
        from_grid,
        decode_weight,
        hidden_grad,
    )
    moved = swap_all(*sums)
    arrived = [moved[p - 1] for p in (1, 2, 3, 4)]
    prediction = (grid.astype(SINGLE) + back_mul(out_weight, hidden)).astype(HALF)
    half_rows = split_rows(width)
    narrow_rows = split_rows(variables)
    square = width * width
    decode_halves = split_gradients(
        lambda *refs: gradient_halves(1, *refs),
        narrow_rows + half_rows,
        width,
        2 * grid_count * square,
        cot,
        hidden,
        decode_in,
        decode_grad,
    )
    to_mesh = whole(
        mesh_counts,
        [shape(grid_count, nodes, HALF)],
        count_macs,
        lax.optimization_barrier((grid_send, decode_in))[0],
        mesh_recv,
        *index[1:],
    )[0]
    state_grad, to_mesh, *decode_halves = lax.optimization_barrier(
        (state_grad, to_mesh, *decode_halves)
    )
    state_grad, layer_1, on, off = whole(
        gather_back,
        [mesh_full, mesh_rows] + [shape(rim + RIM, width, HALF)] * 2,
        0,
        state_grad,
        *arrived,
        silu_slope(pre_1),
    )
    off = swap_off(off)
    on = swap_on(on)
    layer_halves = split_gradients(
        lambda *refs: gradient_halves(0, *refs),
        2 * half_rows,
        width,
        2 * mesh_count * square,
        half_1,
        layer_1,
        nearby_1,
        layer_1,
    )
    halves = [decode_halves[0], swap_on(decode_halves[1])]
    state_grad, *layer_halves, halves[1] = lax.optimization_barrier(
        (state_grad, *layer_halves, halves[1])
    )
    state_grad, layer_0, encode_grad, encode_in_grad = whole(
        process_back,
        [mesh_full, mesh_rows, mesh_rows, mesh_rows],
        (ext + mesh_count) * (ext + 2 * width) * width,
        state_grad,
        layer_1,
        on,
        off,
        turned,
        silu_slope(pre_0),
        slope_encode,
        self_weight,
        neighbor_weight,
        encode_weight,
        scratch=[pltpu.VMEM((ext, width), HALF)],
    )
    rest_halves = split_gradients(
        lambda *refs: gradient_halves(0, *refs),
        3 * half_rows,
        width,
        3 * mesh_count * square,
        half,
        layer_0,
        nearby_0,
        layer_0,
        encode_in,
        encode_grad,
    )
    embed_halves = split_gradients(
        embed_back,
        narrow_rows,
        width,
        grid_count * width * (nodes + GROUPS * variables),
        encode_in_grad,
        to_mesh,
        *slopes,
        *grids,
    )
    for mine, other in (layer_halves, rest_halves, embed_halves):
        halves += [mine, swap_on(other)]
    rows = sum(block.shape[0] for block in halves[::2])
    (part,) = whole(add_halves, [shape(rows, width, HALF)], 0, *halves)
    part = reduce_all(part)
    other = swap_on(part)
    grad_encode, grad_self, grad_near, grad_decode, grad_embed, grad_output = unpack(
        part, other, width, variables
    )
    return (
        prediction.T,
        state_grad,
        grad_embed,
        grad_encode,
        grad_self,
        grad_near,
        grad_decode,
        grad_output.T,
    )


def solution(mesh):
    placed = (
        P(("band", "dom"), None),
        P(("band", "dom"), None),
        P(("band", "dom"), None),
        P(),
        P(),
        P(),
        P(),
        P(),
        P(),
        P(("band", "dom")),
        P(("band", "dom")),
        P(("band", "dom"), None),
        P(("band", "dom")),
        P(("band", "dom")),
    )
    return jax.shard_map(
        shards,
        mesh=mesh,
        in_specs=placed,
        out_specs=(
            P(("band", "dom"), None),
            P(("band", "dom"), None),
            P(),
            P(),
            P(),
            P(),
            P(),
            P(),
        ),
        check_vma=False,
    )
```

```python
import jax
import jax.numpy as jnp
from jax import lax
from jax.experimental import pallas as pl
from jax.experimental.pallas import tpu as pltpu
from jax.sharding import PartitionSpec as P

NEAR = 6
RIM = 64
GROUPS = 5
LANES = 128
HALF = jnp.bfloat16
SINGLE = jnp.float32
MIB = 1024 * 1024
SLOT_ROWS = 6
INDEX_ROWS = 32


def silu_slope(values):
    sigma = jax.nn.sigmoid(values)
    return sigma * (1.0 + values * (1.0 - sigma))


def matmul(left, right):
    return jnp.dot(left, right, preferred_element_type=SINGLE)


def outer_sum(left, right):
    return lax.dot_general(
        left, right, (((0,), (0,)), ((), ())), preferred_element_type=SINGLE
    )


def back_mul(left, right):
    return lax.dot_general(
        left, right, (((1,), (1,)), ((), ())), preferred_element_type=SINGLE
    )


def swap_on(value):
    count = lax.axis_size("dom")
    return lax.ppermute(value, "dom", [(i, i ^ 1) for i in range(count)])


def swap_off(value):
    count = lax.axis_size("dom")
    return lax.ppermute(
        value, "dom", [(i, (i + (1 if i % 2 else -1)) % count) for i in range(count)]
    )


def swap_band(value, first):
    count = lax.axis_size("band")
    pairs = []
    for low in range(first, count - 1, 2):
        pairs += [(low, low + 1), (low + 1, low)]
    return lax.ppermute(value, "band", pairs)


def swap_all(on, off, north, south):
    south = swap_band(south, 1)
    north = swap_band(north, 0)
    off = swap_off(off)
    return swap_on(on), off, north, south


def by_partner(slots, odd_dom, odd_band, incoming):
    flip_dom = odd_dom != incoming
    flip_band = odd_band != incoming
    return [
        slots[0],
        jnp.where(flip_dom, slots[2], slots[1]),
        jnp.where(flip_dom, slots[1], slots[2]),
        jnp.where(flip_band, slots[4], slots[3]),
        jnp.where(flip_band, slots[3], slots[4]),
    ]


def whole(body, outs, macs, *args, limit=32, scratch=()):
    moved = sum(a.size * a.dtype.itemsize for a in (*args, *outs))
    return pl.pallas_call(
        body,
        out_shape=outs,
        scratch_shapes=scratch,
        compiler_params=pltpu.CompilerParams(vmem_limit_bytes=limit * MIB),
        cost_estimate=pl.CostEstimate(flops=2 * macs, bytes_accessed=moved, transcendentals=0),
    )(*args)


def shape(rows, columns, kind):
    return jax.ShapeDtypeStruct((rows, columns), kind)


def odd_along(axis):
    return lax.axis_index(axis) % 2 == 1


def hot(rows, index):
    spots = lax.broadcasted_iota(jnp.int32, (rows, LANES), 0)
    one = [
        jnp.where(spots == index[j : j + 1], 1.0, 0.0).astype(HALF) for j in range(index.shape[0])
    ]
    return jnp.concatenate(one, 1)


def pair_counts(rows, row_count, columns, column_count):
    return back_mul(hot(row_count, rows), hot(column_count, columns)).astype(HALF)


def slots_of(index):
    step = index.shape[0] // GROUPS
    return [index[k * step : (k + 1) * step] for k in range(GROUPS)]


def fetch(sources, buffers, sems):
    copies = [
        pltpu.make_async_copy(source, buffer, sems.at[i])
        for i, (source, buffer) in enumerate(zip(sources, buffers, strict=True))
    ]
    for copy in copies:
        copy.start()
    for copy in copies:
        copy.wait()


def fetching(body, outs, macs, *args, limit):
    moved = sum(a.size * a.dtype.itemsize for a in (*args, *outs))
    return pl.pallas_call(
        body,
        out_shape=outs,
        in_specs=[pl.BlockSpec(memory_space=pltpu.HBM)] * len(args),
        scratch_shapes=[pltpu.VMEM(a.shape, a.dtype) for a in args]
        + [pltpu.SemaphoreType.DMA((len(args),))],
        compiler_params=pltpu.CompilerParams(vmem_limit_bytes=limit * MIB),
        cost_estimate=pl.CostEstimate(flops=2 * macs, bytes_accessed=moved, transcendentals=0),
    )(*[pltpu.with_memory_space_constraint(a, pltpu.HBM) for a in args])


def parcels(*refs):
    inputs, rest = refs[:4], refs[4:]
    outs, buffers, sems = rest[: GROUPS - 1], rest[GROUPS - 1 : -1], rest[-1]
    fetch(inputs, buffers, sems)
    grid_ref, grid_send_ref, mesh_send_ref, near_ref = buffers
    odd_dom, odd_band = odd_along("dom"), odd_along("band")
    grid_send = by_partner(slots_of(grid_send_ref[...]), odd_dom, odd_band, False)
    mesh_send = by_partner(slots_of(mesh_send_ref[...]), odd_dom, odd_band, False)
    near = near_ref[...]
    near = [near[:, j : j + LANES] for j in range(0, near.shape[1], LANES)]
    variables, count = grid_ref.shape
    first = outs[0].shape[0] - INDEX_ROWS // 2
    grid = grid_ref[...]
    for p, out in enumerate(outs):
        parts = [mesh_send[p + 1], grid_send[p + 1], *near]
        used = sum(part.shape[0] for part in parts)
        parts.append(jnp.zeros((INDEX_ROWS - used, LANES), jnp.int32))
        index = jnp.concatenate(parts, 0)
        high = (index >> 1).astype(SINGLE)
        low = (index & 1).astype(SINGLE)
        cut = INDEX_ROWS // 2
        out[:variables] = grid
        out[variables:first] = jnp.zeros((first - variables, count), HALF)
        out[first:] = jnp.concatenate([high[:cut], low[:cut], high[cut:], low[cut:]], 1).astype(HALF)


def index_of(packed):
    packed = packed.astype(SINGLE)
    halves = [
        packed[:, j : j + LANES] * 2.0 + packed[:, j + LANES : j + 2 * LANES]
        for j in (0, 2 * LANES)
    ]
    return jnp.concatenate(halves, 0).astype(jnp.int32)


def embed_own(*refs):
    inputs, (slope_ref, sum_ref, held_ref), buffers, sems = refs[:4], refs[4:7], refs[7:-1], refs[-1]
    fetch(inputs, buffers, sems)
    grid_ref, weight_ref, send_ref, recv_ref = buffers
    step = send_ref.shape[0] // GROUPS
    counts = pair_counts(
        recv_ref[:step], sum_ref.shape[0], send_ref[:step], grid_ref.shape[1]
    )
    pre = outer_sum(grid_ref[...], weight_ref[...])
    sigma = jax.nn.sigmoid(pre)
    slope_ref[...] = (sigma * (1.0 + pre * (1.0 - sigma))).astype(HALF)
    sum_ref[...] = matmul(counts, (pre * sigma).astype(HALF))
    held_ref[...] = weight_ref[...]


def embed_far(p, parcel_ref, weight_ref, recv_ref, sum_ref, index_ref, slope_ref, out_ref):
    index = index_of(parcel_ref[parcel_ref.shape[0] - INDEX_ROWS // 2 :])
    index_ref[...] = index
    step = recv_ref.shape[0] // GROUPS
    recv = by_partner(slots_of(recv_ref[...]), odd_along("dom"), odd_along("band"), True)[p]
    counts = pair_counts(
        recv, out_ref.shape[0], index[step : 2 * step], parcel_ref.shape[1]
    )
    pre = outer_sum(parcel_ref[: weight_ref.shape[0]], weight_ref[...])
    sigma = jax.nn.sigmoid(pre)
    slope_ref[...] = (sigma * (1.0 + pre * (1.0 - sigma))).astype(HALF)
    out_ref[...] = sum_ref[...] + matmul(counts, (pre * sigma).astype(HALF))


def encode(sum_ref, weight_ref, static_ref, in_ref, slope_ref, state_ref, half_ref, on_ref, off_ref):
    encode_in = sum_ref[...].astype(HALF)
    pre = matmul(encode_in, weight_ref[...])
    sigma = jax.nn.sigmoid(pre)
    state = static_ref[...].astype(SINGLE) + pre * sigma
    half = state.astype(HALF)
    in_ref[...] = encode_in
    slope_ref[...] = sigma * (1.0 + pre * (1.0 - sigma))
    state_ref[...] = state
    half_ref[...] = half
    rows = on_ref.shape[0]
    odd = odd_along("dom")
    head, tail = half[:rows], half[half.shape[0] - rows :]
    on_ref[...] = jnp.where(odd, head, tail)
    off_ref[...] = jnp.where(odd, tail, head)


def embed_last(p, parcel_ref, weight_ref, recv_ref, sum_ref, encode_ref, static_ref, *refs):
    index_ref, slope_ref, outs, total_ref = refs[0], refs[1], refs[2:-1], refs[-1]
    embed_far(p, parcel_ref, weight_ref, recv_ref, sum_ref, index_ref, slope_ref, total_ref)
    encode(total_ref, encode_ref, static_ref, *outs)


def near_counts(near_ref, on_ref, off_ref, out_ref, turned_ref):
    step = near_ref.shape[0]
    mesh_count = near_ref.shape[1]
    first = 2 * SLOT_ROWS
    odd_dom = odd_along("dom")
    on, off = on_ref[...], off_ref[...]
    left = jnp.where(odd_dom, on, off)[first + step : first + 2 * step] + (RIM - mesh_count)
    right = jnp.where(odd_dom, off, on)[first : first + step] + (RIM + mesh_count)
    own = near_ref[...] + RIM
    index = jnp.concatenate([left, own, right], 1)
    spots = lax.broadcasted_iota(jnp.int32, out_ref.shape, 0)
    counts = jnp.zeros(out_ref.shape, SINGLE)
    for j in range(step):
        counts = counts + jnp.where(spots == index[j : j + 1], 1.0, 0.0)
    turned_ref[...] = counts.astype(HALF)
    out_ref[...] = counts.T.astype(HALF)


def process(
    half_ref, state_ref, on_ref, off_ref, counts_ref, self_ref, near_ref,
    final_ref, pre_0_ref, pre_1_ref, half_1_ref, nearby_0_ref, nearby_1_ref, whole_ref,
):
    rim = on_ref.shape[0]
    count = half_ref.shape[0]
    own = slice(rim, rim + count)
    odd = odd_along("dom")
    left = jnp.where(odd, on_ref[...], off_ref[...])
    right = jnp.where(odd, off_ref[...], on_ref[...])
    whole_ref[:rim] = left
    whole_ref[own] = half_ref[...]
    whole_ref[rim + count :] = right
    half_0 = whole_ref[...]
    used = slice(RIM, 3 * RIM + count)
    nearby_0 = (matmul(counts_ref[used], half_0) * (1.0 / NEAR)).astype(HALF)
    nearby_0_ref[...] = nearby_0[RIM : RIM + count]
    pre_0 = matmul(half_0[used], self_ref[0]) + matmul(nearby_0, near_ref[0])
    pre_0_ref[...] = pre_0
    grown = pre_0 * jax.nn.sigmoid(pre_0)
    state_1 = state_ref[...] + grown[RIM : RIM + count]
    half_1 = state_1.astype(HALF)
    whole_ref[RIM:rim] = (left[RIM:].astype(SINGLE) + grown[:RIM]).astype(HALF)
    whole_ref[own] = half_1
    whole_ref[rim + count : rim + count + RIM] = (
        right[:RIM].astype(SINGLE) + grown[RIM + count :]
    ).astype(HALF)
    half_1_ref[...] = half_1
    nearby_1 = (matmul(counts_ref[own], whole_ref[...]) * (1.0 / NEAR)).astype(HALF)
    nearby_1_ref[...] = nearby_1
    pre_1 = matmul(half_1, self_ref[1]) + matmul(nearby_1, near_ref[1])
    pre_1_ref[...] = pre_1
    final_ref[...] = (state_1 + pre_1 * jax.nn.sigmoid(pre_1)).astype(HALF)


def grid_counts(turned, send_ref, recv_ref, *refs):
    far, out_ref = refs[: GROUPS - 1], refs[GROUPS - 1]
    odd_dom, odd_band = odd_along("dom"), odd_along("band")
    step = send_ref.shape[0] // GROUPS
    recv = by_partner(slots_of(recv_ref[...]), odd_dom, odd_band, True)
    send = [send_ref[:step]] + [ref[:step] for ref in far]
    nodes = out_ref.shape[0 if turned else 1] // GROUPS
    grids = out_ref.shape[1 if turned else 0]
    for p in range(GROUPS):
        at = slice(p * nodes, (p + 1) * nodes)
        if turned:
            out_ref[at] = pair_counts(send[p], nodes, recv[p], grids)
        else:
            out_ref[:, at] = pair_counts(recv[p], grids, send[p], nodes)


def mesh_counts(send_ref, recv_ref, *refs):
    far, out_ref = refs[: GROUPS - 1], refs[GROUPS - 1]
    step = send_ref.shape[0] // GROUPS
    send = [send_ref[:step]] + [ref[step : 2 * step] for ref in far]
    recv = by_partner(slots_of(recv_ref[...]), odd_along("dom"), odd_along("band"), True)
    grids, nodes = out_ref.shape[0], out_ref.shape[1] // GROUPS
    for p in range(GROUPS):
        out_ref[:, p * nodes : (p + 1) * nodes] = pair_counts(send[p], grids, recv[p], nodes)


def decode(*refs):
    finals = [refs[i] for i in (0, 4, 3, 2, 1)]
    counts_ref, turned_ref, weight_ref, back_ref = refs[GROUPS : GROUPS + 4]
    in_ref, hidden_ref, grad_ref, own_ref, *outs = refs[GROUPS + 4 :]
    nodes = own_ref.shape[0]
    total = matmul(counts_ref[:, :nodes], finals[0][...])
    for p in range(1, GROUPS):
        total = total + matmul(counts_ref[:, p * nodes : (p + 1) * nodes], finals[p][...])
    decode_in = total.astype(HALF)
    in_ref[...] = decode_in
    pre = matmul(decode_in, weight_ref[...])
    sigma = jax.nn.sigmoid(pre)
    hidden_ref[...] = (pre * sigma).astype(HALF)
    grad = (back_ref[...] * (sigma * (1.0 + pre * (1.0 - sigma)))).astype(HALF)
    grad_ref[...] = grad
    in_grad = back_mul(grad, weight_ref[...]).astype(HALF)
    own_ref[...] = matmul(turned_ref[:nodes], in_grad)
    for p, out in enumerate(outs):
        out[...] = matmul(turned_ref[(p + 1) * nodes : (p + 2) * nodes], in_grad).astype(HALF)


def gather_back(*refs):
    total = refs[0][...]
    for ref in refs[1:GROUPS]:
        total = total + ref[...].astype(SINGLE)
    slope_ref, state_ref, layer_ref, on_ref, off_ref = refs[GROUPS:]
    state_ref[...] = total
    layer = (total * slope_ref[...]).astype(HALF)
    layer_ref[...] = layer
    half = total.astype(HALF)
    odd = odd_along("dom")
    rim, count = RIM, total.shape[0]
    heads = jnp.concatenate([layer[: 2 * rim], half[:rim]], 0)
    tails = jnp.concatenate([layer[count - 2 * rim :], half[count - rim :]], 0)
    on_ref[...] = jnp.where(odd, heads, tails)
    off_ref[...] = jnp.where(odd, tails, heads)


def process_back(
    state_ref, layer_ref, on_ref, off_ref, turned_ref, slope_0_ref, slope_in_ref,
    self_ref, near_ref, encode_ref, static_ref, layer_0_ref, encode_grad_ref, back_ref, whole_ref,
):
    rim = RIM
    count = state_ref.shape[0]
    own = slice(2 * rim, 2 * rim + count)
    odd = odd_along("dom")
    on, off = on_ref[...], off_ref[...]
    left, right = jnp.where(odd, on, off), jnp.where(odd, off, on)
    whole_ref[: 2 * rim] = left[: 2 * rim]
    whole_ref[own] = layer_ref[...]
    whole_ref[2 * rim + count :] = right[: 2 * rim]
    layer_1 = whole_ref[...]
    used = slice(rim, 3 * rim + count)
    inner = slice(rim, rim + count)
    spread = (matmul(turned_ref[used], layer_1) * (1.0 / NEAR)).astype(HALF)
    back = back_mul(layer_1[used], self_ref[1]) + back_mul(spread, near_ref[1])
    state_own = state_ref[...] + back[inner]
    first = left[2 * rim :].astype(SINGLE) + back[:rim]
    last = right[2 * rim :].astype(SINGLE) + back[rim + count :]
    layer_0 = (state_own * slope_0_ref[inner]).astype(HALF)
    layer_0_ref[...] = layer_0
    whole_ref[:rim] = jnp.zeros((rim, back.shape[1]), HALF)
    whole_ref[rim : 2 * rim] = (first * slope_0_ref[:rim]).astype(HALF)
    whole_ref[own] = layer_0
    whole_ref[2 * rim + count : 3 * rim + count] = (last * slope_0_ref[rim + count :]).astype(HALF)
    whole_ref[3 * rim + count :] = jnp.zeros((rim, back.shape[1]), HALF)
    spread = (matmul(turned_ref[own], whole_ref[...]) * (1.0 / NEAR)).astype(HALF)
    state = state_own + back_mul(layer_0, self_ref[0]) + back_mul(spread, near_ref[0])
    static_ref[...] = state
    grad = (state * slope_in_ref[...]).astype(HALF)
    encode_grad_ref[...] = grad
    back_ref[...] = back_mul(grad, encode_ref[...]).astype(HALF)


def split_rows(count):
    return -(-count // (2 * LANES)) * LANES


def store_halves(value, at, mine_ref, other_ref, wide_ref):
    odd = lax.axis_index("dom") % 2
    count, rows = value.shape[0], split_rows(value.shape[0])
    wide_ref[:count] = value
    if count < 2 * rows:
        wide_ref[count : 2 * rows] = jnp.zeros((2 * rows - count, value.shape[1]), SINGLE)
    mine = pl.ds(pl.multiple_of(odd * rows, rows), rows)
    other = pl.ds(pl.multiple_of((1 - odd) * rows, rows), rows)
    mine_ref[at : at + rows] = wide_ref[mine].astype(HALF)
    other_ref[at : at + rows] = wide_ref[other].astype(HALF)
    return at + rows


def gradient_halves(turned, *refs):
    mine_ref, other_ref, wide_ref = refs[-3:]
    at = 0
    for i, (left, right) in enumerate(zip(refs[:-3:2], refs[1:-3:2], strict=True)):
        product = matmul if i < turned else outer_sum
        value = product(left[...], right[...])
        at = store_halves(value, at, mine_ref, other_ref, wide_ref)


def embed_back(*refs):
    back_ref, counts_ref = refs[:2]
    slopes, grids = refs[2 : 2 + GROUPS], refs[2 + GROUPS : 2 + 2 * GROUPS]
    mine_ref, other_ref, wide_ref = refs[2 + 2 * GROUPS :]
    nodes = back_ref.shape[0]
    variables = grids[0].shape[0]
    grads = []
    for p in range(GROUPS):
        latent = matmul(counts_ref[:, p * nodes : (p + 1) * nodes], back_ref[...])
        grads.append((latent * slopes[p][...].astype(SINGLE)).astype(HALF))
    total = matmul(
        jnp.concatenate([grid[:variables] for grid in grids], 1), jnp.concatenate(grads, 0)
    )
    store_halves(total, 0, mine_ref, other_ref, wide_ref)


def split_gradients(body, rows, width, macs, *args):
    outs = [shape(rows, width, HALF)] * 2
    return whole(body, outs, macs, *args, scratch=[pltpu.VMEM((width, width), SINGLE)])


def add_halves(*refs):
    out_ref = refs[-1]
    at = 0
    for mine, other in zip(refs[:-1:2], refs[1:-1:2], strict=True):
        rows = mine.shape[0]
        out_ref[at : at + rows] = (
            mine[...].astype(SINGLE) + other[...].astype(SINGLE)
        ).astype(HALF)
        at += rows


def add_pieces(pieces_ref, out_ref):
    total = pieces_ref[0].astype(SINGLE)
    for i in range(1, pieces_ref.shape[0]):
        total = total + pieces_ref[i].astype(SINGLE)
    out_ref[...] = total.astype(HALF)


def add_bands(*refs):
    out_ref = refs[-1]
    total = refs[0][...].astype(SINGLE)
    for ref in refs[1:-1]:
        total = total + ref[...].astype(SINGLE)
    total = total.astype(HALF)
    for i in range(out_ref.shape[0]):
        out_ref[i] = total


def places(outs):
    encode, self_, near, decode = outs
    return [(decode, None), (self_, 1), (near, 1), (self_, 0), (near, 0), (encode, None)]


def store_squares(first, half, value_ref, outs, buffer_ref, sems):
    rows = outs[0].shape[0] // 2
    spot = pl.ds(pl.multiple_of(half * rows, rows), rows)
    copies = []
    for i, (out, which) in enumerate(places(outs)):
        at = i * rows
        buffer_ref[at : at + rows] = value_ref[first + at : first + at + rows].astype(SINGLE)
        target = out.at[spot] if which is None else out.at[which, spot]
        copies.append(
            pltpu.make_async_copy(buffer_ref.at[at : at + rows], target, sems.at[i])
        )
        copies[-1].start()
    return copies


def unpack_own(part_ref, *refs):
    outs, (buffer_ref, sems) = refs[:4], refs[4:]
    first = (part_ref.shape[0] - buffer_ref.shape[0]) // 2
    half = lax.axis_index("dom") % 2
    for copy in store_squares(first, half, part_ref, outs, buffer_ref, sems):
        copy.wait()


def unpack_other(part_ref, other_ref, *refs):
    outs, narrow, (buffer_ref, sems, *held) = refs[4:8], refs[8:10], refs[10:]
    rows = (part_ref.shape[0] - buffer_ref.shape[0]) // 2
    half = lax.axis_index("dom") % 2
    copies = []
    odd = odd_along("dom")
    for i, at in enumerate((part_ref.shape[0] - rows, 0)):
        own = part_ref[at : at + rows].astype(SINGLE)
        far = other_ref[at : at + rows].astype(SINGLE)
        held[i][:rows] = jnp.where(odd, far, own)
        held[i][rows:] = jnp.where(odd, own, far)[: held[i].shape[0] - rows]
        copies.append(pltpu.make_async_copy(held[i], narrow[i], sems.at[6 + i]))
        copies[-1].start()
    copies += store_squares(rows, 1 - half, other_ref, outs, buffer_ref, sems)
    for copy in copies:
        copy.wait()


def unpack(part, other, width, variables):
    full = shape(width, width, SINGLE)
    pair = jax.ShapeDtypeStruct((2, width, width), SINGLE)
    narrow = shape(variables, width, SINGLE)
    squares = [full, pair, pair, full]
    hbm = pl.BlockSpec(memory_space=pltpu.HBM)
    vmem = pl.BlockSpec(memory_space=pltpu.VMEM)
    scratch = [
        pltpu.VMEM((6 * split_rows(width), width), SINGLE),
        pltpu.SemaphoreType.DMA((8,)),
    ]
    params = pltpu.CompilerParams(vmem_limit_bytes=32 * MIB)
    size = part.size * 6
    cost = pl.CostEstimate(flops=0, bytes_accessed=size, transcendentals=0)
    grads = pl.pallas_call(
        unpack_own,
        out_shape=squares,
        in_specs=[vmem],
        out_specs=[hbm] * 4,
        scratch_shapes=scratch,
        compiler_params=params,
        cost_estimate=cost,
    )(part)
    return pl.pallas_call(
        unpack_other,
        out_shape=[*squares, narrow, narrow],
        in_specs=[vmem, vmem] + [hbm] * 4,
        out_specs=[hbm] * 6,
        input_output_aliases={2: 0, 3: 1, 4: 2, 5: 3},
        scratch_shapes=scratch + [pltpu.VMEM((variables, width), SINGLE)] * 2,
        compiler_params=params,
        cost_estimate=cost,
    )(part, other, *grads)


def reduce_all(part):
    count = lax.axis_size("dom")
    bands = lax.axis_size("band")
    groups = [list(range(c, count, 2)) for c in range(2)]
    chips = count // 2
    rows, width = part.shape[0] // chips, part.shape[1]
    pieces = lax.all_to_all(
        part.reshape(chips, rows, width), "dom", 0, 0, axis_index_groups=groups
    )
    (piece,) = whole(add_pieces, [shape(rows, width, HALF)], 0, pieces)
    others = [
        lax.ppermute(piece, "band", [(i, (i + step) % bands) for i in range(bands)])
        for step in range(1, bands)
    ]
    copies = jax.ShapeDtypeStruct((chips, rows, width), HALF)
    (copies,) = whole(add_bands, [copies], 0, piece, *others)
    return lax.all_to_all(copies, "dom", 0, 0, axis_index_groups=groups).reshape(part.shape)


def shards(
    grid_vars,
    cotangent,
    mesh_static,
    embed_weight,
    encode_weight,
    self_weight,
    neighbor_weight,
    decode_weight,
    output_weight,
    grid_sender,
    mesh_receiver,
    neighbors,
    mesh_sender,
    grid_receiver,
):
    grid_count, variables = grid_vars.shape
    mesh_count, width = mesh_static.shape
    rim = 2 * RIM
    ext = mesh_count + 2 * rim
    grid, cot, near, out_weight = grid_vars.T, cotangent.T, neighbors.T, output_weight.T
    grid_send, mesh_recv, mesh_send, grid_recv = (
        index.reshape(-1, LANES) for index in (grid_sender, mesh_receiver, mesh_sender, grid_receiver)
    )
    step = grid_send.shape[0] // GROUPS * LANES
    nodes = GROUPS * mesh_count
    mesh_rows = shape(mesh_count, width, HALF)
    mesh_full = shape(mesh_count, width, SINGLE)
    grid_rows = shape(grid_count, width, HALF)
    grid_full = shape(grid_count, width, SINGLE)
    parcel = shape(variables + -variables % 16 + INDEX_ROWS // 2, grid_count, HALF)
    sent = fetching(
        parcels, [parcel] * (GROUPS - 1), 0, grid, grid_send, mesh_send, near, limit=32
    )
    arrived = swap_all(*sent)
    embed_macs = grid_count * variables * width + mesh_count * grid_count * (step + width)
    slope_embed, total, held_weight = fetching(
        embed_own,
        [grid_rows, mesh_full, shape(variables, width, HALF)],
        embed_macs,
        grid,
        embed_weight,
        grid_send,
        mesh_recv,
        limit=32,
    )
    index = [None] * GROUPS
    slopes = [slope_embed] + [None] * (GROUPS - 1)
    grids = [grid, *arrived]
    embedded = [shape(INDEX_ROWS, LANES, jnp.int32), grid_rows]
    for p in (1, 3, 2):
        index[p], slopes[p], total = whole(
            lambda *refs, p=p: embed_far(p, *refs),
            [*embedded, mesh_full],
            embed_macs,
            arrived[p - 1],
            held_weight,
            mesh_recv,
            total,
        )
    index[4], slopes[4], encode_in, slope_encode, state, half, on, off = whole(
        lambda *refs: embed_last(4, *refs),
        [*embedded, mesh_rows, mesh_full, mesh_full, mesh_rows]
        + [shape(rim, width, HALF)] * 2,
        embed_macs + mesh_count * width * width,
        arrived[3],
        held_weight,
        mesh_recv,
        total,
        encode_weight,
        mesh_static,
        scratch=[pltpu.VMEM((mesh_count, width), SINGLE)],
    )
    off = swap_off(off)
    on = swap_on(on)
    counts, turned = whole(
        near_counts, [shape(ext, ext, HALF)] * 2, ext * ext * 64, near, index[1], index[2]
    )
    count_macs = nodes * grid_count * step
    (to_grid,) = whole(
        lambda *refs: grid_counts(False, *refs),
        [shape(grid_count, nodes, HALF)],
        count_macs,
        mesh_send,
        grid_recv,
        *index[1:],
    )
    state, to_grid = lax.optimization_barrier((state, to_grid))
    final_half, pre_0, pre_1, half_1, nearby_0, nearby_1 = whole(
        process,
        [mesh_rows, shape(ext - rim, width, SINGLE), mesh_full] + [mesh_rows] * 3,
        (ext + mesh_count) * (ext + 2 * width) * width,
        half,
        state,
        on,
        off,
        counts,
        self_weight,
        neighbor_weight,
        scratch=[pltpu.VMEM((ext, width), HALF)],
    )
    moved = swap_all(*[final_half] * 4)
    finals = [final_half] + [moved[p - 1] for p in (4, 3, 2, 1)]
    (from_grid,) = whole(
        lambda *refs: grid_counts(True, *refs),
        [shape(nodes, grid_count, HALF)],
        count_macs,
        lax.optimization_barrier((mesh_send, final_half))[0],
        grid_recv,
        *index[1:],
    )
    hidden_grad = outer_sum(cot, out_weight)
    decode_in, hidden, decode_grad, state_grad, *sums = whole(
        decode,
        [grid_rows] * 3 + [mesh_full] + [mesh_rows] * (GROUPS - 1),
        2 * grid_count * width * (nodes + width),
        *finals,
        to_grid,
        from_grid,
        decode_weight,
        hidden_grad,
    )
    moved = swap_all(*sums)
    arrived = [moved[p - 1] for p in (1, 2, 3, 4)]
    prediction = (grid.astype(SINGLE) + back_mul(out_weight, hidden)).astype(HALF)
    half_rows = split_rows(width)
    narrow_rows = split_rows(variables)
    square = width * width
    decode_halves = split_gradients(
        lambda *refs: gradient_halves(1, *refs),
        narrow_rows + half_rows,
        width,
        2 * grid_count * square,
        cot,
        hidden,
        decode_in,
        decode_grad,
    )
    to_mesh = whole(
        mesh_counts,
        [shape(grid_count, nodes, HALF)],
        count_macs,
        lax.optimization_barrier((grid_send, decode_in))[0],
        mesh_recv,
        *index[1:],
    )[0]
    state_grad, to_mesh, *decode_halves = lax.optimization_barrier(
        (state_grad, to_mesh, *decode_halves)
    )
    state_grad, layer_1, on, off = whole(
        gather_back,
        [mesh_full, mesh_rows] + [shape(rim + RIM, width, HALF)] * 2,
        0,
        state_grad,
        *arrived,
        silu_slope(pre_1),
    )
    off = swap_off(off)
    on = swap_on(on)
    layer_halves = split_gradients(
        lambda *refs: gradient_halves(0, *refs),
        2 * half_rows,
        width,
        2 * mesh_count * square,
        half_1,
        layer_1,
        nearby_1,
        layer_1,
    )
    halves = [decode_halves[0], swap_on(decode_halves[1])]
    state_grad, *layer_halves, halves[1] = lax.optimization_barrier(
        (state_grad, *layer_halves, halves[1])
    )
    state_grad, layer_0, encode_grad, encode_in_grad = whole(
        process_back,
        [mesh_full, mesh_rows, mesh_rows, mesh_rows],
        (ext + mesh_count) * (ext + 2 * width) * width,
        state_grad,
        layer_1,
        on,
        off,
        turned,
        silu_slope(pre_0),
        slope_encode,
        self_weight,
        neighbor_weight,
        encode_weight,
        scratch=[pltpu.VMEM((ext, width), HALF)],
    )
    rest_halves = split_gradients(
        lambda *refs: gradient_halves(0, *refs),
        3 * half_rows,
        width,
        3 * mesh_count * square,
        half,
        layer_0,
        nearby_0,
        layer_0,
        encode_in,
        encode_grad,
    )
    embed_halves = split_gradients(
        embed_back,
        narrow_rows,
        width,
        grid_count * width * (nodes + GROUPS * variables),
        encode_in_grad,
        to_mesh,
        *slopes,
        *grids,
    )
    for mine, other in (layer_halves, rest_halves, embed_halves):
        halves += [mine, swap_on(other)]
    rows = sum(block.shape[0] for block in halves[::2])
    (part,) = whole(add_halves, [shape(rows, width, HALF)], 0, *halves)
    part = reduce_all(part)
    other = swap_on(part)
    grad_encode, grad_self, grad_near, grad_decode, grad_embed, grad_output = unpack(
        part, other, width, variables
    )
    return (
        prediction.T,
        state_grad,
        grad_embed,
        grad_encode,
        grad_self,
        grad_near,
        grad_decode,
        grad_output.T,
    )


def solution(mesh):
    placed = (
        P(("band", "dom"), None),
        P(("band", "dom"), None),
        P(("band", "dom"), None),
        P(),
        P(),
        P(),
        P(),
        P(),
        P(),
        P(("band", "dom")),
        P(("band", "dom")),
        P(("band", "dom"), None),
        P(("band", "dom")),
        P(("band", "dom")),
    )
    return jax.shard_map(
        shards,
        mesh=mesh,
        in_specs=placed,
        out_specs=(
            P(("band", "dom"), None),
            P(("band", "dom"), None),
            P(),
            P(),
            P(),
            P(),
            P(),
            P(),
        ),
        check_vma=False,
    )
```
